512 devices in a mesh: ctx: 32 (over x, y, core), exp: 16 (over z).
Axes of the slice: x: 4, y: 4, z: 16, core: 2. Of those that a mesh axis runs over, the one named last changes fastest.
Arguments:
- queries: bfloat16 [1, 8192, 4096], P(None, 'ctx', 'exp'), may hold values from -80 to 80
- keys: bfloat16 [1, 8192, 1024], P(None, 'ctx'), may hold values from -4 to 4
- values: bfloat16 [1, 8192, 1024], P(None, 'ctx'), may hold values from -8 to 8
- routes: int32 [1, 8192, 1], P(None, 'ctx'), may hold values from 0 to 127; in each aligned block of 256 rows (0 to 255, 256 to 511, ..., all dimensions but the last counted through in order) at most 4 rows name the same one
- route_score: float32 [1, 8192], P(None, 'ctx'), may hold values from 0.3 to 1.5
- output_weight: bfloat16 [4096, 4096], P('exp', 'ctx'), may hold values from -0.09375 to 0.09375
- norm_gain: float32 [4096], P('exp'), may hold values from 0.1 to 1.9
- gate_weight: bfloat16 [128, 4096, 512], P('ctx', 'exp'), may hold values from -0.09375 to 0.09375
- up_weight: bfloat16 [128, 4096, 512], P('ctx', 'exp'), may hold values from -0.09375 to 0.09375
- down_weight: bfloat16 [128, 512, 4096], P('ctx', None, 'exp'), may hold values from -0.25 to 0.25
Outputs:
- moe_out: bfloat16 [1, 8192, 4096], P(None, 'ctx', 'exp')
The draws below stay inside these ranges and needn't reach their ends.
Inputs may be any that keep to these rules, and one draw needn't show every extreme that they name: `routes`: among the 256 tokens at positions j * 256 to j * 256 + 255 of one sequence, at most 4 name the same expert, and 4 is reached.
All inputs are finite; a program needn't handle non-finite values.
Results may differ from the reference program's by a relative error of at most 0.04.
Values may be sent and summed in bfloat16 or wider, within the bound.
A program may use at most 64 MiB of HBM per device.

```python
import math
import jax
import jax.numpy as jnp
import numpy as np
from jax import lax

HD = 128
FF = 512
SEQS = 1
TOK_DEV = 256
HQ = 32
KVH = 8
D = 4096
EXPERTS = 128
LEN = 8192
MOST = 4
N_CTX = 32
N_EXP = 16


def linked_keys(key):
    first, second = jax.random.split(key)
    shape = (SEQS, LEN, KVH, HD)
    base = jnp.clip(jax.random.normal(first, shape, jnp.float32), -4.0, 4.0)
    noise = jnp.clip(jax.random.normal(second, shape, jnp.float32), -4.0, 4.0)
    tied = (jnp.arange(LEN) % 32 == 1)[None, :, None, None]
    return jnp.where(tied, noise, base)


def draw_keys(key, part):
    linked = linked_keys(key)
    return linked.reshape(SEQS, LEN, KVH * HD).astype(jnp.bfloat16)


def draw_queries(key, part):
    key = jax.random.fold_in(key, 7)
    fresh = jnp.clip(jax.random.normal(key, (SEQS, LEN, HQ, HD), jnp.float32), -4.0, 4.0)
    return fresh.reshape(SEQS, LEN, HQ * HD).astype(jnp.bfloat16)


def draw_values(key, part):
    key = jax.random.fold_in(key, 13)
    first = jax.random.fold_in(key, 0)
    head_scale = 0.6 + 1.4 * jnp.arange(KVH, dtype=jnp.float32) / max(KVH - 1, 1)
    drawn = jnp.clip(jax.random.normal(first, (SEQS, LEN, KVH, HD), jnp.float32), -4.0, 4.0)
    return (drawn * head_scale[None, None, :, None]).reshape(SEQS, LEN, KVH * HD).astype(jnp.bfloat16)


def levels(own_key, shape, cuts, least, high):
    factor_of = 1.0
    for axis_at, blocks in cuts:
        draws = jax.random.uniform(jax.random.fold_in(jax.random.fold_in(own_key, 6), axis_at), (blocks,), jnp.float32, least / len(cuts), high / len(cuts))
        factor_of = factor_of * jnp.repeat(jnp.exp(draws), shape[axis_at] // blocks).reshape((-1,) + (1,) * (len(shape) - 1 - axis_at))
    return factor_of


def shared_out(own_key, own, number, rows, count, top, reach, skew):
    sequence = jax.random.permutation(own_key, count)
    packed, ordinary = portions_of(count, rows * top, reach, skew, True), portions_of(count, rows * top, reach, skew, False)
    places = jnp.arange(count)

    def named(sizes, rotation):
        used = int((sizes > 0).sum())
        fixed = max(1, used // 4)
        moved = fixed + (places - fixed + rotation * (used - fixed)) % max(1, count - fixed)
        return jnp.zeros((count,), jnp.int32).at[sequence[jnp.where(places < fixed, places, moved)]].set(jnp.asarray(sizes, jnp.int32))

    sizes = jnp.where(number % 4 == 0, named(packed, number // 4), named(ordinary, number - number // 4 - 1))
    mixed = jax.random.permutation(jax.random.fold_in(own, 3), count)
    source_of, taker = mixed[0:count // 2 * 2:2], mixed[1:count // 2 * 2:2]
    room = jnp.minimum(sizes[source_of] - 1, reach - sizes[taker]) // 2
    room = jnp.where((source_of == sequence[0]) | (taker == sequence[0]) | (sizes[taker] == 0), 0, jnp.maximum(room, 0))
    moved = jax.random.randint(jax.random.fold_in(own, 4), (count // 2,), 0, 1 << 20) % (room + 1)
    sizes = sizes.at[source_of].add(-moved).at[taker].add(moved)
    labels = jnp.searchsorted(jnp.cumsum(sizes), jnp.arange(rows * top), side="right").astype(jnp.int32)
    table = labels.reshape(top, rows).T
    table = table[jax.random.permutation(jax.random.fold_in(own, 1), rows)]
    rotation = jax.random.randint(jax.random.fold_in(own, 2), (rows, 1), 0, top)
    return jnp.take_along_axis(table, (jnp.arange(top)[None, :] + rotation) % top, axis=1)


def portions_of(number_of, total, most, lean, full):
    loads = [(1 << 20) // math.isqrt(rank ** lean) + 1 for rank in range(1, number_of + 1)]
    largest = most if full else min(most, max(-(-total // number_of), total * loads[0] // sum(loads)))
    least = 1 if total - largest >= number_of - 1 else 0
    given, surplus = [largest] + [least] * (number_of - 1), total - largest - least * (number_of - 1)
    while surplus > 0:
        candidates = [i for i in range(1, number_of) if given[i] < largest] or [i for i in range(1, number_of) if given[i] < most]
        whole, remaining = sum([loads[i] for i in candidates]), surplus
        for i in candidates:
            addition = min(most - given[i], max(1, remaining * loads[i] // whole), surplus)
            given[i] = given[i] + addition
            surplus = surplus - addition
    return np.array(given)


def scatter_about(own_key, dims, spread, reach, cuts=(), kind=jnp.bfloat16):
    entries = jax.random.normal(own_key, dims, jnp.float32) * spread
    if len(cuts) > 0:
        entries = levels(own_key, dims, cuts, -0.22, 0.18) * entries
    return jnp.clip(entries, min=-reach, max=reach).astype(kind)


def setup_inputs(seed: int = 0) -> dict:
    key_of = jax.random.split(jax.random.key(seed), 11)
    queries = draw_queries(jax.random.fold_in(key_of[10], 71), 0)
    keys = draw_keys(jax.random.fold_in(key_of[10], 71), 0)
    values = draw_values(jax.random.fold_in(key_of[10], 71), 0)
    routes_keys = jax.random.split(jax.random.fold_in(key_of[3], 1), SEQS * LEN // TOK_DEV)
    routes_turns = jax.random.permutation(jax.random.fold_in(key_of[3], 3), SEQS * LEN // TOK_DEV)
    routes = jax.vmap(lambda own, number: shared_out(jax.random.fold_in(key_of[3], 2), own, number, TOK_DEV, EXPERTS, 1, MOST, 2))(routes_keys, routes_turns).reshape((SEQS, LEN, 1))
    route_score = jnp.clip(0.3 + 1.2 * jax.random.uniform(key_of[4], (SEQS, LEN), jnp.float32) ** levels(key_of[4], (SEQS, LEN), ((1, 32),), -0.2, 0.2), 0.3, 1.5)
    output_weight = scatter_about(key_of[5], (D, D), D ** -0.5, 0.09375, ((0, 16), (1, 32)))
    norm_gain = jnp.clip(1.0 + 0.18 * jax.random.normal(key_of[6], (D,), jnp.float32), 0.1, 1.9)
    gate_weight = scatter_about(key_of[7], (EXPERTS, D, FF), D ** -0.5, 0.09375, ((0, 32), (1, 16)))
    up_weight = scatter_about(key_of[8], (EXPERTS, D, FF), D ** -0.5, 0.09375, ((0, 32), (1, 16)))
    down_weight = scatter_about(key_of[9], (EXPERTS, FF, D), FF ** -0.5, 0.25, ((0, 32), (2, 16)))
    return {"queries": queries, "keys": keys, "values": values, "routes": routes, "route_score": route_score, "output_weight": output_weight, "norm_gain": norm_gain, "gate_weight": gate_weight, "up_weight": up_weight, "down_weight": down_weight}


eps = 1e-05
far_below = -1e+30

def attend_block(query_block, key_all, value_all, query_start):
    block_rows = query_block.shape[0]
    groups = HQ // KVH
    query_f = query_block.astype(jnp.float32).reshape(block_rows, KVH, groups, HD)
    key_f = key_all.astype(jnp.float32)
    scores = jnp.einsum('qhgd,khd->hgqk', query_f, key_f) * (1.0 / math.sqrt(HD))
    query_pos = query_start + jnp.arange(block_rows, dtype=jnp.int32)
    key_pos = jnp.arange(key_all.shape[0], dtype=jnp.int32)
    visible = key_pos[None, :] <= query_pos[:, None]
    scores = jnp.where(visible, scores, far_below)
    highest = lax.optimization_barrier(jnp.max(scores, axis=-1, keepdims=True))
    weights = jnp.where(visible, jnp.exp(scores - highest), 0.0)
    total = lax.optimization_barrier(jnp.sum(weights, axis=-1))
    rounded = lax.optimization_barrier(weights.astype(jnp.bfloat16)).astype(jnp.float32)
    mixed = jnp.einsum('hgqk,khd->qhgd', rounded, value_all.astype(jnp.float32))
    result = mixed / jnp.transpose(total, (2, 0, 1))[..., None]
    return result.reshape(block_rows, HQ * HD).astype(jnp.bfloat16)

def reference(queries, keys, values, routes, route_score, output_weight, norm_gain, gate_weight, up_weight, down_weight):
    length = queries.shape[1]
    block_rows = min(length, 128)
    block_count = length // block_rows

    def single_sequence(operands):
        query_seq, key_seq, value_seq = operands
        key_heads = key_seq.reshape(length, KVH, HD)
        value_heads = value_seq.reshape(length, KVH, HD)
        query_block_list = query_seq.reshape(block_count, block_rows, HQ, HD)
        starts = jnp.arange(block_count, dtype=jnp.int32) * block_rows
        mapped = lax.map(lambda pair: attend_block(pair[0], key_heads, value_heads, pair[1]), (query_block_list, starts))
        return mapped.reshape(length, HQ * HD)
    attn = lax.map(single_sequence, (queries, keys, values))
    width = attn.shape[-1]
    group = width // N_EXP
    attn_groups = jnp.transpose(attn.reshape(-1, N_EXP, group), (1, 0, 2))
    weight_groups = output_weight.reshape(N_EXP, group, width)

    def group_adder(carry, pair):
        part = jnp.dot(pair[0], pair[1], preferred_element_type=jnp.float32)
        part = lax.optimization_barrier(part.astype(jnp.bfloat16)).astype(jnp.float32)
        return (carry + part, None)
    start_sum = jnp.zeros((attn_groups.shape[1], width), jnp.float32)
    projected, unused = lax.scan(group_adder, start_sum, (attn_groups, weight_groups))
    squares = lax.optimization_barrier(jnp.mean(projected * projected, axis=-1, keepdims=True))
    normed = (projected * lax.rsqrt(squares + eps) * norm_gain.astype(jnp.float32)).astype(jnp.bfloat16)
    flat = normed
    chosen = routes.reshape(-1).astype(jnp.int32)
    token_count = chosen.shape[0]
    expert_count = gate_weight.shape[0]
    capacity = SEQS * N_CTX * MOST
    order = jnp.argsort(chosen, stable=True).astype(jnp.int32)
    counts = lax.optimization_barrier(jnp.sum((chosen[:, None] == jnp.arange(expert_count, dtype=jnp.int32)[None, :]).astype(jnp.int32), axis=0))
    starts = (jnp.cumsum(counts) - counts).astype(jnp.int32)
    padded = jnp.concatenate([order, jnp.full((capacity,), token_count, jnp.int32)])

    def one_expert(expert):
        picked = lax.dynamic_slice_in_dim(padded, starts[expert], capacity)
        live = jnp.arange(capacity, dtype=jnp.int32) < counts[expert]
        index = jnp.where(live, picked, token_count).astype(jnp.int32)
        taken = flat[jnp.minimum(index, token_count - 1)]
        gate = jnp.dot(taken, gate_weight[expert], preferred_element_type=jnp.float32)
        upper = jnp.dot(taken, up_weight[expert], preferred_element_type=jnp.float32)
        hidden = (jax.nn.silu(gate) * upper).astype(jnp.bfloat16)
        produced = jnp.dot(hidden, down_weight[expert], preferred_element_type=jnp.float32).astype(jnp.bfloat16)
        return (index, produced)
    index_all, produced_all = lax.map(one_expert, jnp.arange(expert_count, dtype=jnp.int32))
    expert_out = jnp.zeros((token_count, width), jnp.bfloat16).at[index_all.reshape(-1)].set(produced_all.reshape(-1, width), mode='drop')
    scored = route_score.reshape(-1)[:, None].astype(jnp.float32) * expert_out.astype(jnp.float32)
    return scored.astype(jnp.bfloat16).reshape(queries.shape[0], length, width)
```

```python
import functools
import math

import jax
import jax.numpy as jnp
from jax import lax
from jax.experimental import pallas as pl
from jax.experimental.pallas import tpu as pltpu
from jax.sharding import PartitionSpec as P

HD = 128
EPS = 1e-05
FAR_BELOW = -1e30
F32 = jnp.float32
BF16 = jnp.bfloat16
VMEM_LIMIT = 56 * 1024 * 1024


def dot(a, b):
    return jnp.dot(a, b, preferred_element_type=F32)


NX = 4
NY = 4
STEPS_OFF = (0, 1, -1, 2)
MESSAGES = 36
CHUNKS = 4
PARTS = 2


def layer_kernel(
    n_ctx,
    n_exp,
    query_ref,
    route_col_ref,
    route_row_ref,
    gain_ref,
    keys_hbm,
    values_hbm,
    weight_hbm,
    gate_hbm,
    up_hbm,
    down_hbm,
    out_ref,
    kv_ref,
    weight_ref,
    high_ref,
    total_ref,
    attn_ref,
    gu_ref,
    down_ref,
    proj_out,
    proj_in,
    proj_ref,
    packed_ref,
    arrived_ref,
    part_ref,
    gu_out,
    gu_in,
    squares_out,
    squares_in,
    hidden_ref,
    made_ref,
    back_ref,
    load_sem,
    flow_send,
    flow_recv,
    proj_send,
    proj_recv,
    there_send,
    there_recv,
    gu_send,
    gu_recv,
    sq_send,
    sq_recv,
    hid_send,
    hid_recv,
    home_send,
    home_recv,
):
    me = lax.axis_index("ctx")
    z = lax.axis_index("exp")
    half = n_exp // 2
    tokens, local = query_ref.shape
    experts, _, twice = gu_ref.shape
    units = twice // 2
    lots = packed_ref.shape[0]
    each = lots // n_ctx
    most = each // experts
    neighbour = (lax.rem(z + 1, n_exp), lax.rem(z + n_exp - 1, n_exp))

    kv_heads = keys_hbm.shape[1] // HD
    columns = pl.ds(pl.multiple_of(z * kv_heads // n_exp * HD, HD), HD)
    own_loads = [
        pltpu.make_async_copy(keys_hbm.at[:, columns], kv_ref.at[0, me], load_sem.at[3]),
        pltpu.make_async_copy(values_hbm.at[:, columns], kv_ref.at[1, me], load_sem.at[4]),
        pltpu.make_async_copy(weight_hbm, weight_ref.at[me], load_sem.at[5]),
    ]
    for load in own_loads:
        load.start()
    loads = [
        pltpu.make_async_copy(gate_hbm, gu_ref.at[:, :, pl.ds(0, units)], load_sem.at[0]),
        pltpu.make_async_copy(up_hbm, gu_ref.at[:, :, pl.ds(units, units)], load_sem.at[1]),
        pltpu.make_async_copy(down_hbm, down_ref, load_sem.at[2]),
    ]
    for load in loads:
        load.start()

    barrier = pltpu.get_barrier_semaphore()

    def greet_ctx(r, carry):
        pl.semaphore_signal(
            barrier, inc=1, device_id=(lax.rem(me + r, n_ctx), z), device_id_type=pl.DeviceIdType.MESH
        )
        return carry

    def greet_exp(r, carry):
        pl.semaphore_signal(
            barrier, inc=1, device_id=(me, lax.rem(z + r, n_exp)), device_id_type=pl.DeviceIdType.MESH
        )
        return carry

    lax.fori_loop(1, n_ctx, greet_ctx, 0)
    lax.fori_loop(1, n_exp, greet_exp, 0)
    pl.semaphore_wait(barrier, n_ctx - 1 + n_exp - 1)

    def along(source, target, send_sem, recv_sem, way):
        return pltpu.make_async_remote_copy(
            src_ref=source,
            dst_ref=target,
            send_sem=send_sem,
            recv_sem=recv_sem,
            device_id=(me, neighbour[way]),
            device_id_type=pl.DeviceIdType.MESH,
        )

    def target_of(way, step):
        if way == 0:
            return lax.rem(z + half - step, n_exp)
        return lax.rem(z + n_exp - half + step, n_exp)

    lane = me % 2
    chip = me // 2
    at_x, at_y = chip // NY, chip % NY

    def chip_at(dx, dy):
        return lax.rem(at_x + dx + NX, NX) * NY + lax.rem(at_y + dy + NY, NY)

    class Stream:
        def __init__(self, number, ref, first_row, rows, y_first):
            self.number, self.ref, self.first_row, self.rows = number, ref, first_row, rows
            self.y_first = y_first

        def chip(self, da, db):
            return chip_at(db, da) if self.y_first else chip_at(da, db)

        def copy(self, message, da, db, part, to, its_lane=None):
            start, size = self.first_row, self.rows
            if part is not None:
                size = size // 2
                start = start + part * size
            block = self.chip(da, db) * 2 + (lane if its_lane is None else its_lane)
            here = self.ref.at[block, pl.ds(start, size)]
            target = self.chip(0, 0) * 2 + 1 - lane if to is None else self.chip(*to) * 2 + lane
            return pltpu.make_async_remote_copy(
                src_ref=here,
                dst_ref=here,
                send_sem=flow_send.at[self.number, message],
                recv_sem=flow_recv.at[self.number, message],
                device_id=(target, z),
                device_id_type=pl.DeviceIdType.MESH,
            )

        def first(self, side):
            return self.copy(side, 0, 0, None, ((1, 0), (-1, 0))[side])

        def first_in(self, side):
            return self.copy(side, (-1, 1)[side], 0, None, (1, 0))

        def relay(self, side):
            return self.copy(2 + side, (-1, 1)[side], 0, side, ((1, 0), (-1, 0))[side])

        def relay_in(self, side):
            return self.copy(2 + side, 2, 0, side, (1, 0))

        def second(self, i, side):
            return self.copy(4 + 2 * i + side, STEPS_OFF[i], 0, None, ((0, 1), (0, -1))[side])

        def second_in(self, i, side):
            return self.copy(4 + 2 * i + side, STEPS_OFF[i], (-1, 1)[side], None, (0, 1))

        def pass_on(self, i, side):
            return self.copy(
                12 + 2 * i + side, STEPS_OFF[i], (-1, 1)[side], side, ((0, 1), (0, -1))[side]
            )

        def pass_on_in(self, i, side):
            return self.copy(12 + 2 * i + side, STEPS_OFF[i], 2, side, (0, 1))

        def twin(self, i, j):
            return self.copy(20 + 4 * i + j, STEPS_OFF[i], STEPS_OFF[j], None, None)

        def twin_in(self, i, j):
            return self.copy(20 + 4 * i + j, STEPS_OFF[i], STEPS_OFF[j], None, None, 1 - lane)

        def stage(self, number):
            if number == 0:
                for side in range(2):
                    self.first(side).start()
                    self.second(0, side).start()
                self.twin(0, 0).start()
            if number == 1:
                for side in range(2):
                    self.first_in(side).wait_recv()
                    self.relay(side).start()
                    i = 2 - side
                    self.second(i, 0).start()
                    self.second(i, 1).start()
                    self.twin(i, 0).start()
                for side in range(2):
                    self.second_in(0, side).wait_recv()
                    self.pass_on(0, side).start()
                    self.twin(0, 2 - side).start()
            if number == 2:
                for side in range(2):
                    self.relay_in(side).wait_recv()
                for side in range(2):
                    self.second(3, side).start()
                self.twin(3, 0).start()
                for side in range(2):
                    self.pass_on_in(0, side).wait_recv()
                self.twin(0, 3).start()
            if number == 3:
                for i in (1, 2):
                    for side in range(2):
                        self.second_in(i, side).wait_recv()
                        self.pass_on(i, side).start()
                        self.twin(i, 2 - side).start()
            if number == 4:
                for side in range(2):
                    self.second_in(3, side).wait_recv()
                    self.pass_on(3, side).start()
                    self.twin(3, 2 - side).start()
                for i in (1, 2):
                    for side in range(2):
                        self.pass_on_in(i, side).wait_recv()
                    self.twin(i, 3).start()
            if number == 5:
                for side in range(2):
                    self.pass_on_in(3, side).wait_recv()
                self.twin(3, 3).start()

        def sent(self):
            for side in range(2):
                self.first(side).wait_send()
                self.relay(side).wait_send()
                for i in range(4):
                    self.second(i, side).wait_send()
                    self.pass_on(i, side).wait_send()
            for i in range(4):
                for j in range(4):
                    self.twin(i, j).wait_send()

    rows_of_weight = weight_hbm.shape[0]
    key_stream = Stream(0, kv_ref.at[0], 0, tokens, True)
    value_stream = Stream(1, kv_ref.at[1], 0, tokens, False)
    weight_streams = (
        Stream(2, weight_ref, 0, rows_of_weight // 2, True),
        Stream(3, weight_ref, rows_of_weight // 2, rows_of_weight // 2, False),
    )

    def kv_stage(number):
        key_stream.stage(number)
        value_stream.stage(number)

    def weight_stage(number):
        for stream in weight_streams:
            stream.stage(number)

    heads = local // HD
    block = 2 * tokens
    factor = math.log2(math.e) / math.sqrt(HD)

    def attend(dx, dy, own):
        i, j = STEPS_OFF.index(dy), STEPS_OFF.index(dx)
        key_stream.twin_in(i, j).wait_recv()
        value_stream.twin_in(j, i).wait_recv()
        source = chip_at(dx, dy)

        def compute():
            keys = kv_ref[0, pl.ds(source * 2, 2)].reshape(block, HD)
            values = kv_ref[1, pl.ds(source * 2, 2)].reshape(block, HD)
            values = jnp.concatenate([values, jnp.ones((block, HD), BF16)], axis=1)
            for head in range(heads):
                query = query_ref[:, head * HD : (head + 1) * HD]
                scores = lax.dot_general(
                    query, keys, (((1,), (1,)), ((), ())), preferred_element_type=F32
                )
                if own:
                    shape = (tokens, block)
                    spot = lane * tokens + lax.broadcasted_iota(jnp.int32, shape, 0)
                    visible = lax.broadcasted_iota(jnp.int32, shape, 1) <= spot
                    scores = jnp.where(visible, scores, FAR_BELOW)
                highest = jnp.max(scores, axis=1, keepdims=True)
                if not own:
                    before = high_ref[head]
                    highest = jnp.maximum(highest, before)
                weights = jnp.exp2((scores - highest) * factor).astype(BF16)
                summed = dot(weights, values)
                if not own:
                    summed = summed + total_ref[head] * jnp.exp2((before - highest) * factor)
                total_ref[head] = summed
                high_ref[head] = highest

        if own:
            compute()
        else:
            pl.when(source < chip)(compute)

    for load in own_loads:
        load.wait()
    kv_stage(0)
    attend(0, 0, True)
    kv_stage(1)
    for dx, dy in ((0, -1), (-1, 0), (0, 1), (1, 0)):
        attend(dx, dy, False)
    kv_stage(2)
    weight_stage(0)
    for dx, dy in ((0, 2), (2, 0)):
        attend(dx, dy, False)
    kv_stage(3)
    weight_stage(1)
    for dx, dy in ((-1, -1), (-1, 1), (1, -1), (1, 1)):
        attend(dx, dy, False)
    kv_stage(4)
    weight_stage(2)
    for dx, dy in ((2, -1), (2, 1), (-1, 2), (1, 2)):
        attend(dx, dy, False)
    kv_stage(5)
    weight_stage(3)
    attend(2, 2, False)
    weight_stage(4)
    for head in range(heads):
        summed = total_ref[head]
        attn_ref[:, head * HD : (head + 1) * HD] = (summed[:, :HD] / summed[:, HD:]).astype(BF16)
    weight_stage(5)
    for stream in weight_streams:
        for i in range(4):
            for j in range(4):
                stream.twin_in(i, j).wait_recv()

    rows = tokens // CHUNKS
    pairs = n_ctx // n_exp

    def proj_copy(way, step, part):
        spot = pl.ds(part * rows, rows)
        return along(
            proj_out.at[way, step, spot],
            proj_in.at[way, step, spot],
            proj_send.at[way, step, part],
            proj_recv.at[way, step, part],
            way,
        )

    def proj_term(target, part):
        columns = jnp.concatenate(
            [weight_ref[target * pairs + i] for i in range(pairs)], axis=1
        )
        return dot(attn_ref[pl.ds(part * rows, rows), :], columns)

    def far(way, part, parts):
        return (part < parts // 2) == (way == 0)

    def proj_step(step, started):
        for part in range(CHUNKS):
            for way in range(2):
                fresh = started == 0 or (started == 1 and not far(way, part, CHUNKS))
                if started == 0 and not far(way, part, CHUNKS):
                    continue
                spot = pl.ds(part * rows, rows)
                term = proj_term(target_of(way, step), part)
                if not fresh:
                    proj_copy(way, step - 1, part).wait_recv()
                    term = term + proj_in[way, step - 1, spot].astype(F32)
                proj_out[way, step, spot] = term.astype(BF16)
                proj_copy(way, step, part).start()

    proj_step(0, 0)
    proj_step(1, 1)

    def proj_loop(step, carry):
        proj_step(step, 2)
        return carry

    lax.fori_loop(2, half, proj_loop, 0)
    for part in range(CHUNKS):
        spot = pl.ds(part * rows, rows)
        term = proj_term(z, part)
        for way in range(2):
            proj_copy(way, half - 1, part).wait_recv()
            term = term + proj_in[way, half - 1, spot].astype(F32)
        proj_ref[spot, :] = term.astype(BF16)

    chosen_col = route_col_ref[...]
    chosen_row = route_row_ref[...]
    square = (tokens, tokens)
    down_axis = lax.broadcasted_iota(jnp.int32, square, 0)
    over_axis = lax.broadcasted_iota(jnp.int32, square, 1)
    same = chosen_col == chosen_row
    rank_col = jnp.sum(
        jnp.where(same & (over_axis < down_axis), 1.0, 0.0), axis=1, keepdims=True
    ).astype(jnp.int32)
    rank_row = jnp.sum(
        jnp.where(same & (down_axis < over_axis), 1.0, 0.0), axis=0, keepdims=True
    ).astype(jnp.int32)
    slot_col = chosen_col * most + rank_col
    slot_row = chosen_row * most + rank_row
    pick = jnp.where(
        lax.broadcasted_iota(jnp.int32, (lots, tokens), 0) == slot_row, 1.0, 0.0
    ).astype(BF16)
    packed_ref[...] = dot(pick, proj_ref[...]).astype(BF16)

    def there_copy(r):
        peer = lax.rem(me + r, n_ctx)
        return pltpu.make_async_remote_copy(
            src_ref=packed_ref.at[pl.ds(pl.multiple_of(peer * each, each), each)],
            dst_ref=arrived_ref.at[pl.ds(pl.multiple_of(me * each, each), each)],
            send_sem=there_send.at[r],
            recv_sem=there_recv.at[r],
            device_id=(peer, z),
            device_id_type=pl.DeviceIdType.MESH,
        )

    def start_there(r, carry):
        there_copy(r).start()
        return carry

    def wait_there(r, carry):
        there_copy(r).wait_recv()
        return carry

    lax.fori_loop(1, n_ctx, start_there, 0)
    own = pl.ds(pl.multiple_of(me * each, each), each)
    arrived_ref[own, :] = packed_ref[own, :]
    for load in loads:
        load.wait()
    lax.fori_loop(1, n_ctx, wait_there, 0)

    grid = (lots, lots)
    to_row = lax.broadcasted_iota(jnp.int32, grid, 0)
    from_row = lax.broadcasted_iota(jnp.int32, grid, 1)
    in_all = lots // experts
    place = (from_row % each) // most * in_all + from_row // each * most + from_row % most
    by_expert = jnp.where(to_row == place, 1.0, 0.0).astype(BF16)
    tokens_in = dot(by_expert, arrived_ref[...])

    share = lots // n_exp
    squares = lax.dot_general(
        jnp.ones((8, local), F32),
        tokens_in * tokens_in,
        (((1,), (1,)), ((), ())),
        preferred_element_type=F32,
        precision=lax.Precision.HIGHEST,
    )
    for to in range(n_exp):
        squares_out[to, :, pl.ds(0, share)] = squares[0:1, to * share : (to + 1) * share]

    def sq_copy(r):
        peer = lax.rem(z + r, n_exp)
        return pltpu.make_async_remote_copy(
            src_ref=squares_out.at[peer],
            dst_ref=squares_in.at[r],
            send_sem=sq_send.at[r],
            recv_sem=sq_recv.at[r],
            device_id=(me, peer),
            device_id_type=pl.DeviceIdType.MESH,
        )

    def start_sq(r, carry):
        sq_copy(r).start()
        return carry

    lax.fori_loop(1, n_exp, start_sq, 0)

    scaled = (tokens_in * gain_ref[...]).astype(BF16)
    for e in range(experts):
        part_ref[pl.ds(e * in_all, in_all), :] = dot(
            scaled[e * in_all : (e + 1) * in_all, :], gu_ref[e]
        ).astype(BF16)
    piece = share // PARTS

    def gu_copy(way, step, part):
        spot = pl.ds(part * piece, piece)
        return along(
            gu_out.at[way, step, spot],
            gu_in.at[way, step, spot],
            gu_send.at[way, step, part],
            gu_recv.at[way, step, part],
            way,
        )

    def gu_term(target, part):
        return part_ref[pl.ds(pl.multiple_of(target * share + part * piece, piece), piece), :].astype(F32)

    def gu_step(step, started):
        for part in range(PARTS):
            for way in range(2):
                fresh = started == 0 or (started == 1 and not far(way, part, PARTS))
                if started == 0 and not far(way, part, PARTS):
                    continue
                spot = pl.ds(part * piece, piece)
                term = gu_term(target_of(way, step), part)
                if not fresh:
                    gu_copy(way, step - 1, part).wait_recv()
                    term = term + gu_in[way, step - 1, spot].astype(F32)
                gu_out[way, step, spot] = term.astype(BF16)
                gu_copy(way, step, part).start()

    gu_step(0, 0)
    gu_step(1, 1)

    def gu_loop(step, carry):
        gu_step(step, 2)
        return carry

    lax.fori_loop(2, half, gu_loop, 0)

    def wait_sq(r, carry):
        sq_copy(r).wait_recv()
        return carry

    lax.fori_loop(1, n_exp, wait_sq, 0)
    squares_in[0] = squares_out[z]
    row = jnp.sum(squares_in[...], axis=0)
    at_lane = lax.broadcasted_iota(jnp.int32, (share, HD), 1)
    at_row = lax.broadcasted_iota(jnp.int32, (share, HD), 0)
    column = jnp.sum(jnp.where(at_lane == at_row, row, 0.0), axis=1, keepdims=True)
    scale = lax.rsqrt(column / (local * n_exp) + EPS)
    for part in range(PARTS):
        spot = pl.ds(part * piece, piece)
        term = gu_term(z, part)
        for way in range(2):
            gu_copy(way, half - 1, part).wait_recv()
            term = term + gu_in[way, half - 1, spot].astype(F32)
        term = term * scale[part * piece : (part + 1) * piece]
        gate, upper = term[:, :units], term[:, units:]
        hidden = gate / (1.0 + jnp.exp(-gate)) * upper
        hidden_ref[pl.ds(pl.multiple_of(z * share + part * piece, piece), piece), :] = hidden.astype(BF16)

    def hid_copy(way, step):
        block = lax.rem(z + n_exp - step, n_exp) if way == 0 else lax.rem(z + step, n_exp)
        spot = pl.ds(pl.multiple_of(block * share, share), share)
        return along(
            hidden_ref.at[spot], hidden_ref.at[spot], hid_send.at[way, step], hid_recv.at[way, step], way
        )

    def hid_arrival(way, step):
        block = lax.rem(z + n_exp - step - 1, n_exp) if way == 0 else lax.rem(z + step + 1, n_exp)
        spot = pl.ds(pl.multiple_of(block * share, share), share)
        return along(
            hidden_ref.at[spot], hidden_ref.at[spot], hid_send.at[way, step], hid_recv.at[way, step], way
        )

    hid_copy(0, 0).start()
    hid_copy(1, 0).start()

    def hid_loop(step, carry):
        for way in range(2):
            hid_arrival(way, step - 1).wait_recv()
            hid_copy(way, step).start()
        return carry

    lax.fori_loop(1, half - 1, hid_loop, 0)
    hid_arrival(0, half - 2).wait_recv()
    hid_copy(0, half - 1).start()
    hid_arrival(1, half - 2).wait_recv()
    hid_arrival(0, half - 1).wait_recv()

    made = jnp.concatenate(
        [dot(hidden_ref[pl.ds(e * in_all, in_all), :], down_ref[e]) for e in range(experts)], axis=0
    ).astype(BF16)
    place_back = (to_row % each) // most * in_all + to_row // each * most + to_row % most
    by_device = jnp.where(from_row == place_back, 1.0, 0.0).astype(BF16)
    made_ref[...] = dot(by_device, made).astype(BF16)

    def home_copy(r):
        peer = lax.rem(me + r, n_ctx)
        return pltpu.make_async_remote_copy(
            src_ref=made_ref.at[pl.ds(pl.multiple_of(peer * each, each), each)],
            dst_ref=back_ref.at[pl.ds(pl.multiple_of(me * each, each), each)],
            send_sem=home_send.at[r],
            recv_sem=home_recv.at[r],
            device_id=(peer, z),
            device_id_type=pl.DeviceIdType.MESH,
        )

    def start_home(r, carry):
        home_copy(r).start()
        return carry

    def wait_home(r, carry):
        home_copy(r).wait_recv()
        return carry

    lax.fori_loop(1, n_ctx, start_home, 0)
    back_ref[own, :] = made_ref[own, :]

    for stream in (key_stream, value_stream, *weight_streams):
        stream.sent()
    def sent_ctx(r, carry):
        there_copy(r).wait_send()
        home_copy(r).wait_send()
        return carry

    def sent_exp(r, carry):
        sq_copy(r).wait_send()
        return carry

    def sent_ring(step, carry):
        for way in range(2):
            for part in range(CHUNKS):
                proj_copy(way, step, part).wait_send()
            for part in range(PARTS):
                gu_copy(way, step, part).wait_send()
        return carry

    for way in range(2):
        for part in range(CHUNKS):
            if far(way, part, CHUNKS):
                proj_copy(way, 0, part).wait_send()
        for part in range(PARTS):
            if far(way, part, PARTS):
                gu_copy(way, 0, part).wait_send()
    lax.fori_loop(1, half, sent_ring, 0)

    def sent_hid(step, carry):
        for way in range(2):
            hid_copy(way, step).wait_send()
        return carry

    lax.fori_loop(0, half - 1, sent_hid, 0)
    hid_copy(0, half - 1).wait_send()
    lax.fori_loop(1, n_exp, sent_exp, 0)
    lax.fori_loop(1, n_ctx, wait_home, 0)
    lax.fori_loop(1, n_ctx, sent_ctx, 0)

    spread = jnp.where(
        lax.broadcasted_iota(jnp.int32, (tokens, lots), 1) == slot_col, 1.0, 0.0
    ).astype(BF16)
    out_ref[...] = dot(spread, back_ref[...]).astype(BF16)


def layer(n_ctx, n_exp, query, route_col, route_row, gain, keys, values, weight, gate, up, down):
    tokens, local = query.shape
    experts, _, units = gate.shape
    most = 2 * tokens // (experts * n_ctx)
    lots = n_ctx * experts * most
    share = lots // n_exp
    half = n_exp // 2
    heads = local // HD
    dma = pltpu.SemaphoreType.DMA
    vmem = pl.BlockSpec(memory_space=pltpu.VMEM)
    anywhere = pl.BlockSpec(memory_space=pl.ANY)
    return pl.pallas_call(
        functools.partial(layer_kernel, n_ctx, n_exp),
        out_shape=jax.ShapeDtypeStruct((tokens, local), BF16),
        in_specs=[vmem] * 4 + [anywhere] * 6,
        out_specs=vmem,
        scratch_shapes=[
            pltpu.VMEM((2, n_ctx, tokens, HD), BF16),
            pltpu.VMEM((n_ctx, *weight.shape), BF16),
            pltpu.VMEM((heads, tokens, 1), F32),
            pltpu.VMEM((heads, tokens, 2 * HD), F32),
            pltpu.VMEM((tokens, local), BF16),
            pltpu.VMEM((experts, local, 2 * units), BF16),
            pltpu.VMEM((experts, units, local), BF16),
            pltpu.VMEM((2, half, tokens, local), BF16),
            pltpu.VMEM((2, half, tokens, local), BF16),
            pltpu.VMEM((tokens, local), BF16),
            pltpu.VMEM((lots, local), BF16),
            pltpu.VMEM((lots, local), BF16),
            pltpu.VMEM((lots, 2 * units), BF16),
            pltpu.VMEM((2, half, share, 2 * units), BF16),
            pltpu.VMEM((2, half, share, 2 * units), BF16),
            pltpu.VMEM((n_exp, 1, HD), F32),
            pltpu.VMEM((n_exp, 1, HD), F32),
            pltpu.VMEM((lots, units), BF16),
            pltpu.VMEM((lots, local), BF16),
            pltpu.VMEM((lots, local), BF16),
            dma((6,)),
            dma((4, MESSAGES)),
            dma((4, MESSAGES)),
            dma((2, half, CHUNKS)),
            dma((2, half, CHUNKS)),
            dma((n_ctx,)),
            dma((n_ctx,)),
            dma((2, half, PARTS)),
            dma((2, half, PARTS)),
            dma((n_exp,)),
            dma((n_exp,)),
            dma((2, half)),
            dma((2, half)),
            dma((n_ctx,)),
            dma((n_ctx,)),
        ],
        compiler_params=pltpu.CompilerParams(
            collective_id=0, has_side_effects=True, vmem_limit_bytes=VMEM_LIMIT
        ),
        name="layer",
    )(query, route_col, route_row, gain, keys, values, weight, gate, up, down)


def body(
    queries,
    keys,
    values,
    routes,
    route_score,
    output_weight,
    norm_gain,
    gate_weight,
    up_weight,
    down_weight,
):
    tokens, local = queries.shape[1:]
    returned = layer(
        lax.axis_size("ctx"),
        lax.axis_size("exp"),
        queries[0],
        routes[0],
        routes[0].reshape(1, tokens),
        norm_gain.reshape(1, local),
        keys[0],
        values[0],
        output_weight,
        gate_weight,
        up_weight,
        down_weight,
    )
    scored = route_score[0][:, None] * returned.astype(F32)
    return scored.astype(BF16)[None]


def solution(mesh):
    placed = (
        P(None, "ctx", "exp"),
        P(None, "ctx", None),
        P(None, "ctx", None),
        P(None, "ctx", None),
        P(None, "ctx"),
        P("exp", "ctx"),
        P("exp"),
        P("ctx", "exp", None),
        P("ctx", "exp", None),
        P("ctx", None, "exp"),
    )
    return jax.shard_map(
        body, mesh=mesh, in_specs=placed, out_specs=P(None, "ctx", "exp"), check_vma=False
    )
```

```python
import functools
import math

import jax
import jax.numpy as jnp
from jax import lax
from jax.experimental import pallas as pl
from jax.experimental.pallas import tpu as pltpu
from jax.sharding import PartitionSpec as P

HD = 128
EPS = 1e-05
FAR_BELOW = -1e30
F32 = jnp.float32
BF16 = jnp.bfloat16
VMEM_LIMIT = 56 * 1024 * 1024


def dot(a, b):
    return jnp.dot(a, b, preferred_element_type=F32)


NX = 4
NY = 4
STEPS_OFF = (0, 1, -1, 2)
MESSAGES = 36
CHUNKS = 4
PARTS = 2


def layer_kernel(
    n_ctx,
    n_exp,
    query_ref,
    route_ref,
    gain_ref,
    keys_hbm,
    values_hbm,
    weight_hbm,
    gate_hbm,
    up_hbm,
    down_hbm,
    out_ref,
    kv_ref,
    weight_ref,
    high_ref,
    total_ref,
    attn_ref,
    gu_ref,
    down_ref,
    proj_out,
    proj_in,
    proj_ref,
    term_ref,
    pick_ref,
    spread_ref,
    by_expert_ref,
    by_device_ref,
    packed_ref,
    arrived_ref,
    scaled_ref,
    part_ref,
    gu_out,
    gu_in,
    squares_out,
    squares_in,
    hidden_ref,
    made_ref,
    back_ref,
    load_sem,
    flow_send,
    flow_recv,
    proj_send,
    proj_recv,
    there_send,
    there_recv,
    gu_send,
    gu_recv,
    sq_send,
    sq_recv,
    hid_send,
    hid_recv,
    home_send,
    home_recv,
):
    me = lax.axis_index("ctx")
    z = lax.axis_index("exp")
    half = n_exp // 2
    tokens, local = query_ref.shape
    experts, _, twice = gu_ref.shape
    units = twice // 2
    lots = packed_ref.shape[0]
    each = lots // n_ctx
    most = each // experts
    neighbour = (lax.rem(z + 1, n_exp), lax.rem(z + n_exp - 1, n_exp))

    kv_heads = keys_hbm.shape[1] // HD
    columns = pl.ds(pl.multiple_of(z * kv_heads // n_exp * HD, HD), HD)
    own_loads = [
        pltpu.make_async_copy(keys_hbm.at[:, columns], kv_ref.at[0, me], load_sem.at[3]),
        pltpu.make_async_copy(values_hbm.at[:, columns], kv_ref.at[1, me], load_sem.at[4]),
        pltpu.make_async_copy(weight_hbm, weight_ref.at[me], load_sem.at[5]),
    ]
    for load in own_loads:
        load.start()
    loads = [
        pltpu.make_async_copy(gate_hbm, gu_ref.at[:, :, pl.ds(0, units)], load_sem.at[0]),
        pltpu.make_async_copy(up_hbm, gu_ref.at[:, :, pl.ds(units, units)], load_sem.at[1]),
        pltpu.make_async_copy(down_hbm, down_ref, load_sem.at[2]),
    ]
    for load in loads:
        load.start()

    barrier = pltpu.get_barrier_semaphore()

    def greet_ctx(r, carry):
        pl.semaphore_signal(
            barrier, inc=1, device_id=(lax.rem(me + r, n_ctx), z), device_id_type=pl.DeviceIdType.MESH
        )
        return carry

    def greet_exp(r, carry):
        pl.semaphore_signal(
            barrier, inc=1, device_id=(me, lax.rem(z + r, n_exp)), device_id_type=pl.DeviceIdType.MESH
        )
        return carry

    lax.fori_loop(1, n_ctx, greet_ctx, 0)
    lax.fori_loop(1, n_exp, greet_exp, 0)
    pl.semaphore_wait(barrier, n_ctx - 1 + n_exp - 1)

    def along(source, target, send_sem, recv_sem, way):
        return pltpu.make_async_remote_copy(
            src_ref=source,
            dst_ref=target,
            send_sem=send_sem,
            recv_sem=recv_sem,
            device_id=(me, neighbour[way]),
            device_id_type=pl.DeviceIdType.MESH,
        )

    def target_of(way, step):
        if way == 0:
            return lax.rem(z + half - step, n_exp)
        return lax.rem(z + n_exp - half + step, n_exp)

    lane = me % 2
    chip = me // 2
    at_x, at_y = chip // NY, chip % NY

    def chip_at(dx, dy):
        return lax.rem(at_x + dx + NX, NX) * NY + lax.rem(at_y + dy + NY, NY)

    class Stream:
        def __init__(self, number, ref, first_row, rows, y_first):
            self.number, self.ref, self.first_row, self.rows = number, ref, first_row, rows
            self.y_first = y_first

        def chip(self, da, db):
            return chip_at(db, da) if self.y_first else chip_at(da, db)

        def copy(self, message, da, db, part, to, its_lane=None):
            start, size = self.first_row, self.rows
            if part is not None:
                size = size // 2
                start = start + part * size
            block = self.chip(da, db) * 2 + (lane if its_lane is None else its_lane)
            here = self.ref.at[block, pl.ds(start, size)]
            target = self.chip(0, 0) * 2 + 1 - lane if to is None else self.chip(*to) * 2 + lane
            return pltpu.make_async_remote_copy(
                src_ref=here,
                dst_ref=here,
                send_sem=flow_send.at[self.number, message],
                recv_sem=flow_recv.at[self.number, message],
                device_id=(target, z),
                device_id_type=pl.DeviceIdType.MESH,
            )

        def first(self, side):
            return self.copy(side, 0, 0, None, ((1, 0), (-1, 0))[side])

        def first_in(self, side):
            return self.copy(side, (-1, 1)[side], 0, None, (1, 0))

        def relay(self, side):
            return self.copy(2 + side, (-1, 1)[side], 0, side, ((1, 0), (-1, 0))[side])

        def relay_in(self, side):
            return self.copy(2 + side, 2, 0, side, (1, 0))

        def second(self, i, side):
            return self.copy(4 + 2 * i + side, STEPS_OFF[i], 0, None, ((0, 1), (0, -1))[side])

        def second_in(self, i, side):
            return self.copy(4 + 2 * i + side, STEPS_OFF[i], (-1, 1)[side], None, (0, 1))

        def pass_on(self, i, side):
            return self.copy(
                12 + 2 * i + side, STEPS_OFF[i], (-1, 1)[side], side, ((0, 1), (0, -1))[side]
            )

        def pass_on_in(self, i, side):
            return self.copy(12 + 2 * i + side, STEPS_OFF[i], 2, side, (0, 1))

        def twin(self, i, j):
            return self.copy(20 + 4 * i + j, STEPS_OFF[i], STEPS_OFF[j], None, None)

        def twin_in(self, i, j):
            return self.copy(20 + 4 * i + j, STEPS_OFF[i], STEPS_OFF[j], None, None, 1 - lane)

        def stage(self, number):
            if number == 0:
                for side in range(2):
                    self.first(side).start()
                    self.second(0, side).start()
                self.twin(0, 0).start()
            if number == 1:
                for side in range(2):
                    self.first_in(side).wait_recv()
                    self.relay(side).start()
                    i = 2 - side
                    self.second(i, 0).start()
                    self.second(i, 1).start()
                    self.twin(i, 0).start()
                for side in range(2):
                    self.second_in(0, side).wait_recv()
                    self.pass_on(0, side).start()
                    self.twin(0, 2 - side).start()
            if number == 2:
                for side in range(2):
                    self.relay_in(side).wait_recv()
                for side in range(2):
                    self.second(3, side).start()
                self.twin(3, 0).start()
                for side in range(2):
                    self.pass_on_in(0, side).wait_recv()
                self.twin(0, 3).start()
            if number == 3:
                for i in (1, 2):
                    for side in range(2):
                        self.second_in(i, side).wait_recv()
                        self.pass_on(i, side).start()
                        self.twin(i, 2 - side).start()
            if number == 4:
                for side in range(2):
                    self.second_in(3, side).wait_recv()
                    self.pass_on(3, side).start()
                    self.twin(3, 2 - side).start()
                for i in (1, 2):
                    for side in range(2):
                        self.pass_on_in(i, side).wait_recv()
                    self.twin(i, 3).start()
            if number == 5:
                for side in range(2):
                    self.pass_on_in(3, side).wait_recv()
                self.twin(3, 3).start()

        def sent(self):
            for side in range(2):
                self.first(side).wait_send()
                self.relay(side).wait_send()
                for i in range(4):
                    self.second(i, side).wait_send()
                    self.pass_on(i, side).wait_send()
            for i in range(4):
                for j in range(4):
                    self.twin(i, j).wait_send()

    rows_of_weight = weight_hbm.shape[0]
    key_stream = Stream(0, kv_ref.at[0], 0, tokens, True)
    value_stream = Stream(1, kv_ref.at[1], 0, tokens, False)
    weight_streams = (
        Stream(2, weight_ref, 0, rows_of_weight // 2, True),
        Stream(3, weight_ref, rows_of_weight // 2, rows_of_weight // 2, False),
    )

    def kv_stage(number):
        key_stream.stage(number)
        value_stream.stage(number)

    def weight_stage(number):
        for stream in weight_streams:
            stream.stage(number)

    heads = local // HD
    block = 2 * tokens
    factor = math.log2(math.e) / math.sqrt(HD)

    def attend(dx, dy, own):
        i, j = STEPS_OFF.index(dy), STEPS_OFF.index(dx)
        key_stream.twin_in(i, j).wait_recv()
        value_stream.twin_in(j, i).wait_recv()
        source = chip_at(dx, dy)

        def compute():
            keys = kv_ref[0, pl.ds(source * 2, 2)].reshape(block, HD)
            values = kv_ref[1, pl.ds(source * 2, 2)].reshape(block, HD)
            values = jnp.concatenate([values, jnp.ones((block, HD), BF16)], axis=1)
            for head in range(heads):
                query = query_ref[:, head * HD : (head + 1) * HD]
                scores = lax.dot_general(
                    query, keys, (((1,), (1,)), ((), ())), preferred_element_type=F32
                )
                if own:
                    shape = (tokens, block)
                    spot = lane * tokens + lax.broadcasted_iota(jnp.int32, shape, 0)
                    visible = lax.broadcasted_iota(jnp.int32, shape, 1) <= spot
                    scores = jnp.where(visible, scores, FAR_BELOW)
                highest = jnp.max(scores, axis=1, keepdims=True)
                if not own:
                    before = high_ref[head]
                    highest = jnp.maximum(highest, before)
                weights = jnp.exp2((scores - highest) * factor).astype(BF16)
                summed = dot(weights, values)
                if not own:
                    summed = summed + total_ref[head] * jnp.exp2((before - highest) * factor)
                total_ref[head] = summed
                high_ref[head] = highest

        if own:
            compute()
        else:
            pl.when(source < chip)(compute)

    in_all = lots // experts

    def make_tables():
        chosen_row = route_ref[...]
        square = (tokens, tokens)
        down_axis = lax.broadcasted_iota(jnp.int32, square, 0)
        over_axis = lax.broadcasted_iota(jnp.int32, square, 1)
        chosen_col = jnp.sum(
            jnp.where(down_axis == over_axis, chosen_row.astype(F32), 0.0), axis=1, keepdims=True
        ).astype(jnp.int32)
        same = chosen_col == chosen_row
        rank_col = jnp.sum(
            jnp.where(same & (over_axis < down_axis), 1.0, 0.0), axis=1, keepdims=True
        ).astype(jnp.int32)
        rank_row = jnp.sum(
            jnp.where(same & (down_axis < over_axis), 1.0, 0.0), axis=0, keepdims=True
        ).astype(jnp.int32)
        slot_col = chosen_col * most + rank_col
        slot_row = chosen_row * most + rank_row
        pick_ref[...] = jnp.where(
            lax.broadcasted_iota(jnp.int32, (lots, tokens), 0) == slot_row, 1.0, 0.0
        ).astype(BF16)
        spread_ref[...] = jnp.where(
            lax.broadcasted_iota(jnp.int32, (tokens, lots), 1) == slot_col, 1.0, 0.0
        ).astype(BF16)
        lot = lax.broadcasted_iota(jnp.int32, (1, lots), 1)
        to_row = lax.broadcasted_iota(jnp.int32, (lots, lots), 0)
        place = (lot % each) // most * in_all + lot // each * most + lot % most
        by_expert_ref[...] = jnp.where(to_row == place, 1.0, 0.0).astype(BF16)
        place = (lot % in_all) // most * each + lot // in_all * most + lot % most
        by_device_ref[...] = jnp.where(to_row == place, 1.0, 0.0).astype(BF16)

    for load in own_loads:
        load.wait()
    kv_stage(0)
    make_tables()
    attend(0, 0, True)
    kv_stage(1)
    weight_stage(0)
    for dx, dy in ((0, -1), (-1, 0)):
        attend(dx, dy, False)
    kv_stage(2)
    for dx, dy in ((0, 1), (1, 0)):
        attend(dx, dy, False)
    weight_stage(1)
    for dx, dy in ((0, 2), (2, 0)):
        attend(dx, dy, False)
    kv_stage(3)
    weight_stage(2)
    for dx, dy in ((-1, -1), (-1, 1), (1, -1), (1, 1)):
        attend(dx, dy, False)
    kv_stage(4)
    weight_stage(3)
    for dx, dy in ((2, -1), (2, 1), (-1, 2), (1, 2)):
        attend(dx, dy, False)
    kv_stage(5)
    weight_stage(4)
    attend(2, 2, False)
    weight_stage(5)
    for head in range(heads):
        summed = total_ref[head]
        attn_ref[:, head * HD : (head + 1) * HD] = (summed[:, :HD] / summed[:, HD:]).astype(BF16)
    for stream in weight_streams:
        for i in range(4):
            for j in range(4):
                stream.twin_in(i, j).wait_recv()

    rows = tokens // CHUNKS
    pairs = n_ctx // n_exp

    def proj_copy(way, step, part):
        spot = pl.ds(part * rows, rows)
        return along(
            proj_out.at[way, step, spot],
            proj_in.at[way, step, spot],
            proj_send.at[way, step, part],
            proj_recv.at[way, step, part],
            way,
        )

    def make_term(target):
        columns = jnp.concatenate(
            [weight_ref[target * pairs + i] for i in range(pairs)], axis=1
        )
        term_ref[target] = dot(attn_ref[...], columns).astype(BF16)

    def proj_term(target, part):
        return term_ref[target, pl.ds(part * rows, rows)].astype(F32)

    def far(way, part, parts):
        return (part < parts // 2) == (way == 0)

    def proj_step(step, started):
        for part in range(CHUNKS):
            for way in range(2):
                fresh = started == 0 or (started == 1 and not far(way, part, CHUNKS))
                if started == 0 and not far(way, part, CHUNKS):
                    continue
                spot = pl.ds(part * rows, rows)
                term = proj_term(target_of(way, step), part)
                if not fresh:
                    proj_copy(way, step - 1, part).wait_recv()
                    term = term + proj_in[way, step - 1, spot].astype(F32)
                proj_out[way, step, spot] = term.astype(BF16)
                proj_copy(way, step, part).start()

    make_term(target_of(0, 0))
    proj_step(0, 0)
    make_term(target_of(0, 1))
    make_term(target_of(1, 1))
    proj_step(1, 1)

    def proj_loop(step, carry):
        make_term(target_of(0, step))
        make_term(target_of(1, step))
        proj_step(step, 2)
        for i, stream in enumerate((key_stream, value_stream, *weight_streams)):
            pl.when(step == 2 + i)(stream.sent)
        return carry

    lax.fori_loop(2, half, proj_loop, 0)
    make_term(z)
    for part in range(CHUNKS):
        spot = pl.ds(part * rows, rows)
        term = proj_term(z, part)
        for way in range(2):
            proj_copy(way, half - 1, part).wait_recv()
            term = term + proj_in[way, half - 1, spot].astype(F32)
        proj_ref[spot, :] = term.astype(BF16)

    packed_ref[...] = dot(pick_ref[...], proj_ref[...]).astype(BF16)

    def there_copy(r):
        peer = lax.rem(me + r, n_ctx)
        return pltpu.make_async_remote_copy(
            src_ref=packed_ref.at[pl.ds(pl.multiple_of(peer * each, each), each)],
            dst_ref=arrived_ref.at[pl.ds(pl.multiple_of(me * each, each), each)],
            send_sem=there_send.at[r],
            recv_sem=there_recv.at[r],
            device_id=(peer, z),
            device_id_type=pl.DeviceIdType.MESH,
        )

    def start_there(r, carry):
        there_copy(r).start()
        return carry

    def wait_there(r, carry):
        there_copy(r).wait_recv()
        return carry

    lax.fori_loop(1, n_ctx, start_there, 0)
    own = pl.ds(pl.multiple_of(me * each, each), each)
    arrived_ref[own, :] = packed_ref[own, :]
    for load in loads:
        load.wait()
    lax.fori_loop(1, n_ctx, wait_there, 0)

    share = lots // n_exp
    tokens_in = dot(by_expert_ref[...], arrived_ref[...])
    scaled_ref[...] = (tokens_in * gain_ref[...]).astype(BF16)
    first_expert = lax.rem(z + half, n_exp) * share // in_all

    def make_part(i):
        e = lax.rem(first_expert + i, experts)
        spot = pl.ds(pl.multiple_of(e * in_all, in_all), in_all)
        part_ref[spot, :] = dot(scaled_ref[spot, :], gu_ref[e]).astype(BF16)

    piece = share // PARTS

    def gu_copy(way, step, part):
        spot = pl.ds(part * piece, piece)
        return along(
            gu_out.at[way, step, spot],
            gu_in.at[way, step, spot],
            gu_send.at[way, step, part],
            gu_recv.at[way, step, part],
            way,
        )

    def gu_term(target, part):
        return part_ref[pl.ds(pl.multiple_of(target * share + part * piece, piece), piece), :].astype(F32)

    def gu_step(step, started):
        for part in range(PARTS):
            for way in range(2):
                fresh = started == 0 or (started == 1 and not far(way, part, PARTS))
                if started == 0 and not far(way, part, PARTS):
                    continue
                spot = pl.ds(part * piece, piece)
                term = gu_term(target_of(way, step), part)
                if not fresh:
                    gu_copy(way, step - 1, part).wait_recv()
                    term = term + gu_in[way, step - 1, spot].astype(F32)
                gu_out[way, step, spot] = term.astype(BF16)
                gu_copy(way, step, part).start()

    make_part(0)
    gu_step(0, 0)
    for i in range(1, experts):
        make_part(i)
    gu_step(1, 1)

    squares = lax.dot_general(
        jnp.ones((8, local), BF16),
        (tokens_in * tokens_in).astype(BF16),
        (((1,), (1,)), ((), ())),
        preferred_element_type=F32,
    )
    for to in range(n_exp):
        squares_out[to, :, pl.ds(0, share)] = squares[0:1, to * share : (to + 1) * share]

    def sq_copy(r):
        peer = lax.rem(z + r, n_exp)
        return pltpu.make_async_remote_copy(
            src_ref=squares_out.at[peer],
            dst_ref=squares_in.at[r],
            send_sem=sq_send.at[r],
            recv_sem=sq_recv.at[r],
            device_id=(me, peer),
            device_id_type=pl.DeviceIdType.MESH,
        )

    def start_sq(r, carry):
        sq_copy(r).start()
        return carry

    lax.fori_loop(1, n_exp, start_sq, 0)

    def gu_loop(step, carry):
        gu_step(step, 2)
        for way in range(2):
            for part in range(CHUNKS):
                proj_copy(way, step, part).wait_send()
        return carry

    lax.fori_loop(2, half, gu_loop, 0)

    def wait_sq(r, carry):
        sq_copy(r).wait_recv()
        return carry

    lax.fori_loop(1, n_exp, wait_sq, 0)
    squares_in[0] = squares_out[z]
    row = jnp.sum(squares_in[...], axis=0)
    at_lane = lax.broadcasted_iota(jnp.int32, (share, HD), 1)
    at_row = lax.broadcasted_iota(jnp.int32, (share, HD), 0)
    column = jnp.sum(jnp.where(at_lane == at_row, row, 0.0), axis=1, keepdims=True)
    scale = lax.rsqrt(column / (local * n_exp) + EPS)
    for part in range(PARTS):
        spot = pl.ds(part * piece, piece)
        term = gu_term(z, part)
        for way in range(2):
            gu_copy(way, half - 1, part).wait_recv()
            term = term + gu_in[way, half - 1, spot].astype(F32)
        term = term * scale[part * piece : (part + 1) * piece]
        gate, upper = term[:, :units], term[:, units:]
        hidden = gate / (1.0 + jnp.exp(-gate)) * upper
        hidden_ref[pl.ds(pl.multiple_of(z * share + part * piece, piece), piece), :] = hidden.astype(BF16)

    def hid_copy(way, step, part, ahead=0):
        block = lax.rem(z + n_exp - step - ahead, n_exp) if way == 0 else lax.rem(z + step + ahead, n_exp)
        spot = pl.ds(pl.multiple_of(block * share + part * piece, piece), piece)
        return along(
            hidden_ref.at[spot],
            hidden_ref.at[spot],
            hid_send.at[way, step, part],
            hid_recv.at[way, step, part],
            way,
        )

    def hid_arrival(way, step, part):
        return hid_copy(way, step, part, 1)

    for part in range(PARTS):
        hid_copy(0, 0, part).start()
        hid_copy(1, 0, part).start()

    def hid_loop(step, carry):
        for part in range(PARTS):
            for way in range(2):
                hid_arrival(way, step - 1, part).wait_recv()
                hid_copy(way, step, part).start()
        for way in range(2):
            for part in range(PARTS):
                gu_copy(way, step, part).wait_send()
        return carry

    lax.fori_loop(1, half - 1, hid_loop, 0)
    for part in range(PARTS):
        hid_arrival(0, half - 2, part).wait_recv()
        hid_copy(0, half - 1, part).start()
    for part in range(PARTS):
        hid_arrival(1, half - 2, part).wait_recv()
    for part in range(PARTS):
        hid_arrival(0, half - 1, part).wait_recv()

    made = jnp.concatenate(
        [dot(hidden_ref[pl.ds(e * in_all, in_all), :], down_ref[e]) for e in range(experts)], axis=0
    ).astype(BF16)
    made_ref[...] = dot(by_device_ref[...], made).astype(BF16)

    def home_copy(r):
        peer = lax.rem(me + r, n_ctx)
        return pltpu.make_async_remote_copy(
            src_ref=made_ref.at[pl.ds(pl.multiple_of(peer * each, each), each)],
            dst_ref=back_ref.at[pl.ds(pl.multiple_of(me * each, each), each)],
            send_sem=home_send.at[r],
            recv_sem=home_recv.at[r],
            device_id=(peer, z),
            device_id_type=pl.DeviceIdType.MESH,
        )

    def start_home(r, carry):
        home_copy(r).start()
        return carry

    def wait_home(r, carry):
        home_copy(r).wait_recv()
        return carry

    lax.fori_loop(1, n_ctx, start_home, 0)
    back_ref[own, :] = made_ref[own, :]

    def sent_ctx(r, carry):
        there_copy(r).wait_send()
        return carry

    def sent_home(r, carry):
        home_copy(r).wait_send()
        return carry

    def sent_exp(r, carry):
        sq_copy(r).wait_send()
        return carry

    for way in range(2):
        for part in range(CHUNKS):
            if far(way, part, CHUNKS):
                proj_copy(way, 0, part).wait_send()
            proj_copy(way, 1, part).wait_send()
        for part in range(PARTS):
            if far(way, part, PARTS):
                gu_copy(way, 0, part).wait_send()
            gu_copy(way, half - 1, part).wait_send()

    def sent_hid(step, carry):
        for way in range(2):
            for part in range(PARTS):
                hid_copy(way, step, part).wait_send()
        return carry

    lax.fori_loop(0, half - 1, sent_hid, 0)
    for part in range(PARTS):
        hid_copy(0, half - 1, part).wait_send()
    lax.fori_loop(1, n_exp, sent_exp, 0)
    lax.fori_loop(1, n_ctx, sent_ctx, 0)
    lax.fori_loop(1, n_ctx, wait_home, 0)
    out_ref[...] = dot(spread_ref[...], back_ref[...]).astype(BF16)
    lax.fori_loop(1, n_ctx, sent_home, 0)


def layer(n_ctx, n_exp, query, route, gain, keys, values, weight, gate, up, down):
    tokens, local = query.shape
    experts, _, units = gate.shape
    most = 2 * tokens // (experts * n_ctx)
    lots = n_ctx * experts * most
    share = lots // n_exp
    half = n_exp // 2
    heads = local // HD
    dma = pltpu.SemaphoreType.DMA
    vmem = pl.BlockSpec(memory_space=pltpu.VMEM)
    anywhere = pl.BlockSpec(memory_space=pl.ANY)
    return pl.pallas_call(
        functools.partial(layer_kernel, n_ctx, n_exp),
        out_shape=jax.ShapeDtypeStruct((tokens, local), BF16),
        in_specs=[vmem] * 3 + [anywhere] * 6,
        out_specs=vmem,
        scratch_shapes=[
            pltpu.VMEM((2, n_ctx, tokens, HD), BF16),
            pltpu.VMEM((n_ctx, *weight.shape), BF16),
            pltpu.VMEM((heads, tokens, 1), F32),
            pltpu.VMEM((heads, tokens, 2 * HD), F32),
            pltpu.VMEM((tokens, local), BF16),
            pltpu.VMEM((experts, local, 2 * units), BF16),
            pltpu.VMEM((experts, units, local), BF16),
            pltpu.VMEM((2, half, tokens, local), BF16),
            pltpu.VMEM((2, half, tokens, local), BF16),
            pltpu.VMEM((tokens, local), BF16),
            pltpu.VMEM((n_exp, tokens, local), BF16),
            pltpu.VMEM((lots, tokens), BF16),
            pltpu.VMEM((tokens, lots), BF16),
            pltpu.VMEM((lots, lots), BF16),
            pltpu.VMEM((lots, lots), BF16),
            pltpu.VMEM((lots, local), BF16),
            pltpu.VMEM((lots, local), BF16),
            pltpu.VMEM((lots, local), BF16),
            pltpu.VMEM((lots, 2 * units), BF16),
            pltpu.VMEM((2, half, share, 2 * units), BF16),
            pltpu.VMEM((2, half, share, 2 * units), BF16),
            pltpu.VMEM((n_exp, 1, HD), F32),
            pltpu.VMEM((n_exp, 1, HD), F32),
            pltpu.VMEM((lots, units), BF16),
            pltpu.VMEM((lots, local), BF16),
            pltpu.VMEM((lots, local), BF16),
            dma((6,)),
            dma((4, MESSAGES)),
            dma((4, MESSAGES)),
            dma((2, half, CHUNKS)),
            dma((2, half, CHUNKS)),
            dma((n_ctx,)),
            dma((n_ctx,)),
            dma((2, half, PARTS)),
            dma((2, half, PARTS)),
            dma((n_exp,)),
            dma((n_exp,)),
            dma((2, half, PARTS)),
            dma((2, half, PARTS)),
            dma((n_ctx,)),
            dma((n_ctx,)),
        ],
        compiler_params=pltpu.CompilerParams(
            collective_id=0, has_side_effects=True, vmem_limit_bytes=VMEM_LIMIT
        ),
        name="layer",
    )(query, route, gain, keys, values, weight, gate, up, down)


def body(
    queries,
    keys,
    values,
    routes,
    route_score,
    output_weight,
    norm_gain,
    gate_weight,
    up_weight,
    down_weight,
):
    tokens, local = queries.shape[1:]
    returned = layer(
        lax.axis_size("ctx"),
        lax.axis_size("exp"),
        queries[0],
        routes[0].reshape(1, tokens),
        norm_gain.reshape(1, local),
        keys[0],
        values[0],
        output_weight,
        gate_weight,
        up_weight,
        down_weight,
    )
    scored = route_score[0][:, None] * returned.astype(F32)
    return scored.astype(BF16)[None]


def solution(mesh):
    placed = (
        P(None, "ctx", "exp"),
        P(None, "ctx", None),
        P(None, "ctx", None),
        P(None, "ctx", None),
        P(None, "ctx"),
        P("exp", "ctx"),
        P("exp"),
        P("ctx", "exp", None),
        P("ctx", "exp", None),
        P("ctx", None, "exp"),
    )
    return jax.shard_map(
        body, mesh=mesh, in_specs=placed, out_specs=P(None, "ctx", "exp"), check_vma=False
    )
```

```python
import functools
import math

import jax
import jax.numpy as jnp
from jax import lax
from jax.experimental import pallas as pl
from jax.experimental.pallas import tpu as pltpu
from jax.sharding import PartitionSpec as P

HD = 128
EPS = 1e-05
FAR_BELOW = -1e30
F32 = jnp.float32
BF16 = jnp.bfloat16
VMEM_LIMIT = 56 * 1024 * 1024


def dot(a, b):
    return jnp.dot(a, b, preferred_element_type=F32)


NX = 4
NY = 4
STEPS_OFF = (0, 1, -1, 2)
MESSAGES = 36
CHUNKS = 4
PARTS = 2


def layer_kernel(
    n_ctx,
    n_exp,
    query_ref,
    route_ref,
    gain_ref,
    keys_hbm,
    values_hbm,
    weight_hbm,
    gate_hbm,
    up_hbm,
    down_hbm,
    out_ref,
    kv_ref,
    weight_ref,
    high_ref,
    total_ref,
    attn_ref,
    gu_ref,
    down_ref,
    proj_out,
    proj_in,
    proj_ref,
    term_ref,
    pick_ref,
    spread_ref,
    by_expert_ref,
    by_device_ref,
    packed_ref,
    arrived_ref,
    scaled_ref,
    part_ref,
    gu_out,
    gu_in,
    squares_out,
    squares_in,
    hidden_ref,
    made_ref,
    back_ref,
    load_sem,
    flow_send,
    flow_recv,
    proj_send,
    proj_recv,
    there_send,
    there_recv,
    gu_send,
    gu_recv,
    sq_send,
    sq_recv,
    hid_send,
    hid_recv,
    home_send,
    home_recv,
):
    me = lax.axis_index("ctx")
    z = lax.axis_index("exp")
    half = n_exp // 2
    tokens, local = query_ref.shape
    experts, _, twice = gu_ref.shape
    units = twice // 2
    lots = packed_ref.shape[0]
    each = lots // n_ctx
    most = each // experts
    neighbour = (lax.rem(z + 1, n_exp), lax.rem(z + n_exp - 1, n_exp))

    kv_heads = keys_hbm.shape[1] // HD
    columns = pl.ds(pl.multiple_of(z * kv_heads // n_exp * HD, HD), HD)
    own_loads = [
        pltpu.make_async_copy(keys_hbm.at[:, columns], kv_ref.at[0, me], load_sem.at[3]),
        pltpu.make_async_copy(values_hbm.at[:, columns], kv_ref.at[1, me], load_sem.at[4]),
        pltpu.make_async_copy(weight_hbm, weight_ref.at[me], load_sem.at[5]),
    ]
    for load in own_loads:
        load.start()
    loads = [
        pltpu.make_async_copy(gate_hbm, gu_ref.at[:, :, pl.ds(0, units)], load_sem.at[0]),
        pltpu.make_async_copy(up_hbm, gu_ref.at[:, :, pl.ds(units, units)], load_sem.at[1]),
        pltpu.make_async_copy(down_hbm, down_ref, load_sem.at[2]),
    ]
    for load in loads:
        load.start()

    barrier = pltpu.get_barrier_semaphore()

    def greet_ctx(r, carry):
        pl.semaphore_signal(
            barrier, inc=1, device_id=(lax.rem(me + r, n_ctx), z), device_id_type=pl.DeviceIdType.MESH
        )
        return carry

    def greet_exp(r, carry):
        pl.semaphore_signal(
            barrier, inc=1, device_id=(me, lax.rem(z + r, n_exp)), device_id_type=pl.DeviceIdType.MESH
        )
        return carry

    lax.fori_loop(1, n_ctx, greet_ctx, 0)
    lax.fori_loop(1, n_exp, greet_exp, 0)
    pl.semaphore_wait(barrier, n_ctx - 1 + n_exp - 1)

    def along(source, target, send_sem, recv_sem, way):
        return pltpu.make_async_remote_copy(
            src_ref=source,
            dst_ref=target,
            send_sem=send_sem,
            recv_sem=recv_sem,
            device_id=(me, neighbour[way]),
            device_id_type=pl.DeviceIdType.MESH,
        )

    def target_of(way, step):
        if way == 0:
            return lax.rem(z + half - step, n_exp)
        return lax.rem(z + n_exp - half + step, n_exp)

    lane = me % 2
    chip = me // 2
    at_x, at_y = chip // NY, chip % NY

    def chip_at(dx, dy):
        return lax.rem(at_x + dx + NX, NX) * NY + lax.rem(at_y + dy + NY, NY)

    class Stream:
        def __init__(self, number, ref, first_row, rows, y_first):
            self.number, self.ref, self.first_row, self.rows = number, ref, first_row, rows
            self.y_first = y_first

        def chip(self, da, db):
            return chip_at(db, da) if self.y_first else chip_at(da, db)

        def copy(self, message, da, db, part, to, its_lane=None):
            start, size = self.first_row, self.rows
            if part is not None:
                size = size // 2
                start = start + part * size
            block = self.chip(da, db) * 2 + (lane if its_lane is None else its_lane)
            here = self.ref.at[block, pl.ds(start, size)]
            target = self.chip(0, 0) * 2 + 1 - lane if to is None else self.chip(*to) * 2 + lane
            return pltpu.make_async_remote_copy(
                src_ref=here,
                dst_ref=here,
                send_sem=flow_send.at[self.number, message],
                recv_sem=flow_recv.at[self.number, message],
                device_id=(target, z),
                device_id_type=pl.DeviceIdType.MESH,
            )

        def first(self, side):
            return self.copy(side, 0, 0, None, ((1, 0), (-1, 0))[side])

        def first_in(self, side):
            return self.copy(side, (-1, 1)[side], 0, None, (1, 0))

        def relay(self, side):
            return self.copy(2 + side, (-1, 1)[side], 0, side, ((1, 0), (-1, 0))[side])

        def relay_in(self, side):
            return self.copy(2 + side, 2, 0, side, (1, 0))

        def second(self, i, side):
            return self.copy(4 + 2 * i + side, STEPS_OFF[i], 0, None, ((0, 1), (0, -1))[side])

        def second_in(self, i, side):
            return self.copy(4 + 2 * i + side, STEPS_OFF[i], (-1, 1)[side], None, (0, 1))

        def pass_on(self, i, side):
            return self.copy(
                12 + 2 * i + side, STEPS_OFF[i], (-1, 1)[side], side, ((0, 1), (0, -1))[side]
            )

        def pass_on_in(self, i, side):
            return self.copy(12 + 2 * i + side, STEPS_OFF[i], 2, side, (0, 1))

        def twin(self, i, j):
            return self.copy(20 + 4 * i + j, STEPS_OFF[i], STEPS_OFF[j], None, None)

        def twin_in(self, i, j):
            return self.copy(20 + 4 * i + j, STEPS_OFF[i], STEPS_OFF[j], None, None, 1 - lane)

        def stage(self, number):
            if number == 0:
                for side in range(2):
                    self.first(side).start()
                    self.second(0, side).start()
                self.twin(0, 0).start()
            if number == 1:
                for side in range(2):
                    self.first_in(side).wait_recv()
                    self.relay(side).start()
                    i = 2 - side
                    self.second(i, 0).start()
                    self.second(i, 1).start()
                    self.twin(i, 0).start()
                for side in range(2):
                    self.second_in(0, side).wait_recv()
                    self.pass_on(0, side).start()
                    self.twin(0, 2 - side).start()
            if number == 2:
                for side in range(2):
                    self.relay_in(side).wait_recv()
                for side in range(2):
                    self.second(3, side).start()
                self.twin(3, 0).start()
                for side in range(2):
                    self.pass_on_in(0, side).wait_recv()
                self.twin(0, 3).start()
            if number == 3:
                for i in (1, 2):
                    for side in range(2):
                        self.second_in(i, side).wait_recv()
                        self.pass_on(i, side).start()
                        self.twin(i, 2 - side).start()
            if number == 4:
                for side in range(2):
                    self.second_in(3, side).wait_recv()
                    self.pass_on(3, side).start()
                    self.twin(3, 2 - side).start()
                for i in (1, 2):
                    for side in range(2):
                        self.pass_on_in(i, side).wait_recv()
                    self.twin(i, 3).start()
            if number == 5:
                for side in range(2):
                    self.pass_on_in(3, side).wait_recv()
                self.twin(3, 3).start()

        def sent(self):
            for side in range(2):
                self.first(side).wait_send()
                self.relay(side).wait_send()
                for i in range(4):
                    self.second(i, side).wait_send()
                    self.pass_on(i, side).wait_send()
            for i in range(4):
                for j in range(4):
                    self.twin(i, j).wait_send()

    rows_of_weight = weight_hbm.shape[0]
    key_stream = Stream(0, kv_ref.at[0], 0, tokens, True)
    value_stream = Stream(1, kv_ref.at[1], 0, tokens, False)
    weight_streams = (
        Stream(2, weight_ref, 0, rows_of_weight // 2, True),
        Stream(3, weight_ref, rows_of_weight // 2, rows_of_weight // 2, False),
    )

    def kv_stage(number):
        key_stream.stage(number)
        value_stream.stage(number)

    def weight_stage(number):
        for stream in weight_streams:
            stream.stage(number)

    heads = local // HD
    block = 2 * tokens
    factor = math.log2(math.e) / math.sqrt(HD)

    def attend(dx, dy, own):
        i, j = STEPS_OFF.index(dy), STEPS_OFF.index(dx)
        key_stream.twin_in(i, j).wait_recv()
        value_stream.twin_in(j, i).wait_recv()
        source = chip_at(dx, dy)

        def compute():
            keys = kv_ref[0, pl.ds(source * 2, 2)].reshape(block, HD)
            values = kv_ref[1, pl.ds(source * 2, 2)].reshape(block, HD)
            values = jnp.concatenate([values, jnp.ones((block, HD), BF16)], axis=1)
            for head in range(heads):
                query = query_ref[:, head * HD : (head + 1) * HD]
                scores = lax.dot_general(
                    query, keys, (((1,), (1,)), ((), ())), preferred_element_type=F32
                )
                if own:
                    shape = (tokens, block)
                    spot = lane * tokens + lax.broadcasted_iota(jnp.int32, shape, 0)
                    visible = lax.broadcasted_iota(jnp.int32, shape, 1) <= spot
                    scores = jnp.where(visible, scores, FAR_BELOW)
                highest = jnp.max(scores, axis=1, keepdims=True)
                if not own:
                    before = high_ref[head]
                    highest = jnp.maximum(highest, before)
                weights = jnp.exp2((scores - highest) * factor).astype(BF16)
                summed = dot(weights, values)
                if not own:
                    summed = summed + total_ref[head] * jnp.exp2((before - highest) * factor)
                total_ref[head] = summed
                high_ref[head] = highest

        if own:
            compute()
        else:
            pl.when(source < chip)(compute)

    in_all = lots // experts

    def make_tables():
        chosen_row = route_ref[...]
        square = (tokens, tokens)
        down_axis = lax.broadcasted_iota(jnp.int32, square, 0)
        over_axis = lax.broadcasted_iota(jnp.int32, square, 1)
        chosen_col = jnp.sum(
            jnp.where(down_axis == over_axis, chosen_row.astype(F32), 0.0), axis=1, keepdims=True
        ).astype(jnp.int32)
        same = chosen_col == chosen_row
        rank_col = jnp.sum(
            jnp.where(same & (over_axis < down_axis), 1.0, 0.0), axis=1, keepdims=True
        ).astype(jnp.int32)
        rank_row = jnp.sum(
            jnp.where(same & (down_axis < over_axis), 1.0, 0.0), axis=0, keepdims=True
        ).astype(jnp.int32)
        slot_col = chosen_col * most + rank_col
        slot_row = chosen_row * most + rank_row
        pick_ref[...] = jnp.where(
            lax.broadcasted_iota(jnp.int32, (lots, tokens), 0) == slot_row, 1.0, 0.0
        ).astype(BF16)
        spread_ref[...] = jnp.where(
            lax.broadcasted_iota(jnp.int32, (tokens, lots), 1) == slot_col, 1.0, 0.0
        ).astype(BF16)
        lot = lax.broadcasted_iota(jnp.int32, (1, lots), 1)
        to_row = lax.broadcasted_iota(jnp.int32, (lots, lots), 0)
        place = (lot % each) // most * in_all + lot // each * most + lot % most
        by_expert_ref[...] = jnp.where(to_row == place, 1.0, 0.0).astype(BF16)
        place = (lot % in_all) // most * each + lot // in_all * most + lot % most
        by_device_ref[...] = jnp.where(to_row == place, 1.0, 0.0).astype(BF16)

    for load in own_loads:
        load.wait()
    kv_stage(0)
    make_tables()
    attend(0, 0, True)
    kv_stage(1)
    weight_stage(0)
    for dx, dy in ((0, -1), (-1, 0)):
        attend(dx, dy, False)
    kv_stage(2)
    for dx, dy in ((0, 1), (1, 0)):
        attend(dx, dy, False)
    weight_stage(1)
    for dx, dy in ((0, 2), (2, 0)):
        attend(dx, dy, False)
    kv_stage(3)
    weight_stage(2)
    for dx, dy in ((-1, -1), (-1, 1), (1, -1), (1, 1)):
        attend(dx, dy, False)
    kv_stage(4)
    weight_stage(3)
    for dx, dy in ((2, -1), (2, 1), (-1, 2), (1, 2)):
        attend(dx, dy, False)
    kv_stage(5)
    weight_stage(4)
    attend(2, 2, False)
    weight_stage(5)
    for head in range(heads):
        summed = total_ref[head]
        attn_ref[:, head * HD : (head + 1) * HD] = (summed[:, :HD] / summed[:, HD:]).astype(BF16)
    for stream in weight_streams:
        for i in range(4):
            for j in range(4):
                stream.twin_in(i, j).wait_recv()

    rows = tokens // CHUNKS
    pairs = n_ctx // n_exp

    def proj_copy(way, step, part):
        spot = pl.ds(part * rows, rows)
        return along(
            proj_out.at[way, step, spot],
            proj_in.at[way, step, spot],
            proj_send.at[way, step, part],
            proj_recv.at[way, step, part],
            way,
        )

    def make_term(target):
        columns = jnp.concatenate(
            [weight_ref[target * pairs + i] for i in range(pairs)], axis=1
        )
        term_ref[target] = dot(attn_ref[...], columns).astype(BF16)

    def proj_term(target, part):
        return term_ref[target, pl.ds(part * rows, rows)].astype(F32)

    def far(way, part, parts):
        return (part < parts // 2) == (way == 0)

    def proj_step(step, started):
        for part in range(CHUNKS):
            for way in range(2):
                fresh = started == 0 or (started == 1 and not far(way, part, CHUNKS))
                if started == 0 and not far(way, part, CHUNKS):
                    continue
                spot = pl.ds(part * rows, rows)
                term = proj_term(target_of(way, step), part)
                if not fresh:
                    proj_copy(way, step - 1, part).wait_recv()
                    term = term + proj_in[way, step - 1, spot].astype(F32)
                proj_out[way, step, spot] = term.astype(BF16)
                proj_copy(way, step, part).start()

    make_term(target_of(0, 0))
    proj_step(0, 0)
    make_term(target_of(0, 1))
    make_term(target_of(1, 1))
    proj_step(1, 1)

    def proj_loop(step, carry):
        make_term(target_of(0, step))
        make_term(target_of(1, step))
        proj_step(step, 2)
        for i, stream in enumerate((key_stream, value_stream, *weight_streams)):
            pl.when(step == 2 + i)(stream.sent)
        return carry

    lax.fori_loop(2, half, proj_loop, 0)
    make_term(z)
    for part in range(CHUNKS):
        spot = pl.ds(part * rows, rows)
        term = proj_term(z, part)
        for way in range(2):
            proj_copy(way, half - 1, part).wait_recv()
            term = term + proj_in[way, half - 1, spot].astype(F32)
        proj_ref[spot, :] = term.astype(BF16)

    packed_ref[...] = dot(pick_ref[...], proj_ref[...]).astype(BF16)

    def there_copy(r):
        peer = lax.rem(me + r, n_ctx)
        return pltpu.make_async_remote_copy(
            src_ref=packed_ref.at[pl.ds(pl.multiple_of(peer * each, each), each)],
            dst_ref=arrived_ref.at[pl.ds(pl.multiple_of(me * each, each), each)],
            send_sem=there_send.at[r],
            recv_sem=there_recv.at[r],
            device_id=(peer, z),
            device_id_type=pl.DeviceIdType.MESH,
        )

    def start_there(r, carry):
        there_copy(r).start()
        return carry

    def wait_there(r, carry):
        there_copy(r).wait_recv()
        return carry

    lax.fori_loop(1, n_ctx, start_there, 0)
    own = pl.ds(pl.multiple_of(me * each, each), each)
    arrived_ref[own, :] = packed_ref[own, :]
    for load in loads:
        load.wait()
    lax.fori_loop(1, n_ctx, wait_there, 0)

    share = lots // n_exp
    tokens_in = dot(by_expert_ref[...], arrived_ref[...])
    scaled_ref[...] = (tokens_in * gain_ref[...]).astype(BF16)
    first_expert = lax.rem(z + half, n_exp) * share // in_all

    def make_part(i):
        e = lax.rem(first_expert + i, experts)
        spot = pl.ds(pl.multiple_of(e * in_all, in_all), in_all)
        part_ref[spot, :] = dot(scaled_ref[spot, :], gu_ref[e]).astype(BF16)

    piece = share // PARTS

    hops = half // 2

    def place_at(way, offset):
        return lax.rem(z + (offset if way == 0 else n_exp - offset), n_exp)

    def move(source, target, send_sem, recv_sem, way, distance):
        return pltpu.make_async_remote_copy(
            src_ref=source,
            dst_ref=target,
            send_sem=send_sem,
            recv_sem=recv_sem,
            device_id=(me, place_at(way, distance)),
            device_id_type=pl.DeviceIdType.MESH,
        )

    def part_rows(target, part):
        return pl.ds(pl.multiple_of(target * share + part * piece, piece), piece)

    def gu_chain(way, step, part):
        spot = pl.ds(part * piece, piece)
        if step == 0:
            source = part_ref.at[part_rows(place_at(way, half), part)]
        else:
            source = gu_out.at[way, step, spot]
        return move(
            source,
            gu_in.at[way, step, spot],
            gu_send.at[way, step, part],
            gu_recv.at[way, step, part],
            way,
            2,
        )

    def gu_leaf(way, step, part):
        spot = pl.ds(part * piece, piece)
        return move(
            part_ref.at[part_rows(place_at(way, half - 1 - 2 * step), part)],
            gu_in.at[way, hops + step, spot],
            gu_send.at[way, hops + step, part],
            gu_recv.at[way, hops + step, part],
            way,
            1,
        )

    def gu_term(target, part):
        return part_ref[part_rows(target, part), :].astype(F32)

    def gu_arrived(term, way, step, part):
        spot = pl.ds(part * piece, piece)
        gu_leaf(way, step, part).wait_recv()
        term = term + gu_in[way, hops + step, spot].astype(F32)
        if step > 0 or far(way, part, PARTS):
            gu_chain(way, step, part).wait_recv()
            term = term + gu_in[way, step, spot].astype(F32)
        return term

    both = [(way, part) for part in range(PARTS) for way in range(2)]

    def gu_leaves(step):
        for way, part in both:
            gu_leaf(way, step, part).start()

    def gu_step(step):
        gu_leaves(step)
        for way, part in both:
            term = gu_arrived(gu_term(place_at(way, half - 2 * step), part), way, step - 1, part)
            gu_out[way, step, pl.ds(part * piece, piece)] = term.astype(BF16)
            gu_chain(way, step, part).start()

    make_part(0)
    for way, part in both:
        if far(way, part, PARTS):
            gu_chain(way, 0, part).start()
    for i in range(1, experts):
        make_part(i)
    gu_leaves(0)

    squares = lax.dot_general(
        jnp.ones((8, local), BF16),
        (tokens_in * tokens_in).astype(BF16),
        (((1,), (1,)), ((), ())),
        preferred_element_type=F32,
    )
    for to in range(n_exp):
        squares_out[to, :, pl.ds(0, share)] = squares[0:1, to * share : (to + 1) * share]

    def sq_copy(r):
        peer = lax.rem(z + r, n_exp)
        return pltpu.make_async_remote_copy(
            src_ref=squares_out.at[peer],
            dst_ref=squares_in.at[r],
            send_sem=sq_send.at[r],
            recv_sem=sq_recv.at[r],
            device_id=(me, peer),
            device_id_type=pl.DeviceIdType.MESH,
        )

    def start_sq(r, carry):
        sq_copy(r).start()
        return carry

    lax.fori_loop(1, n_exp, start_sq, 0)

    def sent_proj(step, carry):
        for way in range(2):
            for part in range(CHUNKS):
                proj_copy(way, step, part).wait_send()
        return carry

    for step in range(1, hops):
        gu_step(step)
        if step == 1:
            lax.fori_loop(1, half // 2, sent_proj, 0)
        if step == 2:
            lax.fori_loop(half // 2, half, sent_proj, 0)

    def wait_sq(r, carry):
        sq_copy(r).wait_recv()
        return carry

    lax.fori_loop(1, n_exp, wait_sq, 0)
    squares_in[0] = squares_out[z]
    row = jnp.sum(squares_in[...], axis=0)
    at_lane = lax.broadcasted_iota(jnp.int32, (share, HD), 1)
    at_row = lax.broadcasted_iota(jnp.int32, (share, HD), 0)
    column = jnp.sum(jnp.where(at_lane == at_row, row, 0.0), axis=1, keepdims=True)
    scale = lax.rsqrt(column / (local * n_exp) + EPS)
    for part in range(PARTS):
        term = gu_term(z, part)
        for way in range(2):
            term = gu_arrived(term, way, hops - 1, part)
        term = term * scale[part * piece : (part + 1) * piece]
        gate, upper = term[:, :units], term[:, units:]
        hidden = gate / (1.0 + jnp.exp(-gate)) * upper
        hidden_ref[pl.ds(pl.multiple_of(z * share + part * piece, piece), piece), :] = hidden.astype(BF16)

    def hid_copy(way, step, part, distance, ahead=0):
        block = place_at(1 - way, 2 * step + ahead)
        spot = hidden_ref.at[part_rows(block, part)]
        lane_of = (2 - distance) * hops + step
        return move(
            spot, spot, hid_send.at[way, lane_of, part], hid_recv.at[way, lane_of, part], way, distance
        )

    def hid_far(way, step, part):
        return step < hops - 1 or far(way, part, PARTS)

    for step in range(hops):
        for way, part in both:
            if step > 0:
                hid_copy(way, step - 1, part, 2, 2).wait_recv()
            if hid_far(way, step, part):
                hid_copy(way, step, part, 2).start()
            hid_copy(way, step, part, 1).start()
        if step == 0:
            for way, part in both:
                if far(way, part, PARTS):
                    gu_chain(way, 0, part).wait_send()
                gu_leaf(way, 0, part).wait_send()
        else:
            for way, part in both:
                gu_chain(way, step, part).wait_send()
                gu_leaf(way, step, part).wait_send()
    for step in range(hops):
        for way, part in both:
            hid_copy(way, step, part, 1, 1).wait_recv()
    for way, part in both:
        if hid_far(way, hops - 1, part):
            hid_copy(way, hops - 1, part, 2, 2).wait_recv()

    made = jnp.concatenate(
        [dot(hidden_ref[pl.ds(e * in_all, in_all), :], down_ref[e]) for e in range(experts)], axis=0
    ).astype(BF16)
    made_ref[...] = dot(by_device_ref[...], made).astype(BF16)

    def home_copy(r):
        peer = lax.rem(me + r, n_ctx)
        return pltpu.make_async_remote_copy(
            src_ref=made_ref.at[pl.ds(pl.multiple_of(peer * each, each), each)],
            dst_ref=back_ref.at[pl.ds(pl.multiple_of(me * each, each), each)],
            send_sem=home_send.at[r],
            recv_sem=home_recv.at[r],
            device_id=(peer, z),
            device_id_type=pl.DeviceIdType.MESH,
        )

    def start_home(r, carry):
        home_copy(r).start()
        return carry

    def wait_home(r, carry):
        home_copy(r).wait_recv()
        return carry

    lax.fori_loop(1, n_ctx, start_home, 0)
    back_ref[own, :] = made_ref[own, :]

    def sent_ctx(r, carry):
        there_copy(r).wait_send()
        return carry

    def sent_home(r, carry):
        home_copy(r).wait_send()
        return carry

    def sent_exp(r, carry):
        sq_copy(r).wait_send()
        return carry

    for way in range(2):
        for part in range(CHUNKS):
            if far(way, part, CHUNKS):
                proj_copy(way, 0, part).wait_send()
    for step in range(hops):
        for way, part in both:
            if hid_far(way, step, part):
                hid_copy(way, step, part, 2).wait_send()
            hid_copy(way, step, part, 1).wait_send()
    lax.fori_loop(1, n_exp, sent_exp, 0)
    lax.fori_loop(1, n_ctx, sent_ctx, 0)
    lax.fori_loop(1, n_ctx, wait_home, 0)
    out_ref[...] = dot(spread_ref[...], back_ref[...]).astype(BF16)
    lax.fori_loop(1, n_ctx, sent_home, 0)


def layer(n_ctx, n_exp, query, route, gain, keys, values, weight, gate, up, down):
    tokens, local = query.shape
    experts, _, units = gate.shape
    most = 2 * tokens // (experts * n_ctx)
    lots = n_ctx * experts * most
    share = lots // n_exp
    half = n_exp // 2
    heads = local // HD
    dma = pltpu.SemaphoreType.DMA
    vmem = pl.BlockSpec(memory_space=pltpu.VMEM)
    anywhere = pl.BlockSpec(memory_space=pl.ANY)
    return pl.pallas_call(
        functools.partial(layer_kernel, n_ctx, n_exp),
        out_shape=jax.ShapeDtypeStruct((tokens, local), BF16),
        in_specs=[vmem] * 3 + [anywhere] * 6,
        out_specs=vmem,
        scratch_shapes=[
            pltpu.VMEM((2, n_ctx, tokens, HD), BF16),
            pltpu.VMEM((n_ctx, *weight.shape), BF16),
            pltpu.VMEM((heads, tokens, 1), F32),
            pltpu.VMEM((heads, tokens, 2 * HD), F32),
            pltpu.VMEM((tokens, local), BF16),
            pltpu.VMEM((experts, local, 2 * units), BF16),
            pltpu.VMEM((experts, units, local), BF16),
            pltpu.VMEM((2, half, tokens, local), BF16),
            pltpu.VMEM((2, half, tokens, local), BF16),
            pltpu.VMEM((tokens, local), BF16),
            pltpu.VMEM((n_exp, tokens, local), BF16),
            pltpu.VMEM((lots, tokens), BF16),
            pltpu.VMEM((tokens, lots), BF16),
            pltpu.VMEM((lots, lots), BF16),
            pltpu.VMEM((lots, lots), BF16),
            pltpu.VMEM((lots, local), BF16),
            pltpu.VMEM((lots, local), BF16),
            pltpu.VMEM((lots, local), BF16),
            pltpu.VMEM((lots, 2 * units), BF16),
            pltpu.VMEM((2, half, share, 2 * units), BF16),
            pltpu.VMEM((2, half, share, 2 * units), BF16),
            pltpu.VMEM((n_exp, 1, HD), F32),
            pltpu.VMEM((n_exp, 1, HD), F32),
            pltpu.VMEM((lots, units), BF16),
            pltpu.VMEM((lots, local), BF16),
            pltpu.VMEM((lots, local), BF16),
            dma((6,)),
            dma((4, MESSAGES)),
            dma((4, MESSAGES)),
            dma((2, half, CHUNKS)),
            dma((2, half, CHUNKS)),
            dma((n_ctx,)),
            dma((n_ctx,)),
            dma((2, half, PARTS)),
            dma((2, half, PARTS)),
            dma((n_exp,)),
            dma((n_exp,)),
            dma((2, half, PARTS)),
            dma((2, half, PARTS)),
            dma((n_ctx,)),
            dma((n_ctx,)),
        ],
        compiler_params=pltpu.CompilerParams(
            collective_id=0, has_side_effects=True, vmem_limit_bytes=VMEM_LIMIT
        ),
        name="layer",
    )(query, route, gain, keys, values, weight, gate, up, down)


def body(
    queries,
    keys,
    values,
    routes,
    route_score,
    output_weight,
    norm_gain,
    gate_weight,
    up_weight,
    down_weight,
):
    tokens, local = queries.shape[1:]
    returned = layer(
        lax.axis_size("ctx"),
        lax.axis_size("exp"),
        queries[0],
        routes[0].reshape(1, tokens),
        norm_gain.reshape(1, local),
        keys[0],
        values[0],
        output_weight,
        gate_weight,
        up_weight,
        down_weight,
    )
    scored = route_score[0][:, None] * returned.astype(F32)
    return scored.astype(BF16)[None]


def solution(mesh):
    placed = (
        P(None, "ctx", "exp"),
        P(None, "ctx", None),
        P(None, "ctx", None),
        P(None, "ctx", None),
        P(None, "ctx"),
        P("exp", "ctx"),
        P("exp"),
        P("ctx", "exp", None),
        P("ctx", "exp", None),
        P("ctx", None, "exp"),
    )
    return jax.shard_map(
        body, mesh=mesh, in_specs=placed, out_specs=P(None, "ctx", "exp"), check_vma=False
    )
```

```python
import functools
import math

import jax
import jax.numpy as jnp
from jax import lax
from jax.experimental import pallas as pl
from jax.experimental.pallas import tpu as pltpu
from jax.sharding import PartitionSpec as P

HD = 128
EPS = 1e-05
FAR_BELOW = -1e30
F32 = jnp.float32
BF16 = jnp.bfloat16
VMEM_LIMIT = 56 * 1024 * 1024


def dot(a, b):
    return jnp.dot(a, b, preferred_element_type=F32)


NX = 4
NY = 4
STEPS_OFF = (0, 1, -1, 2)
MESSAGES = 36
CHUNKS = 4
PARTS = 2


def layer_kernel(
    n_ctx,
    n_exp,
    query_ref,
    route_ref,
    gain_ref,
    keys_hbm,
    values_hbm,
    weight_hbm,
    gate_hbm,
    up_hbm,
    down_hbm,
    out_ref,
    kv_ref,
    weight_ref,
    high_ref,
    total_ref,
    attn_ref,
    gu_ref,
    down_ref,
    proj_out,
    proj_in,
    proj_ref,
    term_ref,
    pick_ref,
    spread_ref,
    by_expert_ref,
    by_device_ref,
    packed_ref,
    arrived_ref,
    scaled_ref,
    part_ref,
    gu_out,
    gu_in,
    squares_out,
    squares_in,
    hidden_ref,
    made_ref,
    back_ref,
    load_sem,
    flow_send,
    flow_recv,
    proj_send,
    proj_recv,
    there_send,
    there_recv,
    gu_send,
    gu_recv,
    sq_send,
    sq_recv,
    hid_send,
    hid_recv,
    home_send,
    home_recv,
):
    me = lax.axis_index("ctx")
    z = lax.axis_index("exp")
    half = n_exp // 2
    tokens, local = query_ref.shape
    experts, _, twice = gu_ref.shape
    units = twice // 2
    lots = packed_ref.shape[0]
    each = lots // n_ctx
    most = each // experts

    kv_heads = keys_hbm.shape[1] // HD
    columns = pl.ds(pl.multiple_of(z * kv_heads // n_exp * HD, HD), HD)
    own_loads = [
        pltpu.make_async_copy(keys_hbm.at[:, columns], kv_ref.at[me, 0], load_sem.at[3]),
        pltpu.make_async_copy(values_hbm.at[:, columns], kv_ref.at[me, 1], load_sem.at[4]),
        pltpu.make_async_copy(weight_hbm, weight_ref.at[me], load_sem.at[5]),
    ]
    for load in own_loads:
        load.start()
    loads = [
        pltpu.make_async_copy(gate_hbm, gu_ref.at[:, :, pl.ds(0, units)], load_sem.at[0]),
        pltpu.make_async_copy(up_hbm, gu_ref.at[:, :, pl.ds(units, units)], load_sem.at[1]),
        pltpu.make_async_copy(down_hbm, down_ref, load_sem.at[2]),
    ]
    for load in loads:
        load.start()

    barrier = pltpu.get_barrier_semaphore()

    def greet_ctx(r, carry):
        pl.semaphore_signal(
            barrier, inc=1, device_id=(lax.rem(me + r, n_ctx), z), device_id_type=pl.DeviceIdType.MESH
        )
        return carry

    def greet_exp(r, carry):
        pl.semaphore_signal(
            barrier, inc=1, device_id=(me, lax.rem(z + r, n_exp)), device_id_type=pl.DeviceIdType.MESH
        )
        return carry

    lax.fori_loop(1, n_ctx, greet_ctx, 0)
    lax.fori_loop(1, n_exp, greet_exp, 0)
    pl.semaphore_wait(barrier, n_ctx - 1 + n_exp - 1)

    lane = me % 2
    chip = me // 2
    at_x, at_y = chip // NY, chip % NY

    def chip_at(dx, dy):
        return lax.rem(at_x + dx + NX, NX) * NY + lax.rem(at_y + dy + NY, NY)

    class Stream:
        def __init__(self, number, ref, size):
            self.number, self.ref, self.size = number, ref, size

        def chip(self, da, db):
            return chip_at(lane * da + (1 - lane) * db, lane * db + (1 - lane) * da)

        def copy(self, message, da, db, part, to, twin=False):
            block = self.chip(da, db) * 2 + (1 - lane if twin else lane)
            half_size = self.size // 2
            here = self.ref.at[block]
            if part is not None:
                here = self.ref.at[block, pl.ds(part * half_size, half_size)]
            target = chip * 2 + 1 - lane if to is None else self.chip(*to) * 2 + lane
            return pltpu.make_async_remote_copy(
                src_ref=here,
                dst_ref=here,
                send_sem=flow_send.at[self.number, message],
                recv_sem=flow_recv.at[self.number, message],
                device_id=(target, z),
                device_id_type=pl.DeviceIdType.MESH,
            )

        def first(self, side):
            return self.copy(side, 0, 0, None, ((1, 0), (-1, 0))[side])

        def first_in(self, side):
            return self.copy(side, (-1, 1)[side], 0, None, (1, 0))

        def relay(self, side):
            return self.copy(2 + side, (-1, 1)[side], 0, side, ((1, 0), (-1, 0))[side])

        def relay_in(self, side):
            return self.copy(2 + side, 2, 0, side, (1, 0))

        def second(self, i, side):
            return self.copy(4 + 2 * i + side, STEPS_OFF[i], 0, None, ((0, 1), (0, -1))[side])

        def second_in(self, i, side):
            return self.copy(4 + 2 * i + side, STEPS_OFF[i], (-1, 1)[side], None, (0, 1))

        def pass_on(self, i, side):
            return self.copy(
                12 + 2 * i + side, STEPS_OFF[i], (-1, 1)[side], side, ((0, 1), (0, -1))[side]
            )

        def pass_on_in(self, i, side):
            return self.copy(12 + 2 * i + side, STEPS_OFF[i], 2, side, (0, 1))

        def twin(self, i, j):
            return self.copy(20 + 4 * i + j, STEPS_OFF[i], STEPS_OFF[j], None, None)

        def twin_in(self, i, j):
            return self.copy(20 + 4 * j + i, STEPS_OFF[i], STEPS_OFF[j], None, None, True)

        def stage(self, number):
            if number == 0:
                for side in range(2):
                    self.first(side).start()
                self.twin(0, 0).start()
                for side in range(2):
                    self.second(0, side).start()
            if number == 1:
                for side in range(2):
                    self.first_in(side).wait_recv()
                    self.relay(side).start()
                    self.twin(2 - side, 0).start()
                for side in range(2):
                    self.second_in(0, side).wait_recv()
                    self.pass_on(0, side).start()
                    self.twin(0, 2 - side).start()
                for i in (2, 1):
                    for side in range(2):
                        self.second(i, side).start()
            if number == 2:
                for side in range(2):
                    self.relay_in(side).wait_recv()
                for side in range(2):
                    self.second(3, side).start()
                self.twin(3, 0).start()
                for side in range(2):
                    self.pass_on_in(0, side).wait_recv()
                self.twin(0, 3).start()
            if number == 3:
                for i in (1, 2):
                    for side in range(2):
                        self.second_in(i, side).wait_recv()
                        self.pass_on(i, side).start()
                        self.twin(i, 2 - side).start()
            if number == 4:
                for side in range(2):
                    self.second_in(3, side).wait_recv()
                    self.pass_on(3, side).start()
                    self.twin(3, 2 - side).start()
                for i in (1, 2):
                    for side in range(2):
                        self.pass_on_in(i, side).wait_recv()
                    self.twin(i, 3).start()
            if number == 5:
                for side in range(2):
                    self.pass_on_in(3, side).wait_recv()
                self.twin(3, 3).start()

        def sent(self):
            for side in range(2):
                self.first(side).wait_send()
                self.relay(side).wait_send()
                for i in range(4):
                    self.second(i, side).wait_send()
                    self.pass_on(i, side).wait_send()
            for i in range(4):
                for j in range(4):
                    self.twin(i, j).wait_send()

    kv_stream = Stream(0, kv_ref, 2)
    weight_stream = Stream(1, weight_ref, weight_hbm.shape[0])

    def stage(number):
        kv_stream.stage(number)
        weight_stream.stage(number)

    heads = local // HD
    block = 2 * tokens
    factor = math.log2(math.e) / math.sqrt(HD)

    def attend(i, j):
        own = i == 0 and j == 0
        kv_stream.twin_in(i, j).wait_recv()
        source = kv_stream.chip(STEPS_OFF[i], STEPS_OFF[j])

        def compute():
            keys = kv_ref[pl.ds(source * 2, 2), 0].reshape(block, HD)
            values = kv_ref[pl.ds(source * 2, 2), 1].reshape(block, HD)
            values = jnp.concatenate([values, jnp.ones((block, HD), BF16)], axis=1)
            for head in range(heads):
                query = query_ref[:, head * HD : (head + 1) * HD]
                scores = lax.dot_general(
                    query, keys, (((1,), (1,)), ((), ())), preferred_element_type=F32
                )
                if own:
                    shape = (tokens, block)
                    spot = lane * tokens + lax.broadcasted_iota(jnp.int32, shape, 0)
                    visible = lax.broadcasted_iota(jnp.int32, shape, 1) <= spot
                    scores = jnp.where(visible, scores, FAR_BELOW)
                highest = jnp.max(scores, axis=1, keepdims=True)
                if not own:
                    before = high_ref[head]
                    highest = jnp.maximum(highest, before)
                weights = jnp.exp2((scores - highest) * factor).astype(BF16)
                summed = dot(weights, values)
                if not own:
                    summed = summed + total_ref[head] * jnp.exp2((before - highest) * factor)
                total_ref[head] = summed
                high_ref[head] = highest

        if own:
            compute()
        else:
            pl.when(source < chip)(compute)

    in_all = lots // experts

    def make_tables():
        chosen_row = route_ref[...]
        square = (tokens, tokens)
        down_axis = lax.broadcasted_iota(jnp.int32, square, 0)
        over_axis = lax.broadcasted_iota(jnp.int32, square, 1)
        chosen_col = jnp.sum(
            jnp.where(down_axis == over_axis, chosen_row.astype(F32), 0.0), axis=1, keepdims=True
        ).astype(jnp.int32)
        same = chosen_col == chosen_row
        rank_col = jnp.sum(
            jnp.where(same & (over_axis < down_axis), 1.0, 0.0), axis=1, keepdims=True
        ).astype(jnp.int32)
        rank_row = jnp.sum(
            jnp.where(same & (down_axis < over_axis), 1.0, 0.0), axis=0, keepdims=True
        ).astype(jnp.int32)
        slot_col = chosen_col * most + rank_col
        slot_row = chosen_row * most + rank_row
        pick_ref[...] = jnp.where(
            lax.broadcasted_iota(jnp.int32, (lots, tokens), 0) == slot_row, 1.0, 0.0
        ).astype(BF16)
        spread_ref[...] = jnp.where(
            lax.broadcasted_iota(jnp.int32, (tokens, lots), 1) == slot_col, 1.0, 0.0
        ).astype(BF16)
        lot = lax.broadcasted_iota(jnp.int32, (1, lots), 1)
        to_row = lax.broadcasted_iota(jnp.int32, (lots, lots), 0)
        place = (lot % each) // most * in_all + lot // each * most + lot % most
        by_expert_ref[...] = jnp.where(to_row == place, 1.0, 0.0).astype(BF16)
        place = (lot % in_all) // most * each + lot // in_all * most + lot % most
        by_device_ref[...] = jnp.where(to_row == place, 1.0, 0.0).astype(BF16)

    for load in own_loads:
        load.wait()
    stage(0)
    make_tables()
    attend(0, 0)
    stage(1)
    stage(2)
    for i, j in ((1, 0), (2, 0), (0, 1), (0, 2)):
        attend(i, j)
    stage(3)
    for i, j in ((3, 0), (0, 3)):
        attend(i, j)
    stage(4)
    for i, j in ((1, 1), (1, 2), (2, 1), (2, 2)):
        attend(i, j)
    stage(5)
    for i, j in ((3, 1), (3, 2), (1, 3), (2, 3), (3, 3)):
        attend(i, j)
    for head in range(heads):
        summed = total_ref[head]
        attn_ref[:, head * HD : (head + 1) * HD] = (summed[:, :HD] / summed[:, HD:]).astype(BF16)
    for i in range(4):
        for j in range(4):
            weight_stream.twin_in(i, j).wait_recv()

    rows = tokens // CHUNKS
    pairs = n_ctx // n_exp

    def place_at(way, offset):
        return lax.rem(z + (offset if way == 0 else n_exp - offset), n_exp)

    def move(source, target, send_sem, recv_sem, way, distance):
        return pltpu.make_async_remote_copy(
            src_ref=source,
            dst_ref=target,
            send_sem=send_sem,
            recv_sem=recv_sem,
            device_id=(me, place_at(way, distance)),
            device_id_type=pl.DeviceIdType.MESH,
        )

    def proj_far(way, part):
        spot = pl.ds(part * rows, rows)
        return move(
            term_ref.at[place_at(way, half), spot],
            proj_in.at[way, 0, spot],
            proj_send.at[way, 0, part],
            proj_recv.at[way, 0, part],
            way,
            2,
        )

    def proj_near(way, part):
        spot = pl.ds(part * rows, rows)
        return move(
            term_ref.at[place_at(way, half - 1), spot],
            proj_in.at[way, half - 1, spot],
            proj_send.at[way, half - 1, part],
            proj_recv.at[way, half - 1, part],
            way,
            1,
        )

    def proj_copy(way, step, part):
        spot = pl.ds(part * rows, rows)
        return move(
            proj_out.at[way, step, spot],
            proj_in.at[way, step, spot],
            proj_send.at[way, step, part],
            proj_recv.at[way, step, part],
            way,
            1,
        )

    def make_term(target):
        columns = jnp.concatenate(
            [weight_ref[target * pairs + i] for i in range(pairs)], axis=1
        )
        term_ref[target] = dot(attn_ref[...], columns).astype(BF16)

    def proj_term(target, part):
        return term_ref[target, pl.ds(part * rows, rows)].astype(F32)

    def far(way, part, parts):
        return (part < parts // 2) == (way == 0)

    def proj_step(step, first):
        for part in range(CHUNKS):
            for way in range(2):
                spot = pl.ds(part * rows, rows)
                term = proj_term(place_at(way, half - 1 - step), part)
                if first:
                    proj_near(way, part).wait_recv()
                    term = term + proj_in[way, half - 1, spot].astype(F32)
                    if far(way, part, CHUNKS):
                        proj_far(way, part).wait_recv()
                        term = term + proj_in[way, 0, spot].astype(F32)
                else:
                    proj_copy(way, step - 1, part).wait_recv()
                    term = term + proj_in[way, step - 1, spot].astype(F32)
                proj_out[way, step, spot] = term.astype(BF16)
                proj_copy(way, step, part).start()

    make_term(place_at(0, half))
    for part in range(CHUNKS):
        for way in range(2):
            if far(way, part, CHUNKS):
                proj_far(way, part).start()
    for way in range(2):
        make_term(place_at(way, half - 1))
        for part in range(CHUNKS):
            proj_near(way, part).start()
    for way in range(2):
        make_term(place_at(way, half - 2))
    proj_step(1, True)

    def proj_loop(step, carry):
        for way in range(2):
            make_term(place_at(way, half - 1 - step))
        proj_step(step, False)
        for i, stream in enumerate((kv_stream, weight_stream)):
            pl.when(step == 2 + i)(stream.sent)
        return carry

    lax.fori_loop(2, half - 1, proj_loop, 0)
    make_term(z)
    for part in range(CHUNKS):
        spot = pl.ds(part * rows, rows)
        term = proj_term(z, part)
        for way in range(2):
            proj_copy(way, half - 2, part).wait_recv()
            term = term + proj_in[way, half - 2, spot].astype(F32)
        proj_ref[spot, :] = term.astype(BF16)

    packed_ref[...] = dot(pick_ref[...], proj_ref[...]).astype(BF16)

    def there_copy(r):
        peer = lax.rem(me + r, n_ctx)
        return pltpu.make_async_remote_copy(
            src_ref=packed_ref.at[pl.ds(pl.multiple_of(peer * each, each), each)],
            dst_ref=arrived_ref.at[pl.ds(pl.multiple_of(me * each, each), each)],
            send_sem=there_send.at[r],
            recv_sem=there_recv.at[r],
            device_id=(peer, z),
            device_id_type=pl.DeviceIdType.MESH,
        )

    def start_there(r, carry):
        there_copy(r).start()
        return carry

    def wait_there(r, carry):
        there_copy(r).wait_recv()
        return carry

    lax.fori_loop(1, n_ctx, start_there, 0)
    own = pl.ds(pl.multiple_of(me * each, each), each)
    arrived_ref[own, :] = packed_ref[own, :]
    for load in loads:
        load.wait()
    lax.fori_loop(1, n_ctx, wait_there, 0)

    share = lots // n_exp
    tokens_in = dot(by_expert_ref[...], arrived_ref[...])
    scaled_ref[...] = (tokens_in * gain_ref[...]).astype(BF16)
    first_expert = lax.rem(z + half, n_exp) * share // in_all

    def make_part(i):
        e = lax.rem(first_expert + i, experts)
        spot = pl.ds(pl.multiple_of(e * in_all, in_all), in_all)
        part_ref[spot, :] = dot(scaled_ref[spot, :], gu_ref[e]).astype(BF16)

    piece = share // PARTS

    hops = half // 2

    def part_rows(target, part):
        return pl.ds(pl.multiple_of(target * share + part * piece, piece), piece)

    def gu_chain(way, step, part):
        spot = pl.ds(part * piece, piece)
        if step == 0:
            source = part_ref.at[part_rows(place_at(way, half), part)]
        else:
            source = gu_out.at[way, step, spot]
        return move(
            source,
            gu_in.at[way, step, spot],
            gu_send.at[way, step, part],
            gu_recv.at[way, step, part],
            way,
            2,
        )

    def gu_leaf(way, step, part):
        spot = pl.ds(part * piece, piece)
        return move(
            part_ref.at[part_rows(place_at(way, half - 1 - 2 * step), part)],
            gu_in.at[way, hops + step, spot],
            gu_send.at[way, hops + step, part],
            gu_recv.at[way, hops + step, part],
            way,
            1,
        )

    def gu_term(target, part):
        return part_ref[part_rows(target, part), :].astype(F32)

    def gu_arrived(term, way, step, part):
        spot = pl.ds(part * piece, piece)
        gu_leaf(way, step, part).wait_recv()
        term = term + gu_in[way, hops + step, spot].astype(F32)
        if step > 0 or far(way, part, PARTS):
            gu_chain(way, step, part).wait_recv()
            term = term + gu_in[way, step, spot].astype(F32)
        return term

    both = [(way, part) for part in range(PARTS) for way in range(2)]

    def gu_leaves(step):
        for way, part in both:
            gu_leaf(way, step, part).start()

    def gu_step(step):
        gu_leaves(step)
        for way, part in both:
            term = gu_arrived(gu_term(place_at(way, half - 2 * step), part), way, step - 1, part)
            gu_out[way, step, pl.ds(part * piece, piece)] = term.astype(BF16)
            gu_chain(way, step, part).start()

    make_part(0)
    for way, part in both:
        if far(way, part, PARTS):
            gu_chain(way, 0, part).start()
    for i in range(1, experts):
        make_part(i)
    gu_leaves(0)

    squares = lax.dot_general(
        jnp.ones((8, local), BF16),
        (tokens_in * tokens_in).astype(BF16),
        (((1,), (1,)), ((), ())),
        preferred_element_type=F32,
    )
    for to in range(n_exp):
        squares_out[to, :, pl.ds(0, share)] = squares[0:1, to * share : (to + 1) * share]

    def sq_copy(r):
        peer = lax.rem(z + r, n_exp)
        return pltpu.make_async_remote_copy(
            src_ref=squares_out.at[peer],
            dst_ref=squares_in.at[r],
            send_sem=sq_send.at[r],
            recv_sem=sq_recv.at[r],
            device_id=(me, peer),
            device_id_type=pl.DeviceIdType.MESH,
        )

    def start_sq(r, carry):
        sq_copy(r).start()
        return carry

    lax.fori_loop(1, n_exp, start_sq, 0)

    def sent_proj(step, carry):
        for way in range(2):
            for part in range(CHUNKS):
                proj_copy(way, step, part).wait_send()
        return carry

    for step in range(1, hops):
        gu_step(step)
        if step == 1:
            lax.fori_loop(1, half // 2, sent_proj, 0)
        if step == 2:
            lax.fori_loop(half // 2, half - 1, sent_proj, 0)

    def wait_sq(r, carry):
        sq_copy(r).wait_recv()
        return carry

    lax.fori_loop(1, n_exp, wait_sq, 0)
    squares_in[0] = squares_out[z]
    row = jnp.sum(squares_in[...], axis=0)
    at_lane = lax.broadcasted_iota(jnp.int32, (share, HD), 1)
    at_row = lax.broadcasted_iota(jnp.int32, (share, HD), 0)
    column = jnp.sum(jnp.where(at_lane == at_row, row, 0.0), axis=1, keepdims=True)
    scale = lax.rsqrt(column / (local * n_exp) + EPS)
    for part in range(PARTS):
        term = gu_term(z, part)
        for way in range(2):
            term = gu_arrived(term, way, hops - 1, part)
        term = term * scale[part * piece : (part + 1) * piece]
        gate, upper = term[:, :units], term[:, units:]
        hidden = gate / (1.0 + jnp.exp(-gate)) * upper
        hidden_ref[pl.ds(pl.multiple_of(z * share + part * piece, piece), piece), :] = hidden.astype(BF16)

    def hid_copy(way, step, part, distance, ahead=0):
        block = place_at(1 - way, 2 * step + ahead)
        spot = hidden_ref.at[part_rows(block, part)]
        lane_of = (2 - distance) * hops + step
        return move(
            spot, spot, hid_send.at[way, lane_of, part], hid_recv.at[way, lane_of, part], way, distance
        )

    def hid_far(way, step, part):
        return step < hops - 1 or far(way, part, PARTS)

    for step in range(hops):
        for way, part in both:
            if step > 0:
                hid_copy(way, step - 1, part, 2, 2).wait_recv()
            if hid_far(way, step, part):
                hid_copy(way, step, part, 2).start()
            hid_copy(way, step, part, 1).start()
        if step == 0:
            for way, part in both:
                if far(way, part, PARTS):
                    gu_chain(way, 0, part).wait_send()
                gu_leaf(way, 0, part).wait_send()
        else:
            for way, part in both:
                gu_chain(way, step, part).wait_send()
                gu_leaf(way, step, part).wait_send()
    for step in range(hops):
        for way, part in both:
            hid_copy(way, step, part, 1, 1).wait_recv()
    for way, part in both:
        if hid_far(way, hops - 1, part):
            hid_copy(way, hops - 1, part, 2, 2).wait_recv()

    made = jnp.concatenate(
        [dot(hidden_ref[pl.ds(e * in_all, in_all), :], down_ref[e]) for e in range(experts)], axis=0
    ).astype(BF16)
    made_ref[...] = dot(by_device_ref[...], made).astype(BF16)

    def home_copy(r):
        peer = lax.rem(me + r, n_ctx)
        return pltpu.make_async_remote_copy(
            src_ref=made_ref.at[pl.ds(pl.multiple_of(peer * each, each), each)],
            dst_ref=back_ref.at[pl.ds(pl.multiple_of(me * each, each), each)],
            send_sem=home_send.at[r],
            recv_sem=home_recv.at[r],
            device_id=(peer, z),
            device_id_type=pl.DeviceIdType.MESH,
        )

    def start_home(r, carry):
        home_copy(r).start()
        return carry

    def wait_home(r, carry):
        home_copy(r).wait_recv()
        return carry

    lax.fori_loop(1, n_ctx, start_home, 0)
    back_ref[own, :] = made_ref[own, :]

    def sent_ctx(r, carry):
        there_copy(r).wait_send()
        return carry

    def sent_home(r, carry):
        home_copy(r).wait_send()
        return carry

    def sent_exp(r, carry):
        sq_copy(r).wait_send()
        return carry

    for way in range(2):
        for part in range(CHUNKS):
            if far(way, part, CHUNKS):
                proj_far(way, part).wait_send()
            proj_near(way, part).wait_send()
    for step in range(hops):
        for way, part in both:
            if hid_far(way, step, part):
                hid_copy(way, step, part, 2).wait_send()
            hid_copy(way, step, part, 1).wait_send()
    lax.fori_loop(1, n_exp, sent_exp, 0)
    lax.fori_loop(1, n_ctx, sent_ctx, 0)
    lax.fori_loop(1, n_ctx, wait_home, 0)
    out_ref[...] = dot(spread_ref[...], back_ref[...]).astype(BF16)
    lax.fori_loop(1, n_ctx, sent_home, 0)


def layer(n_ctx, n_exp, query, route, gain, keys, values, weight, gate, up, down):
    tokens, local = query.shape
    experts, _, units = gate.shape
    most = 2 * tokens // (experts * n_ctx)
    lots = n_ctx * experts * most
    share = lots // n_exp
    half = n_exp // 2
    heads = local // HD
    dma = pltpu.SemaphoreType.DMA
    vmem = pl.BlockSpec(memory_space=pltpu.VMEM)
    anywhere = pl.BlockSpec(memory_space=pl.ANY)
    return pl.pallas_call(
        functools.partial(layer_kernel, n_ctx, n_exp),
        out_shape=jax.ShapeDtypeStruct((tokens, local), BF16),
        in_specs=[vmem] * 3 + [anywhere] * 6,
        out_specs=vmem,
        scratch_shapes=[
            pltpu.VMEM((n_ctx, 2, tokens, HD), BF16),
            pltpu.VMEM((n_ctx, *weight.shape), BF16),
            pltpu.VMEM((heads, tokens, 1), F32),
            pltpu.VMEM((heads, tokens, 2 * HD), F32),
            pltpu.VMEM((tokens, local), BF16),
            pltpu.VMEM((experts, local, 2 * units), BF16),
            pltpu.VMEM((experts, units, local), BF16),
            pltpu.VMEM((2, half, tokens, local), BF16),
            pltpu.VMEM((2, half, tokens, local), BF16),
            pltpu.VMEM((tokens, local), BF16),
            pltpu.VMEM((n_exp, tokens, local), BF16),
            pltpu.VMEM((lots, tokens), BF16),
            pltpu.VMEM((tokens, lots), BF16),
            pltpu.VMEM((lots, lots), BF16),
            pltpu.VMEM((lots, lots), BF16),
            pltpu.VMEM((lots, local), BF16),
            pltpu.VMEM((lots, local), BF16),
            pltpu.VMEM((lots, local), BF16),
            pltpu.VMEM((lots, 2 * units), BF16),
            pltpu.VMEM((2, half, share, 2 * units), BF16),
            pltpu.VMEM((2, half, share, 2 * units), BF16),
            pltpu.VMEM((n_exp, 1, HD), F32),
            pltpu.VMEM((n_exp, 1, HD), F32),
            pltpu.VMEM((lots, units), BF16),
            pltpu.VMEM((lots, local), BF16),
            pltpu.VMEM((lots, local), BF16),
            dma((6,)),
            dma((2, MESSAGES)),
            dma((2, MESSAGES)),
            dma((2, half, CHUNKS)),
            dma((2, half, CHUNKS)),
            dma((n_ctx,)),
            dma((n_ctx,)),
            dma((2, half, PARTS)),
            dma((2, half, PARTS)),
            dma((n_exp,)),
            dma((n_exp,)),
            dma((2, half, PARTS)),
            dma((2, half, PARTS)),
            dma((n_ctx,)),
            dma((n_ctx,)),
        ],
        compiler_params=pltpu.CompilerParams(
            collective_id=0, has_side_effects=True, vmem_limit_bytes=VMEM_LIMIT
        ),
        name="layer",
    )(query, route, gain, keys, values, weight, gate, up, down)


def body(
    queries,
    keys,
    values,
    routes,
    route_score,
    output_weight,
    norm_gain,
    gate_weight,
    up_weight,
    down_weight,
):
    tokens, local = queries.shape[1:]
    returned = layer(
        lax.axis_size("ctx"),
        lax.axis_size("exp"),
        queries[0],
        routes[0].reshape(1, tokens),
        norm_gain.reshape(1, local),
        keys[0],
        values[0],
        output_weight,
        gate_weight,
        up_weight,
        down_weight,
    )
    scored = route_score[0][:, None] * returned.astype(F32)
    return scored.astype(BF16)[None]


def solution(mesh):
    placed = (
        P(None, "ctx", "exp"),
        P(None, "ctx", None),
        P(None, "ctx", None),
        P(None, "ctx", None),
        P(None, "ctx"),
        P("exp", "ctx"),
        P("exp"),
        P("ctx", "exp", None),
        P("ctx", "exp", None),
        P("ctx", None, "exp"),
    )
    return jax.shard_map(
        body, mesh=mesh, in_specs=placed, out_specs=P(None, "ctx", "exp"), check_vma=False
    )
```

```python
import functools
import math

import jax
import jax.numpy as jnp
from jax import lax
from jax.experimental import pallas as pl
from jax.experimental.pallas import tpu as pltpu
from jax.sharding import PartitionSpec as P

HD = 128
EPS = 1e-05
FAR_BELOW = -1e30
F32 = jnp.float32
BF16 = jnp.bfloat16
VMEM_LIMIT = 56 * 1024 * 1024


def dot(a, b):
    return jnp.dot(a, b, preferred_element_type=F32)


NX = 4
NY = 4
STEPS_OFF = (0, 1, -1, 2)
MESSAGES = 36
CHUNKS = 4
PARTS = 2


def layer_kernel(
    n_ctx,
    n_exp,
    query_ref,
    route_ref,
    score_ref,
    gain_ref,
    keys_hbm,
    values_hbm,
    weight_hbm,
    gate_hbm,
    up_hbm,
    down_hbm,
    out_ref,
    kv_ref,
    weight_ref,
    high_ref,
    total_ref,
    attn_ref,
    gu_ref,
    down_ref,
    proj_out,
    proj_in,
    proj_ref,
    term_ref,
    pick_ref,
    spread_ref,
    by_expert_ref,
    by_device_ref,
    packed_ref,
    arrived_ref,
    scaled_ref,
    part_ref,
    gu_out,
    gu_in,
    squares_out,
    squares_in,
    hidden_ref,
    made_ref,
    back_ref,
    load_sem,
    flow_send,
    flow_recv,
    proj_send,
    proj_recv,
    there_send,
    there_recv,
    gu_send,
    gu_recv,
    sq_send,
    sq_recv,
    hid_send,
    hid_recv,
    home_send,
    home_recv,
):
    me = lax.axis_index("ctx")
    z = lax.axis_index("exp")
    half = n_exp // 2
    tokens, local = query_ref.shape
    experts, _, twice = gu_ref.shape
    units = twice // 2
    lots = packed_ref.shape[0]
    each = lots // n_ctx
    most = each // experts

    barrier = pltpu.get_barrier_semaphore()

    def greet_ctx(r, carry):
        pl.semaphore_signal(
            barrier, inc=1, device_id=(lax.rem(me + r, n_ctx), z), device_id_type=pl.DeviceIdType.MESH
        )
        return carry

    def greet_exp(r, carry):
        pl.semaphore_signal(
            barrier, inc=1, device_id=(me, lax.rem(z + r, n_exp)), device_id_type=pl.DeviceIdType.MESH
        )
        return carry

    lax.fori_loop(1, n_ctx, greet_ctx, 0)
    lax.fori_loop(1, n_exp, greet_exp, 0)
    kv_heads = keys_hbm.shape[1] // HD
    columns = pl.ds(pl.multiple_of(z * kv_heads // n_exp * HD, HD), HD)
    own_loads = [
        pltpu.make_async_copy(keys_hbm.at[:, columns], kv_ref.at[me, 0], load_sem.at[3]),
        pltpu.make_async_copy(values_hbm.at[:, columns], kv_ref.at[me, 1], load_sem.at[4]),
        pltpu.make_async_copy(weight_hbm, weight_ref.at[me], load_sem.at[5]),
    ]
    for load in own_loads:
        load.start()
    loads = [
        pltpu.make_async_copy(gate_hbm, gu_ref.at[:, :, pl.ds(0, units)], load_sem.at[0]),
        pltpu.make_async_copy(up_hbm, gu_ref.at[:, :, pl.ds(units, units)], load_sem.at[1]),
        pltpu.make_async_copy(down_hbm, down_ref, load_sem.at[2]),
    ]
    for load in loads:
        load.start()

    pl.semaphore_wait(barrier, n_ctx - 1 + n_exp - 1)

    lane = me % 2
    chip = me // 2
    at_x, at_y = chip // NY, chip % NY

    def chip_at(dx, dy):
        return lax.rem(at_x + dx + NX, NX) * NY + lax.rem(at_y + dy + NY, NY)

    class Stream:
        def __init__(self, number, ref, size):
            self.number, self.ref, self.size = number, ref, size

        def chip(self, da, db):
            return chip_at(lane * da + (1 - lane) * db, lane * db + (1 - lane) * da)

        def copy(self, message, da, db, part, to, twin=False):
            block = self.chip(da, db) * 2 + (1 - lane if twin else lane)
            half_size = self.size // 2
            here = self.ref.at[block]
            if part is not None:
                here = self.ref.at[block, pl.ds(part * half_size, half_size)]
            target = chip * 2 + 1 - lane if to is None else self.chip(*to) * 2 + lane
            return pltpu.make_async_remote_copy(
                src_ref=here,
                dst_ref=here,
                send_sem=flow_send.at[self.number, message],
                recv_sem=flow_recv.at[self.number, message],
                device_id=(target, z),
                device_id_type=pl.DeviceIdType.MESH,
            )

        def first(self, side):
            return self.copy(side, 0, 0, None, ((1, 0), (-1, 0))[side])

        def first_in(self, side):
            return self.copy(side, (-1, 1)[side], 0, None, (1, 0))

        def relay(self, side):
            return self.copy(2 + side, (-1, 1)[side], 0, side, ((1, 0), (-1, 0))[side])

        def relay_in(self, side):
            return self.copy(2 + side, 2, 0, side, (1, 0))

        def second(self, i, side):
            return self.copy(4 + 2 * i + side, STEPS_OFF[i], 0, None, ((0, 1), (0, -1))[side])

        def second_in(self, i, side):
            return self.copy(4 + 2 * i + side, STEPS_OFF[i], (-1, 1)[side], None, (0, 1))

        def pass_on(self, i, side):
            return self.copy(
                12 + 2 * i + side, STEPS_OFF[i], (-1, 1)[side], side, ((0, 1), (0, -1))[side]
            )

        def pass_on_in(self, i, side):
            return self.copy(12 + 2 * i + side, STEPS_OFF[i], 2, side, (0, 1))

        def twin(self, i, j):
            return self.copy(20 + 4 * i + j, STEPS_OFF[i], STEPS_OFF[j], None, None)

        def twin_in(self, i, j):
            return self.copy(20 + 4 * j + i, STEPS_OFF[i], STEPS_OFF[j], None, None, True)

        def stage(self, number):
            if number == 0:
                for side in range(2):
                    self.first(side).start()
                self.twin(0, 0).start()
                for side in range(2):
                    self.second(0, side).start()
            if number == 1:
                for side in range(2):
                    self.first_in(side).wait_recv()
                    self.relay(side).start()
                    self.twin(2 - side, 0).start()
                for side in range(2):
                    self.second_in(0, side).wait_recv()
                    self.pass_on(0, side).start()
                    self.twin(0, 2 - side).start()
                for i in (2, 1):
                    for side in range(2):
                        self.second(i, side).start()
            if number == 2:
                for side in range(2):
                    self.relay_in(side).wait_recv()
                for side in range(2):
                    self.second(3, side).start()
                self.twin(3, 0).start()
                for side in range(2):
                    self.pass_on_in(0, side).wait_recv()
                self.twin(0, 3).start()
            if number == 3:
                for i in (1, 2):
                    for side in range(2):
                        self.second_in(i, side).wait_recv()
                        self.pass_on(i, side).start()
                        self.twin(i, 2 - side).start()
            if number == 4:
                for side in range(2):
                    self.second_in(3, side).wait_recv()
                    self.pass_on(3, side).start()
                    self.twin(3, 2 - side).start()
                for i in (1, 2):
                    for side in range(2):
                        self.pass_on_in(i, side).wait_recv()
                    self.twin(i, 3).start()
            if number == 5:
                for side in range(2):
                    self.pass_on_in(3, side).wait_recv()
                self.twin(3, 3).start()

        def sent(self):
            for side in range(2):
                self.first(side).wait_send()
                self.relay(side).wait_send()
                for i in range(4):
                    self.second(i, side).wait_send()
                    self.pass_on(i, side).wait_send()
            for i in range(4):
                for j in range(4):
                    self.twin(i, j).wait_send()

    kv_stream = Stream(0, kv_ref, 2)
    weight_stream = Stream(1, weight_ref, weight_hbm.shape[0])

    def stage(number):
        kv_stream.stage(number)
        weight_stream.stage(number)

    heads = local // HD
    block = 2 * tokens
    factor = math.log2(math.e) / math.sqrt(HD)

    def update(sources, own):
        width = block * len(sources)

        def gathered(which):
            blocks = [kv_ref[pl.ds(source * 2, 2), which].reshape(block, HD) for source in sources]
            return jnp.concatenate(blocks, axis=0) if len(blocks) > 1 else blocks[0]

        keys = gathered(0)
        values = jnp.concatenate([gathered(1), jnp.ones((width, HD), BF16)], axis=1)
        for head in range(heads):
            query = query_ref[:, head * HD : (head + 1) * HD]
            scores = lax.dot_general(
                query, keys, (((1,), (1,)), ((), ())), preferred_element_type=F32
            )
            if own:
                shape = (tokens, width)
                spot = lane * tokens + lax.broadcasted_iota(jnp.int32, shape, 0)
                visible = lax.broadcasted_iota(jnp.int32, shape, 1) <= spot
                scores = jnp.where(visible, scores, FAR_BELOW)
            highest = jnp.max(scores, axis=1, keepdims=True)
            if not own:
                before = high_ref[head]
                highest = jnp.maximum(highest, before)
            weights = jnp.exp2((scores - highest) * factor).astype(BF16)
            summed = dot(weights, values)
            if not own:
                summed = summed + total_ref[head] * jnp.exp2((before - highest) * factor)
            total_ref[head] = summed
            high_ref[head] = highest

    def source_of(i, j):
        kv_stream.twin_in(i, j).wait_recv()
        return kv_stream.chip(STEPS_OFF[i], STEPS_OFF[j])

    def attend(*places):
        sources = [source_of(i, j) for i, j in places]
        if len(sources) == 1:
            pl.when(sources[0] < chip)(lambda: update(sources, False))
            return
        low, high = jnp.minimum(*sources), jnp.maximum(*sources)
        pl.when(high < chip)(lambda: update(sources, False))
        pl.when(jnp.logical_and(low < chip, high >= chip))(lambda: update([low], False))

    in_all = lots // experts

    def make_tables():
        chosen_row = route_ref[...]
        square = (tokens, tokens)
        down_axis = lax.broadcasted_iota(jnp.int32, square, 0)
        over_axis = lax.broadcasted_iota(jnp.int32, square, 1)
        chosen_col = jnp.sum(
            jnp.where(down_axis == over_axis, chosen_row.astype(F32), 0.0), axis=1, keepdims=True
        ).astype(jnp.int32)
        same = chosen_col == chosen_row
        rank_col = jnp.sum(
            jnp.where(same & (over_axis < down_axis), 1.0, 0.0), axis=1, keepdims=True
        ).astype(jnp.int32)
        rank_row = jnp.sum(
            jnp.where(same & (down_axis < over_axis), 1.0, 0.0), axis=0, keepdims=True
        ).astype(jnp.int32)
        slot_col = chosen_col * most + rank_col
        slot_row = chosen_row * most + rank_row
        pick_ref[...] = jnp.where(
            lax.broadcasted_iota(jnp.int32, (lots, tokens), 0) == slot_row, 1.0, 0.0
        ).astype(BF16)
        spread_ref[...] = jnp.where(
            lax.broadcasted_iota(jnp.int32, (tokens, lots), 1) == slot_col, 1.0, 0.0
        ).astype(BF16)
        lot = lax.broadcasted_iota(jnp.int32, (1, lots), 1)
        to_row = lax.broadcasted_iota(jnp.int32, (lots, lots), 0)
        place = (lot % each) // most * in_all + lot // each * most + lot % most
        by_expert_ref[...] = jnp.where(to_row == place, 1.0, 0.0).astype(BF16)
        place = (lot % in_all) // most * each + lot // in_all * most + lot % most
        by_device_ref[...] = jnp.where(to_row == place, 1.0, 0.0).astype(BF16)

    for load in own_loads:
        load.wait()
    stage(0)
    make_tables()
    update([source_of(0, 0)], True)
    stage(1)
    stage(2)
    attend((1, 0), (2, 0))
    attend((0, 1), (0, 2))
    stage(3)
    attend((3, 0), (0, 3))
    attend((1, 1), (1, 2))
    stage(4)
    attend((2, 1), (2, 2))
    attend((3, 1), (3, 2))
    stage(5)
    attend((1, 3), (2, 3))
    attend((3, 3))
    for head in range(heads):
        summed = total_ref[head]
        attn_ref[:, head * HD : (head + 1) * HD] = (summed[:, :HD] / summed[:, HD:]).astype(BF16)
    for i in range(4):
        for j in range(4):
            weight_stream.twin_in(i, j).wait_recv()

    rows = tokens // CHUNKS
    pairs = n_ctx // n_exp

    def place_at(way, offset):
        return lax.rem(z + (offset if way == 0 else n_exp - offset), n_exp)

    def move(source, target, send_sem, recv_sem, way, distance):
        return pltpu.make_async_remote_copy(
            src_ref=source,
            dst_ref=target,
            send_sem=send_sem,
            recv_sem=recv_sem,
            device_id=(me, place_at(way, distance)),
            device_id_type=pl.DeviceIdType.MESH,
        )

    def proj_far(way, part):
        spot = pl.ds(part * rows, rows)
        return move(
            term_ref.at[place_at(way, half), spot],
            proj_in.at[way, 0, spot],
            proj_send.at[way, 0, part],
            proj_recv.at[way, 0, part],
            way,
            2,
        )

    def proj_near(way, part):
        spot = pl.ds(part * rows, rows)
        return move(
            term_ref.at[place_at(way, half - 1), spot],
            proj_in.at[way, half - 1, spot],
            proj_send.at[way, half - 1, part],
            proj_recv.at[way, half - 1, part],
            way,
            1,
        )

    def proj_copy(way, step, part):
        spot = pl.ds(part * rows, rows)
        return move(
            proj_out.at[way, step, spot],
            proj_in.at[way, step, spot],
            proj_send.at[way, step, part],
            proj_recv.at[way, step, part],
            way,
            1,
        )

    def make_term(target):
        columns = jnp.concatenate(
            [weight_ref[target * pairs + i] for i in range(pairs)], axis=1
        )
        term_ref[target] = dot(attn_ref[...], columns).astype(BF16)

    def proj_term(target, part):
        return term_ref[target, pl.ds(part * rows, rows)].astype(F32)

    def far(way, part, parts):
        return (part < parts // 2) == (way == 0)

    def proj_step(step, first):
        for part in range(CHUNKS):
            for way in range(2):
                spot = pl.ds(part * rows, rows)
                term = proj_term(place_at(way, half - 1 - step), part)
                if first:
                    proj_near(way, part).wait_recv()
                    term = term + proj_in[way, half - 1, spot].astype(F32)
                    if far(way, part, CHUNKS):
                        proj_far(way, part).wait_recv()
                        term = term + proj_in[way, 0, spot].astype(F32)
                else:
                    proj_copy(way, step - 1, part).wait_recv()
                    term = term + proj_in[way, step - 1, spot].astype(F32)
                proj_out[way, step, spot] = term.astype(BF16)
                proj_copy(way, step, part).start()

    make_term(place_at(0, half))
    for part in range(CHUNKS):
        for way in range(2):
            if far(way, part, CHUNKS):
                proj_far(way, part).start()
    for way in range(2):
        make_term(place_at(way, half - 1))
        for part in range(CHUNKS):
            proj_near(way, part).start()
    for way in range(2):
        make_term(place_at(way, half - 2))
    proj_step(1, True)

    def proj_loop(step, carry):
        for way in range(2):
            make_term(place_at(way, half - 1 - step))
        proj_step(step, False)
        for i, stream in enumerate((kv_stream, weight_stream)):
            pl.when(step == 2 + i)(stream.sent)
        return carry

    lax.fori_loop(2, half - 1, proj_loop, 0)
    make_term(z)
    for part in range(CHUNKS):
        spot = pl.ds(part * rows, rows)
        term = proj_term(z, part)
        for way in range(2):
            proj_copy(way, half - 2, part).wait_recv()
            term = term + proj_in[way, half - 2, spot].astype(F32)
        proj_ref[spot, :] = term.astype(BF16)

    packed_ref[...] = dot(pick_ref[...], proj_ref[...]).astype(BF16)

    def there_copy(r):
        peer = lax.rem(me + r, n_ctx)
        return pltpu.make_async_remote_copy(
            src_ref=packed_ref.at[pl.ds(pl.multiple_of(peer * each, each), each)],
            dst_ref=arrived_ref.at[pl.ds(pl.multiple_of(me * each, each), each)],
            send_sem=there_send.at[r],
            recv_sem=there_recv.at[r],
            device_id=(peer, z),
            device_id_type=pl.DeviceIdType.MESH,
        )

    def start_there(r, carry):
        there_copy(r).start()
        return carry

    def wait_there(r, carry):
        there_copy(r).wait_recv()
        return carry

    lax.fori_loop(1, n_ctx, start_there, 0)
    own = pl.ds(pl.multiple_of(me * each, each), each)
    arrived_ref[own, :] = packed_ref[own, :]
    for load in loads:
        load.wait()
    lax.fori_loop(1, n_ctx, wait_there, 0)

    share = lots // n_exp
    tokens_in = dot(by_expert_ref[...], arrived_ref[...])
    scaled_ref[...] = (tokens_in * gain_ref[...]).astype(BF16)
    first_expert = lax.rem(z + half, n_exp) * share // in_all

    def make_part(i):
        e = lax.rem(first_expert + i, experts)
        spot = pl.ds(pl.multiple_of(e * in_all, in_all), in_all)
        part_ref[spot, :] = dot(scaled_ref[spot, :], gu_ref[e]).astype(BF16)

    piece = share // PARTS

    hops = half // 2

    def part_rows(target, part):
        return pl.ds(pl.multiple_of(target * share + part * piece, piece), piece)

    def gu_chain(way, step, part):
        spot = pl.ds(part * piece, piece)
        if step == 0:
            source = part_ref.at[part_rows(place_at(way, half), part)]
        else:
            source = gu_out.at[way, step, spot]
        return move(
            source,
            gu_in.at[way, step, spot],
            gu_send.at[way, step, part],
            gu_recv.at[way, step, part],
            way,
            2,
        )

    def gu_leaf(way, step, part):
        spot = pl.ds(part * piece, piece)
        return move(
            part_ref.at[part_rows(place_at(way, half - 1 - 2 * step), part)],
            gu_in.at[way, hops + step, spot],
            gu_send.at[way, hops + step, part],
            gu_recv.at[way, hops + step, part],
            way,
            1,
        )

    def gu_term(target, part):
        return part_ref[part_rows(target, part), :].astype(F32)

    def gu_arrived(term, way, step, part):
        spot = pl.ds(part * piece, piece)
        gu_leaf(way, step, part).wait_recv()
        term = term + gu_in[way, hops + step, spot].astype(F32)
        if step > 0 or far(way, part, PARTS):
            gu_chain(way, step, part).wait_recv()
            term = term + gu_in[way, step, spot].astype(F32)
        return term

    both = [(way, part) for part in range(PARTS) for way in range(2)]

    def gu_leaves(step):
        for way, part in both:
            gu_leaf(way, step, part).start()

    def gu_step(step):
        gu_leaves(step)
        for way, part in both:
            term = gu_arrived(gu_term(place_at(way, half - 2 * step), part), way, step - 1, part)
            gu_out[way, step, pl.ds(part * piece, piece)] = term.astype(BF16)
            gu_chain(way, step, part).start()

    make_part(0)
    for way, part in both:
        if far(way, part, PARTS):
            gu_chain(way, 0, part).start()
    for i in range(1, experts):
        make_part(i)
    gu_leaves(0)

    squares = lax.dot_general(
        jnp.ones((8, local), BF16),
        (tokens_in * tokens_in).astype(BF16),
        (((1,), (1,)), ((), ())),
        preferred_element_type=F32,
    )
    for to in range(n_exp):
        squares_out[to, :, pl.ds(0, share)] = squares[0:1, to * share : (to + 1) * share]

    def sq_copy(r):
        peer = lax.rem(z + r, n_exp)
        return pltpu.make_async_remote_copy(
            src_ref=squares_out.at[peer],
            dst_ref=squares_in.at[r],
            send_sem=sq_send.at[r],
            recv_sem=sq_recv.at[r],
            device_id=(me, peer),
            device_id_type=pl.DeviceIdType.MESH,
        )

    def start_sq(r, carry):
        sq_copy(r).start()
        return carry

    lax.fori_loop(1, n_exp, start_sq, 0)

    def sent_proj(step, carry):
        for way in range(2):
            for part in range(CHUNKS):
                proj_copy(way, step, part).wait_send()
        return carry

    for step in range(1, hops):
        gu_step(step)
        if step == 1:
            lax.fori_loop(1, half // 2, sent_proj, 0)
        if step == 2:
            lax.fori_loop(half // 2, half - 1, sent_proj, 0)

    def wait_sq(r, carry):
        sq_copy(r).wait_recv()
        return carry

    lax.fori_loop(1, n_exp, wait_sq, 0)
    squares_in[0] = squares_out[z]
    row = jnp.sum(squares_in[...], axis=0)
    at_lane = lax.broadcasted_iota(jnp.int32, (share, HD), 1)
    at_row = lax.broadcasted_iota(jnp.int32, (share, HD), 0)
    column = jnp.sum(jnp.where(at_lane == at_row, row, 0.0), axis=1, keepdims=True)
    scale = lax.rsqrt(column / (local * n_exp) + EPS)

    def hid_copy(way, step, part, distance, ahead=0):
        block = place_at(1 - way, 2 * step + ahead)
        spot = hidden_ref.at[part_rows(block, part)]
        lane_of = (2 - distance) * hops + step
        return move(
            spot, spot, hid_send.at[way, lane_of, part], hid_recv.at[way, lane_of, part], way, distance
        )

    def hid_far(way, step, part):
        return step < hops - 1 or far(way, part, PARTS)

    for part in range(PARTS):
        term = gu_term(z, part)
        for way in range(2):
            term = gu_arrived(term, way, hops - 1, part)
        term = term * scale[part * piece : (part + 1) * piece]
        gate, upper = term[:, :units], term[:, units:]
        hidden = gate / (1.0 + jnp.exp(-gate)) * upper
        hidden_ref[part_rows(z, part), :] = hidden.astype(BF16)
        for way in range(2):
            hid_copy(way, 0, part, 2).start()
            hid_copy(way, 0, part, 1).start()

    for step in range(hops):
        for way, part in both:
            if step > 0:
                hid_copy(way, step - 1, part, 2, 2).wait_recv()
                if hid_far(way, step, part):
                    hid_copy(way, step, part, 2).start()
                hid_copy(way, step, part, 1).start()
        if step == 0:
            for way, part in both:
                if far(way, part, PARTS):
                    gu_chain(way, 0, part).wait_send()
                gu_leaf(way, 0, part).wait_send()
        else:
            for way, part in both:
                gu_chain(way, step, part).wait_send()
                gu_leaf(way, step, part).wait_send()
    for step in range(hops):
        for way, part in both:
            hid_copy(way, step, part, 1, 1).wait_recv()
    for way, part in both:
        if hid_far(way, hops - 1, part):
            hid_copy(way, hops - 1, part, 2, 2).wait_recv()

    made = jnp.concatenate(
        [dot(hidden_ref[pl.ds(e * in_all, in_all), :], down_ref[e]) for e in range(experts)], axis=0
    ).astype(BF16)
    made_ref[...] = dot(by_device_ref[...], made).astype(BF16)

    def home_copy(r):
        peer = lax.rem(me + r, n_ctx)
        return pltpu.make_async_remote_copy(
            src_ref=made_ref.at[pl.ds(pl.multiple_of(peer * each, each), each)],
            dst_ref=back_ref.at[pl.ds(pl.multiple_of(me * each, each), each)],
            send_sem=home_send.at[r],
            recv_sem=home_recv.at[r],
            device_id=(peer, z),
            device_id_type=pl.DeviceIdType.MESH,
        )

    def start_home(r, carry):
        home_copy(r).start()
        return carry

    def wait_home(r, carry):
        home_copy(r).wait_recv()
        return carry

    lax.fori_loop(1, n_ctx, start_home, 0)
    back_ref[own, :] = made_ref[own, :]

    def sent_ctx(r, carry):
        there_copy(r).wait_send()
        return carry

    def sent_home(r, carry):
        home_copy(r).wait_send()
        return carry

    def sent_exp(r, carry):
        sq_copy(r).wait_send()
        return carry

    for way in range(2):
        for part in range(CHUNKS):
            if far(way, part, CHUNKS):
                proj_far(way, part).wait_send()
            proj_near(way, part).wait_send()
    for step in range(hops):
        for way, part in both:
            if hid_far(way, step, part):
                hid_copy(way, step, part, 2).wait_send()
            hid_copy(way, step, part, 1).wait_send()
    lax.fori_loop(1, n_exp, sent_exp, 0)
    lax.fori_loop(1, n_ctx, sent_ctx, 0)
    square = (tokens, tokens)
    at_row = lax.broadcasted_iota(jnp.int32, square, 0)
    at_lane = lax.broadcasted_iota(jnp.int32, square, 1)
    score = jnp.sum(jnp.where(at_row == at_lane, score_ref[...], 0.0), axis=1, keepdims=True)
    lax.fori_loop(1, n_ctx, wait_home, 0)
    out_ref[...] = (dot(spread_ref[...], back_ref[...]) * score).astype(BF16)
    lax.fori_loop(1, n_ctx, sent_home, 0)


def layer(n_ctx, n_exp, query, route, score, gain, keys, values, weight, gate, up, down):
    tokens, local = query.shape
    experts, _, units = gate.shape
    most = 2 * tokens // (experts * n_ctx)
    lots = n_ctx * experts * most
    share = lots // n_exp
    half = n_exp // 2
    heads = local // HD
    dma = pltpu.SemaphoreType.DMA
    vmem = pl.BlockSpec(memory_space=pltpu.VMEM)
    anywhere = pl.BlockSpec(memory_space=pl.ANY)
    return pl.pallas_call(
        functools.partial(layer_kernel, n_ctx, n_exp),
        out_shape=jax.ShapeDtypeStruct((tokens, local), BF16),
        in_specs=[vmem] * 4 + [anywhere] * 6,
        out_specs=vmem,
        scratch_shapes=[
            pltpu.VMEM((n_ctx, 2, tokens, HD), BF16),
            pltpu.VMEM((n_ctx, *weight.shape), BF16),
            pltpu.VMEM((heads, tokens, 1), F32),
            pltpu.VMEM((heads, tokens, 2 * HD), F32),
            pltpu.VMEM((tokens, local), BF16),
            pltpu.VMEM((experts, local, 2 * units), BF16),
            pltpu.VMEM((experts, units, local), BF16),
            pltpu.VMEM((2, half, tokens, local), BF16),
            pltpu.VMEM((2, half, tokens, local), BF16),
            pltpu.VMEM((tokens, local), BF16),
            pltpu.VMEM((n_exp, tokens, local), BF16),
            pltpu.VMEM((lots, tokens), BF16),
            pltpu.VMEM((tokens, lots), BF16),
            pltpu.VMEM((lots, lots), BF16),
            pltpu.VMEM((lots, lots), BF16),
            pltpu.VMEM((lots, local), BF16),
            pltpu.VMEM((lots, local), BF16),
            pltpu.VMEM((lots, local), BF16),
            pltpu.VMEM((lots, 2 * units), BF16),
            pltpu.VMEM((2, half, share, 2 * units), BF16),
            pltpu.VMEM((2, half, share, 2 * units), BF16),
            pltpu.VMEM((n_exp, 1, HD), F32),
            pltpu.VMEM((n_exp, 1, HD), F32),
            pltpu.VMEM((lots, units), BF16),
            pltpu.VMEM((lots, local), BF16),
            pltpu.VMEM((lots, local), BF16),
            dma((6,)),
            dma((2, MESSAGES)),
            dma((2, MESSAGES)),
            dma((2, half, CHUNKS)),
            dma((2, half, CHUNKS)),
            dma((n_ctx,)),
            dma((n_ctx,)),
            dma((2, half, PARTS)),
            dma((2, half, PARTS)),
            dma((n_exp,)),
            dma((n_exp,)),
            dma((2, half, PARTS)),
            dma((2, half, PARTS)),
            dma((n_ctx,)),
            dma((n_ctx,)),
        ],
        compiler_params=pltpu.CompilerParams(
            collective_id=0, has_side_effects=True, vmem_limit_bytes=VMEM_LIMIT
        ),
        name="layer",
    )(query, route, score, gain, keys, values, weight, gate, up, down)


def body(
    queries,
    keys,
    values,
    routes,
    route_score,
    output_weight,
    norm_gain,
    gate_weight,
    up_weight,
    down_weight,
):
    tokens, local = queries.shape[1:]
    return layer(
        lax.axis_size("ctx"),
        lax.axis_size("exp"),
        queries[0],
        routes[0].reshape(1, tokens),
        route_score,
        norm_gain.reshape(1, local),
        keys[0],
        values[0],
        output_weight,
        gate_weight,
        up_weight,
        down_weight,
    )[None]


def solution(mesh):
    placed = (
        P(None, "ctx", "exp"),
        P(None, "ctx", None),
        P(None, "ctx", None),
        P(None, "ctx", None),
        P(None, "ctx"),
        P("exp", "ctx"),
        P("exp"),
        P("ctx", "exp", None),
        P("ctx", "exp", None),
        P("ctx", None, "exp"),
    )
    return jax.shard_map(
        body, mesh=mesh, in_specs=placed, out_specs=P(None, "ctx", "exp"), check_vma=False
    )
```

```python
import functools
import math

import jax
import jax.numpy as jnp
from jax import lax
from jax.experimental import pallas as pl
from jax.experimental.pallas import tpu as pltpu
from jax.sharding import PartitionSpec as P

HD = 128
EPS = 1e-05
FAR_BELOW = -1e30
F32 = jnp.float32
BF16 = jnp.bfloat16
VMEM_LIMIT = 56 * 1024 * 1024


def dot(a, b):
    return jnp.dot(a, b, preferred_element_type=F32)


NX = 4
NY = 4
STEPS_OFF = (0, 1, -1, 2)
MESSAGES = 36
CHUNKS = 4
PARTS = 2


def layer_kernel(
    n_ctx,
    n_exp,
    query_ref,
    route_ref,
    score_ref,
    gain_ref,
    keys_hbm,
    values_hbm,
    weight_hbm,
    gate_hbm,
    up_hbm,
    down_hbm,
    out_ref,
    kv_ref,
    weight_ref,
    high_ref,
    total_ref,
    attn_ref,
    gu_ref,
    down_ref,
    proj_out,
    proj_in,
    proj_ref,
    term_ref,
    pick_ref,
    spread_ref,
    by_expert_ref,
    by_device_ref,
    packed_ref,
    arrived_ref,
    scaled_ref,
    part_ref,
    gu_out,
    gu_in,
    squares_out,
    squares_in,
    hidden_ref,
    made_ref,
    back_ref,
    load_sem,
    flow_send,
    flow_recv,
    proj_send,
    proj_recv,
    there_send,
    there_recv,
    gu_send,
    gu_recv,
    sq_send,
    sq_recv,
    hid_send,
    hid_recv,
    home_send,
    home_recv,
):
    me = lax.axis_index("ctx")
    z = lax.axis_index("exp")
    half = n_exp // 2
    tokens, local = query_ref.shape
    experts, _, twice = gu_ref.shape
    units = twice // 2
    lots = packed_ref.shape[0]
    each = lots // n_ctx
    most = each // experts

    barrier = pltpu.get_barrier_semaphore()

    def greet_ctx(r, carry):
        pl.semaphore_signal(
            barrier, inc=1, device_id=(lax.rem(me + r, n_ctx), z), device_id_type=pl.DeviceIdType.MESH
        )
        return carry

    def greet_exp(r, carry):
        pl.semaphore_signal(
            barrier, inc=1, device_id=(me, lax.rem(z + r, n_exp)), device_id_type=pl.DeviceIdType.MESH
        )
        return carry

    lax.fori_loop(1, n_ctx, greet_ctx, 0)
    lax.fori_loop(1, n_exp, greet_exp, 0)
    kv_heads = keys_hbm.shape[1] // HD
    columns = pl.ds(pl.multiple_of(z * kv_heads // n_exp * HD, HD), HD)
    own_loads = [
        pltpu.make_async_copy(keys_hbm.at[:, columns], kv_ref.at[me, 0], load_sem.at[3]),
        pltpu.make_async_copy(values_hbm.at[:, columns], kv_ref.at[me, 1], load_sem.at[4]),
        pltpu.make_async_copy(weight_hbm, weight_ref.at[me], load_sem.at[5]),
    ]
    for load in own_loads:
        load.start()
    loads = [
        pltpu.make_async_copy(gate_hbm, gu_ref.at[:, :, pl.ds(0, units)], load_sem.at[0]),
        pltpu.make_async_copy(up_hbm, gu_ref.at[:, :, pl.ds(units, units)], load_sem.at[1]),
        pltpu.make_async_copy(down_hbm, down_ref, load_sem.at[2]),
    ]
    for load in loads:
        load.start()

    pl.semaphore_wait(barrier, n_ctx - 1 + n_exp - 1)

    lane = me % 2
    chip = me // 2
    at_x, at_y = chip // NY, chip % NY

    def chip_at(dx, dy):
        return lax.rem(at_x + dx + NX, NX) * NY + lax.rem(at_y + dy + NY, NY)

    class Stream:
        def __init__(self, number, ref, size):
            self.number, self.ref, self.size = number, ref, size

        def chip(self, da, db):
            return chip_at(lane * da + (1 - lane) * db, lane * db + (1 - lane) * da)

        def copy(self, message, da, db, part, to, twin=False):
            block = self.chip(da, db) * 2 + (1 - lane if twin else lane)
            half_size = self.size // 2
            here = self.ref.at[block]
            if part is not None:
                here = self.ref.at[block, pl.ds(part * half_size, half_size)]
            target = chip * 2 + 1 - lane if to is None else self.chip(*to) * 2 + lane
            return pltpu.make_async_remote_copy(
                src_ref=here,
                dst_ref=here,
                send_sem=flow_send.at[self.number, message],
                recv_sem=flow_recv.at[self.number, message],
                device_id=(target, z),
                device_id_type=pl.DeviceIdType.MESH,
            )

        def first(self, side):
            return self.copy(side, 0, 0, None, ((1, 0), (-1, 0))[side])

        def first_in(self, side):
            return self.copy(side, (-1, 1)[side], 0, None, (1, 0))

        def relay(self, side):
            return self.copy(2 + side, (-1, 1)[side], 0, side, ((1, 0), (-1, 0))[side])

        def relay_in(self, side):
            return self.copy(2 + side, 2, 0, side, (1, 0))

        def second(self, i, side):
            return self.copy(4 + 2 * i + side, STEPS_OFF[i], 0, None, ((0, 1), (0, -1))[side])

        def second_in(self, i, side):
            return self.copy(4 + 2 * i + side, STEPS_OFF[i], (-1, 1)[side], None, (0, 1))

        def pass_on(self, i, side):
            return self.copy(
                12 + 2 * i + side, STEPS_OFF[i], (-1, 1)[side], side, ((0, 1), (0, -1))[side]
            )

        def pass_on_in(self, i, side):
            return self.copy(12 + 2 * i + side, STEPS_OFF[i], 2, side, (0, 1))

        def twin(self, i, j):
            return self.copy(20 + 4 * i + j, STEPS_OFF[i], STEPS_OFF[j], None, None)

        def twin_in(self, i, j):
            return self.copy(20 + 4 * j + i, STEPS_OFF[i], STEPS_OFF[j], None, None, True)

        def stage(self, number):
            if number == 0:
                for side in range(2):
                    self.first(side).start()
                self.twin(0, 0).start()
                for side in range(2):
                    self.second(0, side).start()
            if number == 1:
                for side in range(2):
                    self.first_in(side).wait_recv()
                    self.relay(side).start()
                    self.twin(2 - side, 0).start()
                for side in range(2):
                    self.second_in(0, side).wait_recv()
                    self.pass_on(0, side).start()
                    self.twin(0, 2 - side).start()
                for i in (2, 1):
                    for side in range(2):
                        self.second(i, side).start()
            if number == 2:
                for side in range(2):
                    self.relay_in(side).wait_recv()
                for side in range(2):
                    self.second(3, side).start()
                self.twin(3, 0).start()
                for side in range(2):
                    self.pass_on_in(0, side).wait_recv()
                self.twin(0, 3).start()
            if number == 3:
                for i in (1, 2):
                    for side in range(2):
                        self.second_in(i, side).wait_recv()
                        self.pass_on(i, side).start()
                        self.twin(i, 2 - side).start()
            if number == 4:
                for side in range(2):
                    self.second_in(3, side).wait_recv()
                    self.pass_on(3, side).start()
                    self.twin(3, 2 - side).start()
                for i in (1, 2):
                    for side in range(2):
                        self.pass_on_in(i, side).wait_recv()
                    self.twin(i, 3).start()
            if number == 5:
                for side in range(2):
                    self.pass_on_in(3, side).wait_recv()
                self.twin(3, 3).start()

        def sent(self):
            for side in range(2):
                self.first(side).wait_send()
                self.relay(side).wait_send()
                for i in range(4):
                    self.second(i, side).wait_send()
                    self.pass_on(i, side).wait_send()
            for i in range(4):
                for j in range(4):
                    self.twin(i, j).wait_send()

    kv_stream = Stream(0, kv_ref, 2)
    weight_stream = Stream(1, weight_ref, weight_hbm.shape[0])

    def stage(number):
        kv_stream.stage(number)
        weight_stream.stage(number)

    heads = local // HD
    block = 2 * tokens
    factor = math.log2(math.e) / math.sqrt(HD)

    def update(sources, own):
        width = block * len(sources)

        def gathered(which):
            blocks = [kv_ref[pl.ds(source * 2, 2), which].reshape(block, HD) for source in sources]
            return jnp.concatenate(blocks, axis=0) if len(blocks) > 1 else blocks[0]

        keys = gathered(0)
        values = jnp.concatenate([gathered(1), jnp.ones((width, HD), BF16)], axis=1)
        for head in range(heads):
            query = query_ref[:, head * HD : (head + 1) * HD]
            scores = lax.dot_general(
                query, keys, (((1,), (1,)), ((), ())), preferred_element_type=F32
            )
            if own:
                shape = (tokens, width)
                spot = lane * tokens + lax.broadcasted_iota(jnp.int32, shape, 0)
                visible = lax.broadcasted_iota(jnp.int32, shape, 1) <= spot
                scores = jnp.where(visible, scores, FAR_BELOW)
            highest = jnp.max(scores, axis=1, keepdims=True)
            if not own:
                before = high_ref[head]
                highest = jnp.maximum(highest, before)
            weights = jnp.exp2((scores - highest) * factor).astype(BF16)
            summed = dot(weights, values)
            if not own:
                summed = summed + total_ref[head] * jnp.exp2((before - highest) * factor)
            total_ref[head] = summed
            high_ref[head] = highest

    def source_of(i, j):
        kv_stream.twin_in(i, j).wait_recv()
        return kv_stream.chip(STEPS_OFF[i], STEPS_OFF[j])

    def attend(*places):
        sources = [source_of(i, j) for i, j in places]
        if len(sources) == 1:
            pl.when(sources[0] < chip)(lambda: update(sources, False))
            return
        low, high = jnp.minimum(*sources), jnp.maximum(*sources)
        pl.when(high < chip)(lambda: update(sources, False))
        pl.when(jnp.logical_and(low < chip, high >= chip))(lambda: update([low], False))

    in_all = lots // experts

    def make_tables():
        chosen_row = route_ref[...]
        square = (tokens, tokens)
        down_axis = lax.broadcasted_iota(jnp.int32, square, 0)
        over_axis = lax.broadcasted_iota(jnp.int32, square, 1)
        chosen_col = jnp.sum(
            jnp.where(down_axis == over_axis, chosen_row.astype(F32), 0.0), axis=1, keepdims=True
        ).astype(jnp.int32)
        same = chosen_col == chosen_row
        rank_col = jnp.sum(
            jnp.where(same & (over_axis < down_axis), 1.0, 0.0), axis=1, keepdims=True
        ).astype(jnp.int32)
        rank_row = jnp.sum(
            jnp.where(same & (down_axis < over_axis), 1.0, 0.0), axis=0, keepdims=True
        ).astype(jnp.int32)
        slot_col = chosen_col * most + rank_col
        slot_row = chosen_row * most + rank_row
        pick_ref[...] = jnp.where(
            lax.broadcasted_iota(jnp.int32, (lots, tokens), 0) == slot_row, 1.0, 0.0
        ).astype(BF16)
        spread_ref[...] = jnp.where(
            lax.broadcasted_iota(jnp.int32, (tokens, lots), 1) == slot_col, 1.0, 0.0
        ).astype(BF16)
        lot = lax.broadcasted_iota(jnp.int32, (1, lots), 1)
        to_row = lax.broadcasted_iota(jnp.int32, (lots, lots), 0)
        place = (lot % each) // most * in_all + lot // each * most + lot % most
        by_expert_ref[...] = jnp.where(to_row == place, 1.0, 0.0).astype(BF16)
        place = (lot % in_all) // most * each + lot // in_all * most + lot % most
        by_device_ref[...] = jnp.where(to_row == place, 1.0, 0.0).astype(BF16)

    for load in own_loads:
        load.wait()
    stage(0)
    make_tables()
    update([source_of(0, 0)], True)
    stage(1)
    stage(2)
    attend((1, 0), (2, 0))
    attend((0, 1), (0, 2))
    stage(3)
    attend((3, 0), (0, 3))
    attend((1, 1), (1, 2))
    stage(4)
    attend((2, 1), (2, 2))
    attend((3, 1), (3, 2))
    stage(5)
    attend((1, 3), (2, 3))
    attend((3, 3))
    for head in range(heads):
        summed = total_ref[head]
        attn_ref[:, head * HD : (head + 1) * HD] = (summed[:, :HD] / summed[:, HD:]).astype(BF16)
    for i in range(4):
        for j in range(4):
            weight_stream.twin_in(i, j).wait_recv()

    rows = tokens // CHUNKS
    pairs = n_ctx // n_exp

    def place_at(way, offset):
        return lax.rem(z + (offset if way == 0 else n_exp - offset), n_exp)

    def move(source, target, send_sem, recv_sem, way, distance):
        return pltpu.make_async_remote_copy(
            src_ref=source,
            dst_ref=target,
            send_sem=send_sem,
            recv_sem=recv_sem,
            device_id=(me, place_at(way, distance)),
            device_id_type=pl.DeviceIdType.MESH,
        )

    def proj_far(way, part):
        spot = pl.ds(part * rows, rows)
        return move(
            term_ref.at[place_at(way, half), spot],
            proj_in.at[way, 0, spot],
            proj_send.at[way, 0, part],
            proj_recv.at[way, 0, part],
            way,
            2,
        )

    def proj_near(way, part):
        spot = pl.ds(part * rows, rows)
        return move(
            term_ref.at[place_at(way, half - 1), spot],
            proj_in.at[way, half - 1, spot],
            proj_send.at[way, half - 1, part],
            proj_recv.at[way, half - 1, part],
            way,
            1,
        )

    def proj_copy(way, step, part):
        spot = pl.ds(part * rows, rows)
        return move(
            proj_out.at[way, step, spot],
            proj_in.at[way, step, spot],
            proj_send.at[way, step, part],
            proj_recv.at[way, step, part],
            way,
            1,
        )

    def make_term(target):
        columns = jnp.concatenate(
            [weight_ref[target * pairs + i] for i in range(pairs)], axis=1
        )
        term_ref[target] = dot(attn_ref[...], columns).astype(BF16)

    def proj_term(target, part):
        return term_ref[target, pl.ds(part * rows, rows)].astype(F32)

    def far(way, part, parts):
        return (part < parts // 2) == (way == 0)

    def proj_step(step, first):
        for part in range(CHUNKS):
            for way in range(2):
                spot = pl.ds(part * rows, rows)
                term = proj_term(place_at(way, half - 1 - step), part)
                if first:
                    proj_near(way, part).wait_recv()
                    term = term + proj_in[way, half - 1, spot].astype(F32)
                    if far(way, part, CHUNKS):
                        proj_far(way, part).wait_recv()
                        term = term + proj_in[way, 0, spot].astype(F32)
                else:
                    proj_copy(way, step - 1, part).wait_recv()
                    term = term + proj_in[way, step - 1, spot].astype(F32)
                proj_out[way, step, spot] = term.astype(BF16)
                proj_copy(way, step, part).start()

    make_term(place_at(0, half))
    for part in range(CHUNKS):
        for way in range(2):
            if far(way, part, CHUNKS):
                proj_far(way, part).start()
    for way in range(2):
        make_term(place_at(way, half - 1))
        for part in range(CHUNKS):
            proj_near(way, part).start()
    for way in range(2):
        make_term(place_at(way, half - 2))
    proj_step(1, True)

    def proj_loop(step, carry):
        for way in range(2):
            make_term(place_at(way, half - 1 - step))
        proj_step(step, False)
        for i, stream in enumerate((kv_stream, weight_stream)):
            pl.when(step == 2 + i)(stream.sent)
        return carry

    lax.fori_loop(2, half - 1, proj_loop, 0)
    make_term(z)
    for part in range(CHUNKS):
        spot = pl.ds(part * rows, rows)
        term = proj_term(z, part)
        for way in range(2):
            proj_copy(way, half - 2, part).wait_recv()
            term = term + proj_in[way, half - 2, spot].astype(F32)
        proj_ref[spot, :] = term.astype(BF16)

    packed_ref[...] = dot(pick_ref[...], proj_ref[...]).astype(BF16)

    def far_first(r):
        return 1 + lax.rem(r + n_ctx // 3, n_ctx - 1)

    def there_copy(r):
        peer = lax.rem(me + r, n_ctx)
        return pltpu.make_async_remote_copy(
            src_ref=packed_ref.at[pl.ds(pl.multiple_of(peer * each, each), each)],
            dst_ref=arrived_ref.at[pl.ds(pl.multiple_of(me * each, each), each)],
            send_sem=there_send.at[r],
            recv_sem=there_recv.at[r],
            device_id=(peer, z),
            device_id_type=pl.DeviceIdType.MESH,
        )

    def start_there(r, carry):
        there_copy(far_first(r)).start()
        return carry

    def wait_there(r, carry):
        there_copy(r).wait_recv()
        return carry

    lax.fori_loop(1, n_ctx, start_there, 0)
    own = pl.ds(pl.multiple_of(me * each, each), each)
    arrived_ref[own, :] = packed_ref[own, :]
    for load in loads:
        load.wait()
    lax.fori_loop(1, n_ctx, wait_there, 0)

    share = lots // n_exp
    tokens_in = dot(by_expert_ref[...], arrived_ref[...])
    scaled_ref[...] = (tokens_in * gain_ref[...]).astype(BF16)
    first_expert = lax.rem(z + half, n_exp) * share // in_all

    def make_part(i):
        e = lax.rem(first_expert + i, experts)
        spot = pl.ds(pl.multiple_of(e * in_all, in_all), in_all)
        part_ref[spot, :] = dot(scaled_ref[spot, :], gu_ref[e]).astype(BF16)

    piece = share // PARTS

    hops = half // 2

    def part_rows(target, part):
        return pl.ds(pl.multiple_of(target * share + part * piece, piece), piece)

    stops = (*range(half, 2, -2), 2, 1, 0)
    long_hops = len(stops) - 3

    def gu_chain(way, step, part):
        spot = pl.ds(part * piece, piece)
        if step == 0:
            source = part_ref.at[part_rows(place_at(way, half), part)]
        else:
            source = gu_out.at[way, step, spot]
        return move(
            source,
            gu_in.at[way, step, spot],
            gu_send.at[way, step, part],
            gu_recv.at[way, step, part],
            way,
            stops[step] - stops[step + 1],
        )

    def gu_leaf(way, step, part):
        spot = pl.ds(part * piece, piece)
        slot = len(stops) - 1 + step
        return move(
            part_ref.at[part_rows(place_at(way, stops[step] - 1), part)],
            gu_in.at[way, slot, spot],
            gu_send.at[way, slot, part],
            gu_recv.at[way, slot, part],
            way,
            1,
        )

    def gu_term(target, part):
        return part_ref[part_rows(target, part), :].astype(F32)

    def gu_arrived(term, way, step, part):
        spot = pl.ds(part * piece, piece)
        if step < long_hops:
            gu_leaf(way, step, part).wait_recv()
            term = term + gu_in[way, len(stops) - 1 + step, spot].astype(F32)
        if step > 0 or far(way, part, PARTS):
            gu_chain(way, step, part).wait_recv()
            term = term + gu_in[way, step, spot].astype(F32)
        return term

    both = [(way, part) for part in range(PARTS) for way in range(2)]

    def gu_leaves(step):
        for way, part in both:
            gu_leaf(way, step, part).start()

    def gu_step(step):
        if step < long_hops:
            gu_leaves(step)
        for way, part in both:
            term = gu_arrived(gu_term(place_at(way, stops[step]), part), way, step - 1, part)
            gu_out[way, step, pl.ds(part * piece, piece)] = term.astype(BF16)
            gu_chain(way, step, part).start()

    make_part(0)
    for way, part in both:
        if far(way, part, PARTS):
            gu_chain(way, 0, part).start()
    for i in range(1, experts):
        make_part(i)
    gu_leaves(0)

    squares = lax.dot_general(
        jnp.ones((8, local), BF16),
        (tokens_in * tokens_in).astype(BF16),
        (((1,), (1,)), ((), ())),
        preferred_element_type=F32,
    )
    for to in range(n_exp):
        squares_out[to, :, pl.ds(0, share)] = squares[0:1, to * share : (to + 1) * share]

    def sq_copy(r):
        peer = lax.rem(z + r, n_exp)
        return pltpu.make_async_remote_copy(
            src_ref=squares_out.at[peer],
            dst_ref=squares_in.at[r],
            send_sem=sq_send.at[r],
            recv_sem=sq_recv.at[r],
            device_id=(me, peer),
            device_id_type=pl.DeviceIdType.MESH,
        )

    def start_sq(r, carry):
        sq_copy(r).start()
        return carry

    lax.fori_loop(1, n_exp, start_sq, 0)

    def sent_proj(step, carry):
        for way in range(2):
            for part in range(CHUNKS):
                proj_copy(way, step, part).wait_send()
        return carry

    for step in range(1, len(stops) - 1):
        gu_step(step)
        if step == 1:
            lax.fori_loop(1, half // 2, sent_proj, 0)
        if step == 2:
            lax.fori_loop(half // 2, half - 1, sent_proj, 0)

    def wait_sq(r, carry):
        sq_copy(r).wait_recv()
        return carry

    lax.fori_loop(1, n_exp, wait_sq, 0)
    squares_in[0] = squares_out[z]
    row = jnp.sum(squares_in[...], axis=0)
    at_lane = lax.broadcasted_iota(jnp.int32, (share, HD), 1)
    at_row = lax.broadcasted_iota(jnp.int32, (share, HD), 0)
    column = jnp.sum(jnp.where(at_lane == at_row, row, 0.0), axis=1, keepdims=True)
    scale = lax.rsqrt(column / (local * n_exp) + EPS)

    def hid_copy(way, step, part, distance, ahead=0):
        block = place_at(1 - way, 2 * step + ahead)
        spot = hidden_ref.at[part_rows(block, part)]
        lane_of = (2 - distance) * hops + step
        return move(
            spot, spot, hid_send.at[way, lane_of, part], hid_recv.at[way, lane_of, part], way, distance
        )

    def hid_far(way, step, part):
        return step < hops - 1 or far(way, part, PARTS)

    for part in range(PARTS):
        term = gu_term(z, part)
        for way in range(2):
            term = gu_arrived(term, way, len(stops) - 2, part)
        term = term * scale[part * piece : (part + 1) * piece]
        gate, upper = term[:, :units], term[:, units:]
        hidden = gate / (1.0 + jnp.exp(-gate)) * upper
        hidden_ref[part_rows(z, part), :] = hidden.astype(BF16)
        for way in range(2):
            hid_copy(way, 0, part, 2).start()
            hid_copy(way, 0, part, 1).start()

    for step in range(hops):
        for way, part in both:
            if step > 0:
                hid_copy(way, step - 1, part, 2, 2).wait_recv()
                if hid_far(way, step, part):
                    hid_copy(way, step, part, 2).start()
                hid_copy(way, step, part, 1).start()
        for way, part in both:
            if step > 0 or far(way, part, PARTS):
                gu_chain(way, step, part).wait_send()
            if step < long_hops:
                gu_leaf(way, step, part).wait_send()
    for step in range(hops):
        for way, part in both:
            hid_copy(way, step, part, 1, 1).wait_recv()
    for way, part in both:
        if hid_far(way, hops - 1, part):
            hid_copy(way, hops - 1, part, 2, 2).wait_recv()

    made = jnp.concatenate(
        [dot(hidden_ref[pl.ds(e * in_all, in_all), :], down_ref[e]) for e in range(experts)], axis=0
    ).astype(BF16)
    made_ref[...] = dot(by_device_ref[...], made).astype(BF16)

    def home_copy(r):
        peer = lax.rem(me + r, n_ctx)
        return pltpu.make_async_remote_copy(
            src_ref=made_ref.at[pl.ds(pl.multiple_of(peer * each, each), each)],
            dst_ref=back_ref.at[pl.ds(pl.multiple_of(me * each, each), each)],
            send_sem=home_send.at[r],
            recv_sem=home_recv.at[r],
            device_id=(peer, z),
            device_id_type=pl.DeviceIdType.MESH,
        )

    def start_home(r, carry):
        home_copy(far_first(r)).start()
        return carry

    def wait_home(r, carry):
        home_copy(r).wait_recv()
        return carry

    lax.fori_loop(1, n_ctx, start_home, 0)
    back_ref[own, :] = made_ref[own, :]

    def sent_ctx(r, carry):
        there_copy(r).wait_send()
        return carry

    def sent_home(r, carry):
        home_copy(r).wait_send()
        return carry

    def sent_exp(r, carry):
        sq_copy(r).wait_send()
        return carry

    for way in range(2):
        for part in range(CHUNKS):
            if far(way, part, CHUNKS):
                proj_far(way, part).wait_send()
            proj_near(way, part).wait_send()
    for step in range(hops, len(stops) - 1):
        for way, part in both:
            gu_chain(way, step, part).wait_send()
    for step in range(hops):
        for way, part in both:
            if hid_far(way, step, part):
                hid_copy(way, step, part, 2).wait_send()
            hid_copy(way, step, part, 1).wait_send()
    lax.fori_loop(1, n_exp, sent_exp, 0)
    lax.fori_loop(1, n_ctx, sent_ctx, 0)
    square = (tokens, tokens)
    at_row = lax.broadcasted_iota(jnp.int32, square, 0)
    at_lane = lax.broadcasted_iota(jnp.int32, square, 1)
    score = jnp.sum(jnp.where(at_row == at_lane, score_ref[...], 0.0), axis=1, keepdims=True)
    lax.fori_loop(1, n_ctx, wait_home, 0)
    out_ref[...] = (dot(spread_ref[...], back_ref[...]) * score).astype(BF16)
    lax.fori_loop(1, n_ctx, sent_home, 0)


def layer(n_ctx, n_exp, query, route, score, gain, keys, values, weight, gate, up, down):
    tokens, local = query.shape
    experts, _, units = gate.shape
    most = 2 * tokens // (experts * n_ctx)
    lots = n_ctx * experts * most
    share = lots // n_exp
    half = n_exp // 2
    heads = local // HD
    dma = pltpu.SemaphoreType.DMA
    vmem = pl.BlockSpec(memory_space=pltpu.VMEM)
    anywhere = pl.BlockSpec(memory_space=pl.ANY)
    return pl.pallas_call(
        functools.partial(layer_kernel, n_ctx, n_exp),
        out_shape=jax.ShapeDtypeStruct((tokens, local), BF16),
        in_specs=[vmem] * 4 + [anywhere] * 6,
        out_specs=vmem,
        scratch_shapes=[
            pltpu.VMEM((n_ctx, 2, tokens, HD), BF16),
            pltpu.VMEM((n_ctx, *weight.shape), BF16),
            pltpu.VMEM((heads, tokens, 1), F32),
            pltpu.VMEM((heads, tokens, 2 * HD), F32),
            pltpu.VMEM((tokens, local), BF16),
            pltpu.VMEM((experts, local, 2 * units), BF16),
            pltpu.VMEM((experts, units, local), BF16),
            pltpu.VMEM((2, half, tokens, local), BF16),
            pltpu.VMEM((2, half, tokens, local), BF16),
            pltpu.VMEM((tokens, local), BF16),
            pltpu.VMEM((n_exp, tokens, local), BF16),
            pltpu.VMEM((lots, tokens), BF16),
            pltpu.VMEM((tokens, lots), BF16),
            pltpu.VMEM((lots, lots), BF16),
            pltpu.VMEM((lots, lots), BF16),
            pltpu.VMEM((lots, local), BF16),
            pltpu.VMEM((lots, local), BF16),
            pltpu.VMEM((lots, local), BF16),
            pltpu.VMEM((lots, 2 * units), BF16),
            pltpu.VMEM((2, half, share, 2 * units), BF16),
            pltpu.VMEM((2, half, share, 2 * units), BF16),
            pltpu.VMEM((n_exp, 1, HD), F32),
            pltpu.VMEM((n_exp, 1, HD), F32),
            pltpu.VMEM((lots, units), BF16),
            pltpu.VMEM((lots, local), BF16),
            pltpu.VMEM((lots, local), BF16),
            dma((6,)),
            dma((2, MESSAGES)),
            dma((2, MESSAGES)),
            dma((2, half, CHUNKS)),
            dma((2, half, CHUNKS)),
            dma((n_ctx,)),
            dma((n_ctx,)),
            dma((2, half, PARTS)),
            dma((2, half, PARTS)),
            dma((n_exp,)),
            dma((n_exp,)),
            dma((2, half, PARTS)),
            dma((2, half, PARTS)),
            dma((n_ctx,)),
            dma((n_ctx,)),
        ],
        compiler_params=pltpu.CompilerParams(
            collective_id=0, has_side_effects=True, vmem_limit_bytes=VMEM_LIMIT
        ),
        name="layer",
    )(query, route, score, gain, keys, values, weight, gate, up, down)


def body(
    queries,
    keys,
    values,
    routes,
    route_score,
    output_weight,
    norm_gain,
    gate_weight,
    up_weight,
    down_weight,
):
    tokens, local = queries.shape[1:]
    return layer(
        lax.axis_size("ctx"),
        lax.axis_size("exp"),
        queries[0],
        routes[0].reshape(1, tokens),
        route_score,
        norm_gain.reshape(1, local),
        keys[0],
        values[0],
        output_weight,
        gate_weight,
        up_weight,
        down_weight,
    )[None]


def solution(mesh):
    placed = (
        P(None, "ctx", "exp"),
        P(None, "ctx", None),
        P(None, "ctx", None),
        P(None, "ctx", None),
        P(None, "ctx"),
        P("exp", "ctx"),
        P("exp"),
        P("ctx", "exp", None),
        P("ctx", "exp", None),
        P("ctx", None, "exp"),
    )
    return jax.shard_map(
        body, mesh=mesh, in_specs=placed, out_specs=P(None, "ctx", "exp"), check_vma=False
    )
```

```python
import functools
import math

import jax
import jax.numpy as jnp
from jax import lax
from jax.experimental import pallas as pl
from jax.experimental.pallas import tpu as pltpu
from jax.sharding import PartitionSpec as P

HD = 128
EPS = 1e-05
FAR_BELOW = -1e30
F32 = jnp.float32
BF16 = jnp.bfloat16
VMEM_LIMIT = 56 * 1024 * 1024


def dot(a, b):
    return jnp.dot(a, b, preferred_element_type=F32)


NX = 4
NY = 4
STEPS_OFF = (0, 1, -1, 2)
MESSAGES = 36
CHUNKS = 4
PARTS = 2


def layer_kernel(
    n_ctx,
    n_exp,
    query_ref,
    route_ref,
    score_ref,
    gain_ref,
    keys_hbm,
    values_hbm,
    weight_hbm,
    gate_hbm,
    up_hbm,
    down_hbm,
    out_ref,
    kv_ref,
    weight_ref,
    high_ref,
    total_ref,
    attn_ref,
    gu_ref,
    down_ref,
    proj_out,
    proj_in,
    proj_ref,
    term_ref,
    pick_ref,
    spread_ref,
    by_expert_ref,
    by_device_ref,
    packed_ref,
    arrived_ref,
    scaled_ref,
    part_ref,
    gu_out,
    gu_in,
    squares_out,
    squares_in,
    hidden_ref,
    made_ref,
    back_ref,
    load_sem,
    flow_send,
    flow_recv,
    proj_send,
    proj_recv,
    there_send,
    there_recv,
    gu_send,
    gu_recv,
    sq_send,
    sq_recv,
    hid_send,
    hid_recv,
    home_send,
    home_recv,
):
    me = lax.axis_index("ctx")
    z = lax.axis_index("exp")
    half = n_exp // 2
    tokens, local = query_ref.shape
    experts, _, twice = gu_ref.shape
    units = twice // 2
    lots = packed_ref.shape[0]
    each = lots // n_ctx
    most = each // experts

    barrier = pltpu.get_barrier_semaphore()

    def greet_ctx(r, carry):
        pl.semaphore_signal(
            barrier, inc=1, device_id=(lax.rem(me + r, n_ctx), z), device_id_type=pl.DeviceIdType.MESH
        )
        return carry

    def greet_exp(r, carry):
        pl.semaphore_signal(
            barrier, inc=1, device_id=(me, lax.rem(z + r, n_exp)), device_id_type=pl.DeviceIdType.MESH
        )
        return carry

    lax.fori_loop(1, n_ctx, greet_ctx, 0)
    lax.fori_loop(1, n_exp, greet_exp, 0)
    kv_heads = keys_hbm.shape[1] // HD
    columns = pl.ds(pl.multiple_of(z * kv_heads // n_exp * HD, HD), HD)
    own_loads = [
        pltpu.make_async_copy(keys_hbm.at[:, columns], kv_ref.at[me, 0], load_sem.at[3]),
        pltpu.make_async_copy(values_hbm.at[:, columns], kv_ref.at[me, 1], load_sem.at[4]),
        pltpu.make_async_copy(weight_hbm, weight_ref.at[me], load_sem.at[5]),
    ]
    for load in own_loads:
        load.start()
    loads = [
        pltpu.make_async_copy(gate_hbm, gu_ref.at[:, :, pl.ds(0, units)], load_sem.at[0]),
        pltpu.make_async_copy(up_hbm, gu_ref.at[:, :, pl.ds(units, units)], load_sem.at[1]),
        pltpu.make_async_copy(down_hbm, down_ref, load_sem.at[2]),
    ]
    for load in loads:
        load.start()

    pl.semaphore_wait(barrier, n_ctx - 1 + n_exp - 1)

    lane = me % 2
    chip = me // 2
    at_x, at_y = chip // NY, chip % NY

    def chip_at(dx, dy):
        return lax.rem(at_x + dx + NX, NX) * NY + lax.rem(at_y + dy + NY, NY)

    class Stream:
        def __init__(self, number, ref, size):
            self.number, self.ref, self.size = number, ref, size

        def chip(self, da, db):
            return chip_at(lane * da + (1 - lane) * db, lane * db + (1 - lane) * da)

        def copy(self, message, da, db, part, to, twin=False):
            block = self.chip(da, db) * 2 + (1 - lane if twin else lane)
            half_size = self.size // 2
            here = self.ref.at[block]
            if part is not None:
                here = self.ref.at[block, pl.ds(part * half_size, half_size)]
            target = chip * 2 + 1 - lane if to is None else self.chip(*to) * 2 + lane
            return pltpu.make_async_remote_copy(
                src_ref=here,
                dst_ref=here,
                send_sem=flow_send.at[self.number, message],
                recv_sem=flow_recv.at[self.number, message],
                device_id=(target, z),
                device_id_type=pl.DeviceIdType.MESH,
            )

        def first(self, side):
            return self.copy(side, 0, 0, None, ((1, 0), (-1, 0))[side])

        def first_in(self, side):
            return self.copy(side, (-1, 1)[side], 0, None, (1, 0))

        def relay(self, side):
            return self.copy(2 + side, (-1, 1)[side], 0, side, ((1, 0), (-1, 0))[side])

        def relay_in(self, side):
            return self.copy(2 + side, 2, 0, side, (1, 0))

        def second(self, i, side):
            return self.copy(4 + 2 * i + side, STEPS_OFF[i], 0, None, ((0, 1), (0, -1))[side])

        def second_in(self, i, side):
            return self.copy(4 + 2 * i + side, STEPS_OFF[i], (-1, 1)[side], None, (0, 1))

        def pass_on(self, i, side):
            return self.copy(
                12 + 2 * i + side, STEPS_OFF[i], (-1, 1)[side], side, ((0, 1), (0, -1))[side]
            )

        def pass_on_in(self, i, side):
            return self.copy(12 + 2 * i + side, STEPS_OFF[i], 2, side, (0, 1))

        def twin(self, i, j):
            return self.copy(20 + 4 * i + j, STEPS_OFF[i], STEPS_OFF[j], None, None)

        def twin_in(self, i, j):
            return self.copy(20 + 4 * j + i, STEPS_OFF[i], STEPS_OFF[j], None, None, True)

        def stage(self, number):
            if number == 0:
                for side in range(2):
                    self.first(side).start()
                self.twin(0, 0).start()
                for side in range(2):
                    self.second(0, side).start()
            if number == 1:
                for side in range(2):
                    self.first_in(side).wait_recv()
                    self.relay(side).start()
                    self.twin(2 - side, 0).start()
                for side in range(2):
                    self.second_in(0, side).wait_recv()
                    self.pass_on(0, side).start()
                    self.twin(0, 2 - side).start()
                for i in (2, 1):
                    for side in range(2):
                        self.second(i, side).start()
            if number == 2:
                for side in range(2):
                    self.relay_in(side).wait_recv()
                for side in range(2):
                    self.second(3, side).start()
                self.twin(3, 0).start()
                for side in range(2):
                    self.pass_on_in(0, side).wait_recv()
                self.twin(0, 3).start()
            if number == 3:
                for i in (1, 2):
                    for side in range(2):
                        self.second_in(i, side).wait_recv()
                        self.pass_on(i, side).start()
                        self.twin(i, 2 - side).start()
            if number == 4:
                for side in range(2):
                    self.second_in(3, side).wait_recv()
                    self.pass_on(3, side).start()
                    self.twin(3, 2 - side).start()
                for i in (1, 2):
                    for side in range(2):
                        self.pass_on_in(i, side).wait_recv()
                    self.twin(i, 3).start()
            if number == 5:
                for side in range(2):
                    self.pass_on_in(3, side).wait_recv()
                self.twin(3, 3).start()

        def sent(self):
            for side in range(2):
                self.first(side).wait_send()
                self.relay(side).wait_send()
                for i in range(4):
                    self.second(i, side).wait_send()
                    self.pass_on(i, side).wait_send()
            for i in range(4):
                for j in range(4):
                    self.twin(i, j).wait_send()

    kv_stream = Stream(0, kv_ref, 2)
    weight_stream = Stream(1, weight_ref, weight_hbm.shape[0])

    def stage(number):
        kv_stream.stage(number)
        weight_stream.stage(number)

    heads = local // HD
    block = 2 * tokens
    factor = math.log2(math.e) / math.sqrt(HD)

    def update(sources, own):
        width = block * len(sources)

        def gathered(which):
            blocks = [kv_ref[pl.ds(source * 2, 2), which].reshape(block, HD) for source in sources]
            return jnp.concatenate(blocks, axis=0) if len(blocks) > 1 else blocks[0]

        keys = gathered(0)
        values = jnp.concatenate([gathered(1), jnp.ones((width, HD), BF16)], axis=1)
        for head in range(heads):
            query = query_ref[:, head * HD : (head + 1) * HD]
            scores = lax.dot_general(
                query, keys, (((1,), (1,)), ((), ())), preferred_element_type=F32
            )
            if own:
                shape = (tokens, width)
                spot = lane * tokens + lax.broadcasted_iota(jnp.int32, shape, 0)
                visible = lax.broadcasted_iota(jnp.int32, shape, 1) <= spot
                scores = jnp.where(visible, scores, FAR_BELOW)
            highest = jnp.max(scores, axis=1, keepdims=True)
            if not own:
                before = high_ref[head]
                highest = jnp.maximum(highest, before)
            weights = jnp.exp2((scores - highest) * factor).astype(BF16)
            summed = dot(weights, values)
            if not own:
                summed = summed + total_ref[head] * jnp.exp2((before - highest) * factor)
            total_ref[head] = summed
            high_ref[head] = highest

    def source_of(i, j):
        kv_stream.twin_in(i, j).wait_recv()
        return kv_stream.chip(STEPS_OFF[i], STEPS_OFF[j])

    def attend(*places):
        sources = [source_of(i, j) for i, j in places]
        if len(sources) == 1:
            pl.when(sources[0] < chip)(lambda: update(sources, False))
            return
        low, high = jnp.minimum(*sources), jnp.maximum(*sources)
        pl.when(high < chip)(lambda: update(sources, False))
        pl.when(jnp.logical_and(low < chip, high >= chip))(lambda: update([low], False))

    in_all = lots // experts

    def make_tables():
        chosen_row = route_ref[...]
        square = (tokens, tokens)
        down_axis = lax.broadcasted_iota(jnp.int32, square, 0)
        over_axis = lax.broadcasted_iota(jnp.int32, square, 1)
        chosen_col = jnp.sum(
            jnp.where(down_axis == over_axis, chosen_row.astype(F32), 0.0), axis=1, keepdims=True
        ).astype(jnp.int32)
        same = chosen_col == chosen_row
        rank_col = jnp.sum(
            jnp.where(same & (over_axis < down_axis), 1.0, 0.0), axis=1, keepdims=True
        ).astype(jnp.int32)
        rank_row = jnp.sum(
            jnp.where(same & (down_axis < over_axis), 1.0, 0.0), axis=0, keepdims=True
        ).astype(jnp.int32)
        slot_col = chosen_col * most + rank_col
        slot_row = chosen_row * most + rank_row
        pick_ref[...] = jnp.where(
            lax.broadcasted_iota(jnp.int32, (lots, tokens), 0) == slot_row, 1.0, 0.0
        ).astype(BF16)
        spread_ref[...] = jnp.where(
            lax.broadcasted_iota(jnp.int32, (tokens, lots), 1) == slot_col, 1.0, 0.0
        ).astype(BF16)
        lot = lax.broadcasted_iota(jnp.int32, (1, lots), 1)
        to_row = lax.broadcasted_iota(jnp.int32, (lots, lots), 0)
        place = (lot % each) // most * in_all + lot // each * most + lot % most
        by_expert_ref[...] = jnp.where(to_row == place, 1.0, 0.0).astype(BF16)
        place = (lot % in_all) // most * each + lot // in_all * most + lot % most
        by_device_ref[...] = jnp.where(to_row == place, 1.0, 0.0).astype(BF16)

    for load in own_loads:
        load.wait()
    stage(0)
    make_tables()
    update([source_of(0, 0)], True)
    stage(1)
    stage(2)
    attend((1, 0), (2, 0))
    attend((0, 1), (0, 2))
    stage(3)
    attend((3, 0), (0, 3))
    attend((1, 1), (1, 2))
    stage(4)
    attend((2, 1), (2, 2))
    attend((3, 1), (3, 2))
    stage(5)
    attend((1, 3), (2, 3))
    attend((3, 3))
    for head in range(heads):
        summed = total_ref[head]
        attn_ref[:, head * HD : (head + 1) * HD] = (summed[:, :HD] / summed[:, HD:]).astype(BF16)
    for i in range(4):
        for j in range(4):
            weight_stream.twin_in(i, j).wait_recv()

    rows = tokens // CHUNKS
    pairs = n_ctx // n_exp

    def place_at(way, offset):
        return lax.rem(z + (offset if way == 0 else n_exp - offset), n_exp)

    def move(source, target, send_sem, recv_sem, way, distance):
        return pltpu.make_async_remote_copy(
            src_ref=source,
            dst_ref=target,
            send_sem=send_sem,
            recv_sem=recv_sem,
            device_id=(me, place_at(way, distance)),
            device_id_type=pl.DeviceIdType.MESH,
        )

    long_hops = 2
    last = half - 1 - long_hops

    def proj_copy(way, step, part, distance=1):
        spot = pl.ds(part * rows, rows)
        return move(
            proj_out.at[way, step, spot],
            proj_in.at[way, step, spot],
            proj_send.at[way, step, part],
            proj_recv.at[way, step, part],
            way,
            distance,
        )

    def proj_term_copy(way, offset, slot, part, distance):
        spot = pl.ds(part * rows, rows)
        return move(
            term_ref.at[place_at(way, offset), spot],
            proj_in.at[way, slot, spot],
            proj_send.at[way, slot, part],
            proj_recv.at[way, slot, part],
            way,
            distance,
        )

    def proj_far(way, part):
        return proj_term_copy(way, half, 0, part, 2)

    def proj_near(way, step, part):
        return proj_term_copy(way, half - 1 - 2 * step, last + 1 + step, part, 1)

    def make_term(target):
        columns = jnp.concatenate(
            [weight_ref[target * pairs + i] for i in range(pairs)], axis=1
        )
        term_ref[target] = dot(attn_ref[...], columns).astype(BF16)

    def proj_term(target, part):
        return term_ref[target, pl.ds(part * rows, rows)].astype(F32)

    def far(way, part, parts):
        return (part < parts // 2) == (way == 0)

    def proj_step(step, offset):
        for part in range(CHUNKS):
            for way in range(2):
                spot = pl.ds(part * rows, rows)
                term = proj_term(place_at(way, offset), part)
                side = isinstance(step, int) and step <= long_hops
                if side:
                    proj_near(way, step - 1, part).wait_recv()
                    term = term + proj_in[way, last + step, spot].astype(F32)
                if not side or step > 1:
                    proj_copy(way, step - 1, part).wait_recv()
                    term = term + proj_in[way, step - 1, spot].astype(F32)
                elif far(way, part, CHUNKS):
                    proj_far(way, part).wait_recv()
                    term = term + proj_in[way, 0, spot].astype(F32)
                proj_out[way, step, spot] = term.astype(BF16)
                proj_copy(way, step, part, 2 if side and step < long_hops else 1).start()

    def make_terms(offset):
        for way in range(2):
            make_term(place_at(way, offset))

    def start_near(step):
        for part in range(CHUNKS):
            for way in range(2):
                proj_near(way, step, part).start()

    make_term(place_at(0, half))
    for part in range(CHUNKS):
        for way in range(2):
            if far(way, part, CHUNKS):
                proj_far(way, part).start()
    make_terms(half - 1)
    start_near(0)
    make_terms(half - 2)
    make_terms(half - 3)
    start_near(1)
    proj_step(1, half - 2)
    make_terms(half - 4)
    kv_stream.sent()
    proj_step(2, half - 4)

    def proj_loop(step, carry):
        make_terms(last + 1 - step)
        proj_step(step, last + 1 - step)
        return carry

    lax.fori_loop(long_hops + 1, last + 1, proj_loop, 0)
    weight_stream.sent()
    make_term(z)
    for part in range(CHUNKS):
        spot = pl.ds(part * rows, rows)
        term = proj_term(z, part)
        for way in range(2):
            proj_copy(way, last, part).wait_recv()
            term = term + proj_in[way, last, spot].astype(F32)
        proj_ref[spot, :] = term.astype(BF16)

    packed_ref[...] = dot(pick_ref[...], proj_ref[...]).astype(BF16)

    def there_copy(r):
        peer = lax.rem(me + r, n_ctx)
        return pltpu.make_async_remote_copy(
            src_ref=packed_ref.at[pl.ds(pl.multiple_of(peer * each, each), each)],
            dst_ref=arrived_ref.at[pl.ds(pl.multiple_of(me * each, each), each)],
            send_sem=there_send.at[r],
            recv_sem=there_recv.at[r],
            device_id=(peer, z),
            device_id_type=pl.DeviceIdType.MESH,
        )

    def start_there(r, carry):
        there_copy(r).start()
        return carry

    def wait_there(r, carry):
        there_copy(r).wait_recv()
        return carry

    lax.fori_loop(1, n_ctx, start_there, 0)
    own = pl.ds(pl.multiple_of(me * each, each), each)
    arrived_ref[own, :] = packed_ref[own, :]
    for load in loads:
        load.wait()
    lax.fori_loop(1, n_ctx, wait_there, 0)

    share = lots // n_exp
    tokens_in = dot(by_expert_ref[...], arrived_ref[...])
    scaled_ref[...] = (tokens_in * gain_ref[...]).astype(BF16)
    first_expert = lax.rem(z + half, n_exp) * share // in_all

    def make_part(i):
        e = lax.rem(first_expert + i, experts)
        spot = pl.ds(pl.multiple_of(e * in_all, in_all), in_all)
        part_ref[spot, :] = dot(scaled_ref[spot, :], gu_ref[e]).astype(BF16)

    piece = share // PARTS

    hops = half // 2

    def part_rows(target, part):
        return pl.ds(pl.multiple_of(target * share + part * piece, piece), piece)

    def gu_chain(way, step, part):
        spot = pl.ds(part * piece, piece)
        if step == 0:
            source = part_ref.at[part_rows(place_at(way, half), part)]
        else:
            source = gu_out.at[way, step, spot]
        return move(
            source,
            gu_in.at[way, step, spot],
            gu_send.at[way, step, part],
            gu_recv.at[way, step, part],
            way,
            2,
        )

    def gu_leaf(way, step, part):
        spot = pl.ds(part * piece, piece)
        return move(
            part_ref.at[part_rows(place_at(way, half - 1 - 2 * step), part)],
            gu_in.at[way, hops + step, spot],
            gu_send.at[way, hops + step, part],
            gu_recv.at[way, hops + step, part],
            way,
            1,
        )

    def gu_term(target, part):
        return part_ref[part_rows(target, part), :].astype(F32)

    def gu_arrived(term, way, step, part):
        spot = pl.ds(part * piece, piece)
        gu_leaf(way, step, part).wait_recv()
        term = term + gu_in[way, hops + step, spot].astype(F32)
        if step > 0 or far(way, part, PARTS):
            gu_chain(way, step, part).wait_recv()
            term = term + gu_in[way, step, spot].astype(F32)
        return term

    both = [(way, part) for part in range(PARTS) for way in range(2)]

    def gu_leaves(step):
        for way, part in both:
            gu_leaf(way, step, part).start()

    def gu_step(step):
        gu_leaves(step)
        for way, part in both:
            term = gu_arrived(gu_term(place_at(way, half - 2 * step), part), way, step - 1, part)
            gu_out[way, step, pl.ds(part * piece, piece)] = term.astype(BF16)
            gu_chain(way, step, part).start()

    make_part(0)
    for way, part in both:
        if far(way, part, PARTS):
            gu_chain(way, 0, part).start()
    for i in range(1, experts):
        make_part(i)
    gu_leaves(0)

    squares = lax.dot_general(
        jnp.ones((8, local), BF16),
        (tokens_in * tokens_in).astype(BF16),
        (((1,), (1,)), ((), ())),
        preferred_element_type=F32,
    )
    for to in range(n_exp):
        squares_out[to, :, pl.ds(0, share)] = squares[0:1, to * share : (to + 1) * share]

    def sq_copy(r):
        peer = lax.rem(z + r, n_exp)
        return pltpu.make_async_remote_copy(
            src_ref=squares_out.at[peer],
            dst_ref=squares_in.at[r],
            send_sem=sq_send.at[r],
            recv_sem=sq_recv.at[r],
            device_id=(me, peer),
            device_id_type=pl.DeviceIdType.MESH,
        )

    def start_sq(r, carry):
        sq_copy(r).start()
        return carry

    lax.fori_loop(1, n_exp, start_sq, 0)

    def sent_proj(step, carry):
        for way in range(2):
            for part in range(CHUNKS):
                proj_copy(way, step, part).wait_send()
        return carry

    for step in range(1, hops):
        gu_step(step)
        if step == 1:
            lax.fori_loop(1, long_hops + 1, sent_proj, 0)
        if step == 2:
            lax.fori_loop(long_hops + 1, last + 1, sent_proj, 0)

    def wait_sq(r, carry):
        sq_copy(r).wait_recv()
        return carry

    lax.fori_loop(1, n_exp, wait_sq, 0)
    squares_in[0] = squares_out[z]
    row = jnp.sum(squares_in[...], axis=0)
    at_lane = lax.broadcasted_iota(jnp.int32, (share, HD), 1)
    at_row = lax.broadcasted_iota(jnp.int32, (share, HD), 0)
    column = jnp.sum(jnp.where(at_lane == at_row, row, 0.0), axis=1, keepdims=True)
    scale = lax.rsqrt(column / (local * n_exp) + EPS)

    strides = 3

    def hid_copy(way, step, part, distance, ahead=0):
        block = place_at(1 - way, 3 * step + ahead)
        spot = hidden_ref.at[part_rows(block, part)]
        slot = step + (0, 2, 5, 0)[distance]
        return move(spot, spot, hid_send.at[way, slot, part], hid_recv.at[way, slot, part], way, distance)

    def hid_distances(way, step, part):
        if step < strides - 1:
            return (3, 2, 1)
        return (2, 1) if far(way, part, PARTS) else (1,)

    for part in range(PARTS):
        term = gu_term(z, part)
        for way in range(2):
            term = gu_arrived(term, way, hops - 1, part)
        term = term * scale[part * piece : (part + 1) * piece]
        gate, upper = term[:, :units], term[:, units:]
        hidden = gate / (1.0 + jnp.exp(-gate)) * upper
        hidden_ref[part_rows(z, part), :] = hidden.astype(BF16)
        for way in range(2):
            for distance in hid_distances(way, 0, part):
                hid_copy(way, 0, part, distance).start()

    for step in range(strides):
        for way, part in both:
            if step > 0:
                hid_copy(way, step - 1, part, 3, 3).wait_recv()
                for distance in hid_distances(way, step, part):
                    hid_copy(way, step, part, distance).start()
        for way, part in both:
            if step > 0 or far(way, part, PARTS):
                gu_chain(way, step, part).wait_send()
            gu_leaf(way, step, part).wait_send()
    for step in range(strides):
        for way, part in both:
            for distance in hid_distances(way, step, part):
                if distance < 3:
                    hid_copy(way, step, part, distance, distance).wait_recv()

    made = jnp.concatenate(
        [dot(hidden_ref[pl.ds(e * in_all, in_all), :], down_ref[e]) for e in range(experts)], axis=0
    ).astype(BF16)
    made_ref[...] = dot(by_device_ref[...], made).astype(BF16)

    def home_copy(r):
        peer = lax.rem(me + r, n_ctx)
        return pltpu.make_async_remote_copy(
            src_ref=made_ref.at[pl.ds(pl.multiple_of(peer * each, each), each)],
            dst_ref=back_ref.at[pl.ds(pl.multiple_of(me * each, each), each)],
            send_sem=home_send.at[r],
            recv_sem=home_recv.at[r],
            device_id=(peer, z),
            device_id_type=pl.DeviceIdType.MESH,
        )

    def start_home(r, carry):
        home_copy(r).start()
        return carry

    def wait_home(r, carry):
        home_copy(r).wait_recv()
        return carry

    lax.fori_loop(1, n_ctx, start_home, 0)
    back_ref[own, :] = made_ref[own, :]

    def sent_ctx(r, carry):
        there_copy(r).wait_send()
        return carry

    def sent_home(r, carry):
        home_copy(r).wait_send()
        return carry

    def sent_exp(r, carry):
        sq_copy(r).wait_send()
        return carry

    for way in range(2):
        for part in range(CHUNKS):
            if far(way, part, CHUNKS):
                proj_far(way, part).wait_send()
            for step in range(long_hops):
                proj_near(way, step, part).wait_send()
    for way, part in both:
        gu_chain(way, hops - 1, part).wait_send()
        gu_leaf(way, hops - 1, part).wait_send()
    for step in range(strides):
        for way, part in both:
            for distance in hid_distances(way, step, part):
                hid_copy(way, step, part, distance).wait_send()
    lax.fori_loop(1, n_exp, sent_exp, 0)
    lax.fori_loop(1, n_ctx, sent_ctx, 0)
    square = (tokens, tokens)
    at_row = lax.broadcasted_iota(jnp.int32, square, 0)
    at_lane = lax.broadcasted_iota(jnp.int32, square, 1)
    score = jnp.sum(jnp.where(at_row == at_lane, score_ref[...], 0.0), axis=1, keepdims=True)
    lax.fori_loop(1, n_ctx, wait_home, 0)
    out_ref[...] = (dot(spread_ref[...], back_ref[...]) * score).astype(BF16)
    lax.fori_loop(1, n_ctx, sent_home, 0)


def layer(n_ctx, n_exp, query, route, score, gain, keys, values, weight, gate, up, down):
    tokens, local = query.shape
    experts, _, units = gate.shape
    most = 2 * tokens // (experts * n_ctx)
    lots = n_ctx * experts * most
    share = lots // n_exp
    half = n_exp // 2
    heads = local // HD
    dma = pltpu.SemaphoreType.DMA
    vmem = pl.BlockSpec(memory_space=pltpu.VMEM)
    anywhere = pl.BlockSpec(memory_space=pl.ANY)
    return pl.pallas_call(
        functools.partial(layer_kernel, n_ctx, n_exp),
        out_shape=jax.ShapeDtypeStruct((tokens, local), BF16),
        in_specs=[vmem] * 4 + [anywhere] * 6,
        out_specs=vmem,
        scratch_shapes=[
            pltpu.VMEM((n_ctx, 2, tokens, HD), BF16),
            pltpu.VMEM((n_ctx, *weight.shape), BF16),
            pltpu.VMEM((heads, tokens, 1), F32),
            pltpu.VMEM((heads, tokens, 2 * HD), F32),
            pltpu.VMEM((tokens, local), BF16),
            pltpu.VMEM((experts, local, 2 * units), BF16),
            pltpu.VMEM((experts, units, local), BF16),
            pltpu.VMEM((2, half, tokens, local), BF16),
            pltpu.VMEM((2, half, tokens, local), BF16),
            pltpu.VMEM((tokens, local), BF16),
            pltpu.VMEM((n_exp, tokens, local), BF16),
            pltpu.VMEM((lots, tokens), BF16),
            pltpu.VMEM((tokens, lots), BF16),
            pltpu.VMEM((lots, lots), BF16),
            pltpu.VMEM((lots, lots), BF16),
            pltpu.VMEM((lots, local), BF16),
            pltpu.VMEM((lots, local), BF16),
            pltpu.VMEM((lots, local), BF16),
            pltpu.VMEM((lots, 2 * units), BF16),
            pltpu.VMEM((2, half, share, 2 * units), BF16),
            pltpu.VMEM((2, half, share, 2 * units), BF16),
            pltpu.VMEM((n_exp, 1, HD), F32),
            pltpu.VMEM((n_exp, 1, HD), F32),
            pltpu.VMEM((lots, units), BF16),
            pltpu.VMEM((lots, local), BF16),
            pltpu.VMEM((lots, local), BF16),
            dma((6,)),
            dma((2, MESSAGES)),
            dma((2, MESSAGES)),
            dma((2, half, CHUNKS)),
            dma((2, half, CHUNKS)),
            dma((n_ctx,)),
            dma((n_ctx,)),
            dma((2, half, PARTS)),
            dma((2, half, PARTS)),
            dma((n_exp,)),
            dma((n_exp,)),
            dma((2, half, PARTS)),
            dma((2, half, PARTS)),
            dma((n_ctx,)),
            dma((n_ctx,)),
        ],
        compiler_params=pltpu.CompilerParams(
            collective_id=0, has_side_effects=True, vmem_limit_bytes=VMEM_LIMIT
        ),
        name="layer",
    )(query, route, score, gain, keys, values, weight, gate, up, down)


def body(
    queries,
    keys,
    values,
    routes,
    route_score,
    output_weight,
    norm_gain,
    gate_weight,
    up_weight,
    down_weight,
):
    tokens, local = queries.shape[1:]
    return layer(
        lax.axis_size("ctx"),
        lax.axis_size("exp"),
        queries[0],
        routes[0].reshape(1, tokens),
        route_score,
        norm_gain.reshape(1, local),
        keys[0],
        values[0],
        output_weight,
        gate_weight,
        up_weight,
        down_weight,
    )[None]


def solution(mesh):
    placed = (
        P(None, "ctx", "exp"),
        P(None, "ctx", None),
        P(None, "ctx", None),
        P(None, "ctx", None),
        P(None, "ctx"),
        P("exp", "ctx"),
        P("exp"),
        P("ctx", "exp", None),
        P("ctx", "exp", None),
        P("ctx", None, "exp"),
    )
    return jax.shard_map(
        body, mesh=mesh, in_specs=placed, out_specs=P(None, "ctx", "exp"), check_vma=False
    )
```

```python
import functools
import math

import jax
import jax.numpy as jnp
from jax import lax
from jax.experimental import pallas as pl
from jax.experimental.pallas import tpu as pltpu
from jax.sharding import PartitionSpec as P

HD = 128
EPS = 1e-05
FAR_BELOW = -1e30
F32 = jnp.float32
BF16 = jnp.bfloat16
VMEM_LIMIT = 56 * 1024 * 1024


def dot(a, b):
    return jnp.dot(a, b, preferred_element_type=F32)


NX = 4
NY = 4
STEPS_OFF = (0, 1, -1, 2)
ONES = 16
MESSAGES = 36
CHUNKS = 4
PARTS = 2


def layer_kernel(
    n_ctx,
    n_exp,
    query_ref,
    route_ref,
    score_ref,
    gain_ref,
    keys_hbm,
    values_hbm,
    weight_hbm,
    gate_hbm,
    up_hbm,
    down_hbm,
    out_ref,
    kv_ref,
    weight_ref,
    value_ref,
    across_ref,
    high_ref,
    total_ref,
    attn_ref,
    gu_ref,
    down_ref,
    proj_out,
    proj_in,
    proj_ref,
    term_ref,
    pick_ref,
    spread_ref,
    by_expert_ref,
    by_device_ref,
    packed_ref,
    arrived_ref,
    scaled_ref,
    part_ref,
    gu_out,
    gu_in,
    squares_out,
    squares_in,
    hidden_ref,
    made_ref,
    back_ref,
    load_sem,
    flow_send,
    flow_recv,
    proj_send,
    proj_recv,
    there_send,
    there_recv,
    gu_send,
    gu_recv,
    sq_send,
    sq_recv,
    hid_send,
    hid_recv,
    home_send,
    home_recv,
):
    me = lax.axis_index("ctx")
    z = lax.axis_index("exp")
    half = n_exp // 2
    tokens, local = query_ref.shape
    experts, _, twice = gu_ref.shape
    units = twice // 2
    lots = packed_ref.shape[0]
    each = lots // n_ctx
    most = each // experts

    barrier = pltpu.get_barrier_semaphore()

    def greet_ctx(r, carry):
        pl.semaphore_signal(
            barrier, inc=1, device_id=(lax.rem(me + r, n_ctx), z), device_id_type=pl.DeviceIdType.MESH
        )
        return carry

    def greet_exp(r, carry):
        pl.semaphore_signal(
            barrier, inc=1, device_id=(me, lax.rem(z + r, n_exp)), device_id_type=pl.DeviceIdType.MESH
        )
        return carry

    lax.fori_loop(1, n_ctx, greet_ctx, 0)
    lax.fori_loop(1, n_exp, greet_exp, 0)
    kv_heads = keys_hbm.shape[1] // HD
    columns = pl.ds(pl.multiple_of(z * kv_heads // n_exp * HD, HD), HD)
    own_loads = [
        pltpu.make_async_copy(keys_hbm.at[:, columns], kv_ref.at[me, 0], load_sem.at[3]),
        pltpu.make_async_copy(values_hbm.at[:, columns], value_ref, load_sem.at[4]),
        pltpu.make_async_copy(weight_hbm, weight_ref.at[me], load_sem.at[5]),
    ]
    for load in own_loads:
        load.start()
    loads = [
        pltpu.make_async_copy(gate_hbm, gu_ref.at[:, :, pl.ds(0, units)], load_sem.at[0]),
        pltpu.make_async_copy(up_hbm, gu_ref.at[:, :, pl.ds(units, units)], load_sem.at[1]),
        pltpu.make_async_copy(down_hbm, down_ref, load_sem.at[2]),
    ]
    for load in loads:
        load.start()

    heads = local // HD
    for head in range(heads):
        query = query_ref[:, head * HD : (head + 1) * HD].astype(F32)
        across_ref[head] = query.T.astype(BF16)
    for load in own_loads:
        load.wait()
    for square in range(tokens // HD):
        spot = pl.ds(square * HD, HD)
        kv_ref[me, 1, spot, :] = value_ref[spot, :].astype(F32).T.astype(BF16)

    pl.semaphore_wait(barrier, n_ctx - 1 + n_exp - 1)

    lane = me % 2
    chip = me // 2
    at_x, at_y = chip // NY, chip % NY

    def chip_at(dx, dy):
        return lax.rem(at_x + dx + NX, NX) * NY + lax.rem(at_y + dy + NY, NY)

    class Stream:
        def __init__(self, number, ref, size):
            self.number, self.ref, self.size = number, ref, size

        def chip(self, da, db):
            return chip_at(lane * da + (1 - lane) * db, lane * db + (1 - lane) * da)

        def copy(self, message, da, db, part, to, twin=False):
            block = self.chip(da, db) * 2 + (1 - lane if twin else lane)
            half_size = self.size // 2
            here = self.ref.at[block]
            if part is not None:
                here = self.ref.at[block, pl.ds(part * half_size, half_size)]
            target = chip * 2 + 1 - lane if to is None else self.chip(*to) * 2 + lane
            return pltpu.make_async_remote_copy(
                src_ref=here,
                dst_ref=here,
                send_sem=flow_send.at[self.number, message],
                recv_sem=flow_recv.at[self.number, message],
                device_id=(target, z),
                device_id_type=pl.DeviceIdType.MESH,
            )

        def first(self, side):
            return self.copy(side, 0, 0, None, ((1, 0), (-1, 0))[side])

        def first_in(self, side):
            return self.copy(side, (-1, 1)[side], 0, None, (1, 0))

        def relay(self, side):
            return self.copy(2 + side, (-1, 1)[side], 0, side, ((1, 0), (-1, 0))[side])

        def relay_in(self, side):
            return self.copy(2 + side, 2, 0, side, (1, 0))

        def second(self, i, side):
            return self.copy(4 + 2 * i + side, STEPS_OFF[i], 0, None, ((0, 1), (0, -1))[side])

        def second_in(self, i, side):
            return self.copy(4 + 2 * i + side, STEPS_OFF[i], (-1, 1)[side], None, (0, 1))

        def pass_on(self, i, side):
            return self.copy(
                12 + 2 * i + side, STEPS_OFF[i], (-1, 1)[side], side, ((0, 1), (0, -1))[side]
            )

        def pass_on_in(self, i, side):
            return self.copy(12 + 2 * i + side, STEPS_OFF[i], 2, side, (0, 1))

        def twin(self, i, j):
            return self.copy(20 + 4 * i + j, STEPS_OFF[i], STEPS_OFF[j], None, None)

        def twin_in(self, i, j):
            return self.copy(20 + 4 * j + i, STEPS_OFF[i], STEPS_OFF[j], None, None, True)

        def stage(self, number):
            if number == 0:
                for side in range(2):
                    self.first(side).start()
                self.twin(0, 0).start()
                for side in range(2):
                    self.second(0, side).start()
            if number == 1:
                for side in range(2):
                    self.first_in(side).wait_recv()
                    self.relay(side).start()
                    self.twin(2 - side, 0).start()
                for side in range(2):
                    self.second_in(0, side).wait_recv()
                    self.pass_on(0, side).start()
                    self.twin(0, 2 - side).start()
                for i in (2, 1):
                    for side in range(2):
                        self.second(i, side).start()
            if number == 2:
                for side in range(2):
                    self.relay_in(side).wait_recv()
                for side in range(2):
                    self.second(3, side).start()
                self.twin(3, 0).start()
                for side in range(2):
                    self.pass_on_in(0, side).wait_recv()
                self.twin(0, 3).start()
            if number == 3:
                for i in (1, 2):
                    for side in range(2):
                        self.second_in(i, side).wait_recv()
                        self.pass_on(i, side).start()
                        self.twin(i, 2 - side).start()
            if number == 4:
                for side in range(2):
                    self.second_in(3, side).wait_recv()
                    self.pass_on(3, side).start()
                    self.twin(3, 2 - side).start()
                for i in (1, 2):
                    for side in range(2):
                        self.pass_on_in(i, side).wait_recv()
                    self.twin(i, 3).start()
            if number == 5:
                for side in range(2):
                    self.pass_on_in(3, side).wait_recv()
                self.twin(3, 3).start()

        def sent(self):
            for side in range(2):
                self.first(side).wait_send()
                self.relay(side).wait_send()
                for i in range(4):
                    self.second(i, side).wait_send()
                    self.pass_on(i, side).wait_send()
            for i in range(4):
                for j in range(4):
                    self.twin(i, j).wait_send()

    kv_stream = Stream(0, kv_ref, 2)
    weight_stream = Stream(1, weight_ref, weight_hbm.shape[0])

    def stage(number):
        kv_stream.stage(number)
        weight_stream.stage(number)

    block = 2 * tokens
    factor = math.log2(math.e) / math.sqrt(HD)

    def update(sources, own):
        width = block * len(sources)

        keys = jnp.concatenate(
            [kv_ref[source * 2 + core, 0] for source in sources for core in range(2)], axis=0
        )
        squares = [
            kv_ref[source * 2 + core, 1, pl.ds(square * HD, HD), :]
            for source in sources
            for core in range(2)
            for square in range(tokens // HD)
        ]
        values = jnp.concatenate(
            [jnp.concatenate(squares, axis=1), jnp.ones((ONES, width), BF16)], axis=0
        )
        for head in range(heads):
            scores = dot(keys, across_ref[head])
            if own:
                shape = (width, tokens)
                spot = lane * tokens + lax.broadcasted_iota(jnp.int32, shape, 1)
                visible = lax.broadcasted_iota(jnp.int32, shape, 0) <= spot
                scores = jnp.where(visible, scores, FAR_BELOW)
            highest = jnp.max(scores, axis=0, keepdims=True)
            if not own:
                before = high_ref[head]
                highest = jnp.maximum(highest, before)
            weights = jnp.exp2((scores - highest) * factor).astype(BF16)
            summed = dot(values, weights)
            if not own:
                summed = summed + total_ref[head] * jnp.exp2((before - highest) * factor)
            total_ref[head] = summed
            high_ref[head] = highest

    def source_of(i, j):
        kv_stream.twin_in(i, j).wait_recv()
        return kv_stream.chip(STEPS_OFF[i], STEPS_OFF[j])

    def attend(*places):
        sources = [source_of(i, j) for i, j in places]
        if len(sources) == 1:
            pl.when(sources[0] < chip)(lambda: update(sources, False))
            return
        low, high = jnp.minimum(*sources), jnp.maximum(*sources)
        pl.when(high < chip)(lambda: update(sources, False))
        pl.when(jnp.logical_and(low < chip, high >= chip))(lambda: update([low], False))

    in_all = lots // experts

    def make_tables():
        chosen_row = route_ref[...]
        square = (tokens, tokens)
        down_axis = lax.broadcasted_iota(jnp.int32, square, 0)
        over_axis = lax.broadcasted_iota(jnp.int32, square, 1)
        chosen_col = jnp.sum(
            jnp.where(down_axis == over_axis, chosen_row.astype(F32), 0.0), axis=1, keepdims=True
        ).astype(jnp.int32)
        same = chosen_col == chosen_row
        rank_col = jnp.sum(
            jnp.where(same & (over_axis < down_axis), 1.0, 0.0), axis=1, keepdims=True
        ).astype(jnp.int32)
        rank_row = jnp.sum(
            jnp.where(same & (down_axis < over_axis), 1.0, 0.0), axis=0, keepdims=True
        ).astype(jnp.int32)
        slot_col = chosen_col * most + rank_col
        slot_row = chosen_row * most + rank_row
        pick_ref[...] = jnp.where(
            lax.broadcasted_iota(jnp.int32, (lots, tokens), 0) == slot_row, 1.0, 0.0
        ).astype(BF16)
        spread_ref[...] = jnp.where(
            lax.broadcasted_iota(jnp.int32, (tokens, lots), 1) == slot_col, 1.0, 0.0
        ).astype(BF16)
        lot = lax.broadcasted_iota(jnp.int32, (1, lots), 1)
        to_row = lax.broadcasted_iota(jnp.int32, (lots, lots), 0)
        place = (lot % each) // most * in_all + lot // each * most + lot % most
        by_expert_ref[...] = jnp.where(to_row == place, 1.0, 0.0).astype(BF16)
        place = (lot % in_all) // most * each + lot // in_all * most + lot % most
        by_device_ref[...] = jnp.where(to_row == place, 1.0, 0.0).astype(BF16)

    stage(0)
    make_tables()
    update([source_of(0, 0)], True)
    stage(1)
    stage(2)
    attend((1, 0), (2, 0))
    attend((0, 1), (0, 2))
    stage(3)
    attend((3, 0), (0, 3))
    attend((1, 1), (1, 2))
    stage(4)
    attend((2, 1), (2, 2))
    attend((3, 1), (3, 2))
    stage(5)
    attend((1, 3), (2, 3))
    attend((3, 3))
    for head in range(heads):
        summed = total_ref[head]
        weighted = summed[:HD] / summed[HD : HD + 1]
        attn_ref[:, head * HD : (head + 1) * HD] = weighted.T.astype(BF16)
    for i in range(4):
        for j in range(4):
            weight_stream.twin_in(i, j).wait_recv()

    rows = tokens // CHUNKS
    pairs = n_ctx // n_exp

    def place_at(way, offset):
        return lax.rem(z + (offset if way == 0 else n_exp - offset), n_exp)

    def move(source, target, send_sem, recv_sem, way, distance):
        return pltpu.make_async_remote_copy(
            src_ref=source,
            dst_ref=target,
            send_sem=send_sem,
            recv_sem=recv_sem,
            device_id=(me, place_at(way, distance)),
            device_id_type=pl.DeviceIdType.MESH,
        )

    def proj_far(way, part):
        spot = pl.ds(part * rows, rows)
        return move(
            term_ref.at[place_at(way, half), spot],
            proj_in.at[way, 0, spot],
            proj_send.at[way, 0, part],
            proj_recv.at[way, 0, part],
            way,
            2,
        )

    def proj_near(way, part):
        spot = pl.ds(part * rows, rows)
        return move(
            term_ref.at[place_at(way, half - 1), spot],
            proj_in.at[way, half - 1, spot],
            proj_send.at[way, half - 1, part],
            proj_recv.at[way, half - 1, part],
            way,
            1,
        )

    def proj_copy(way, step, part):
        spot = pl.ds(part * rows, rows)
        return move(
            proj_out.at[way, step, spot],
            proj_in.at[way, step, spot],
            proj_send.at[way, step, part],
            proj_recv.at[way, step, part],
            way,
            1,
        )

    def make_term(target):
        columns = jnp.concatenate(
            [weight_ref[target * pairs + i] for i in range(pairs)], axis=1
        )
        term_ref[target] = dot(attn_ref[...], columns).astype(BF16)

    def proj_term(target, part):
        return term_ref[target, pl.ds(part * rows, rows)].astype(F32)

    def far(way, part, parts):
        return (part < parts // 2) == (way == 0)

    def proj_step(step, first):
        for part in range(CHUNKS):
            for way in range(2):
                spot = pl.ds(part * rows, rows)
                term = proj_term(place_at(way, half - 1 - step), part)
                if first:
                    proj_near(way, part).wait_recv()
                    term = term + proj_in[way, half - 1, spot].astype(F32)
                    if far(way, part, CHUNKS):
                        proj_far(way, part).wait_recv()
                        term = term + proj_in[way, 0, spot].astype(F32)
                else:
                    proj_copy(way, step - 1, part).wait_recv()
                    term = term + proj_in[way, step - 1, spot].astype(F32)
                proj_out[way, step, spot] = term.astype(BF16)
                proj_copy(way, step, part).start()

    make_term(place_at(0, half))
    for part in range(CHUNKS):
        for way in range(2):
            if far(way, part, CHUNKS):
                proj_far(way, part).start()
    for way in range(2):
        make_term(place_at(way, half - 1))
        for part in range(CHUNKS):
            proj_near(way, part).start()
    for way in range(2):
        make_term(place_at(way, half - 2))
    proj_step(1, True)

    def proj_loop(step, carry):
        for way in range(2):
            make_term(place_at(way, half - 1 - step))
        proj_step(step, False)
        for i, stream in enumerate((kv_stream, weight_stream)):
            pl.when(step == 2 + i)(stream.sent)
        return carry

    lax.fori_loop(2, half - 1, proj_loop, 0)
    make_term(z)
    for part in range(CHUNKS):
        spot = pl.ds(part * rows, rows)
        term = proj_term(z, part)
        for way in range(2):
            proj_copy(way, half - 2, part).wait_recv()
            term = term + proj_in[way, half - 2, spot].astype(F32)
        proj_ref[spot, :] = term.astype(BF16)

    packed_ref[...] = dot(pick_ref[...], proj_ref[...]).astype(BF16)

    def there_copy(r):
        peer = lax.rem(me + r, n_ctx)
        return pltpu.make_async_remote_copy(
            src_ref=packed_ref.at[pl.ds(pl.multiple_of(peer * each, each), each)],
            dst_ref=arrived_ref.at[pl.ds(pl.multiple_of(me * each, each), each)],
            send_sem=there_send.at[r],
            recv_sem=there_recv.at[r],
            device_id=(peer, z),
            device_id_type=pl.DeviceIdType.MESH,
        )

    def start_there(r, carry):
        there_copy(r).start()
        return carry

    def wait_there(r, carry):
        there_copy(r).wait_recv()
        return carry

    lax.fori_loop(1, n_ctx, start_there, 0)
    own = pl.ds(pl.multiple_of(me * each, each), each)
    arrived_ref[own, :] = packed_ref[own, :]
    for load in loads:
        load.wait()
    lax.fori_loop(1, n_ctx, wait_there, 0)

    share = lots // n_exp
    tokens_in = dot(by_expert_ref[...], arrived_ref[...])
    scaled_ref[...] = (tokens_in * gain_ref[...]).astype(BF16)
    first_expert = lax.rem(z + half, n_exp) * share // in_all

    def make_part(i):
        e = lax.rem(first_expert + i, experts)
        spot = pl.ds(pl.multiple_of(e * in_all, in_all), in_all)
        part_ref[spot, :] = dot(scaled_ref[spot, :], gu_ref[e]).astype(BF16)

    piece = share // PARTS

    hops = half // 2

    def part_rows(target, part):
        return pl.ds(pl.multiple_of(target * share + part * piece, piece), piece)

    def gu_chain(way, step, part):
        spot = pl.ds(part * piece, piece)
        if step == 0:
            source = part_ref.at[part_rows(place_at(way, half), part)]
        else:
            source = gu_out.at[way, step, spot]
        return move(
            source,
            gu_in.at[way, step, spot],
            gu_send.at[way, step, part],
            gu_recv.at[way, step, part],
            way,
            2,
        )

    def gu_leaf(way, step, part):
        spot = pl.ds(part * piece, piece)
        return move(
            part_ref.at[part_rows(place_at(way, half - 1 - 2 * step), part)],
            gu_in.at[way, hops + step, spot],
            gu_send.at[way, hops + step, part],
            gu_recv.at[way, hops + step, part],
            way,
            1,
        )

    def gu_term(target, part):
        return part_ref[part_rows(target, part), :].astype(F32)

    def gu_arrived(term, way, step, part):
        spot = pl.ds(part * piece, piece)
        gu_leaf(way, step, part).wait_recv()
        term = term + gu_in[way, hops + step, spot].astype(F32)
        if step > 0 or far(way, part, PARTS):
            gu_chain(way, step, part).wait_recv()
            term = term + gu_in[way, step, spot].astype(F32)
        return term

    both = [(way, part) for part in range(PARTS) for way in range(2)]

    def gu_leaves(step):
        for way, part in both:
            gu_leaf(way, step, part).start()

    def gu_step(step):
        gu_leaves(step)
        for way, part in both:
            term = gu_arrived(gu_term(place_at(way, half - 2 * step), part), way, step - 1, part)
            gu_out[way, step, pl.ds(part * piece, piece)] = term.astype(BF16)
            gu_chain(way, step, part).start()

    make_part(0)
    for way, part in both:
        if far(way, part, PARTS):
            gu_chain(way, 0, part).start()
    for i in range(1, experts):
        make_part(i)
    gu_leaves(0)

    squares = lax.dot_general(
        jnp.ones((8, local), BF16),
        (tokens_in * tokens_in).astype(BF16),
        (((1,), (1,)), ((), ())),
        preferred_element_type=F32,
    )
    for to in range(n_exp):
        squares_out[to, :, pl.ds(0, share)] = squares[0:1, to * share : (to + 1) * share]

    def sq_copy(r):
        peer = lax.rem(z + r, n_exp)
        return pltpu.make_async_remote_copy(
            src_ref=squares_out.at[peer],
            dst_ref=squares_in.at[r],
            send_sem=sq_send.at[r],
            recv_sem=sq_recv.at[r],
            device_id=(me, peer),
            device_id_type=pl.DeviceIdType.MESH,
        )

    def start_sq(r, carry):
        sq_copy(r).start()
        return carry

    lax.fori_loop(1, n_exp, start_sq, 0)

    def sent_proj(step, carry):
        for way in range(2):
            for part in range(CHUNKS):
                proj_copy(way, step, part).wait_send()
        return carry

    for step in range(1, hops):
        gu_step(step)
        if step == 1:
            lax.fori_loop(1, half // 2, sent_proj, 0)
        if step == 2:
            lax.fori_loop(half // 2, half - 1, sent_proj, 0)

    def wait_sq(r, carry):
        sq_copy(r).wait_recv()
        return carry

    lax.fori_loop(1, n_exp, wait_sq, 0)
    squares_in[0] = squares_out[z]
    row = jnp.sum(squares_in[...], axis=0)
    at_lane = lax.broadcasted_iota(jnp.int32, (share, HD), 1)
    at_row = lax.broadcasted_iota(jnp.int32, (share, HD), 0)
    column = jnp.sum(jnp.where(at_lane == at_row, row, 0.0), axis=1, keepdims=True)
    scale = lax.rsqrt(column / (local * n_exp) + EPS)

    def hid_copy(way, step, part, distance, ahead=0):
        block = place_at(1 - way, 2 * step + ahead)
        spot = hidden_ref.at[part_rows(block, part)]
        lane_of = (2 - distance) * hops + step
        return move(
            spot, spot, hid_send.at[way, lane_of, part], hid_recv.at[way, lane_of, part], way, distance
        )

    def hid_far(way, step, part):
        return step < hops - 1 or far(way, part, PARTS)

    for part in range(PARTS):
        term = gu_term(z, part)
        for way in range(2):
            term = gu_arrived(term, way, hops - 1, part)
        term = term * scale[part * piece : (part + 1) * piece]
        gate, upper = term[:, :units], term[:, units:]
        hidden = gate / (1.0 + jnp.exp(-gate)) * upper
        hidden_ref[part_rows(z, part), :] = hidden.astype(BF16)
        for way in range(2):
            hid_copy(way, 0, part, 2).start()
            hid_copy(way, 0, part, 1).start()

    for step in range(hops):
        for way, part in both:
            if step > 0:
                hid_copy(way, step - 1, part, 2, 2).wait_recv()
                if hid_far(way, step, part):
                    hid_copy(way, step, part, 2).start()
                hid_copy(way, step, part, 1).start()
        if step == 0:
            for way, part in both:
                if far(way, part, PARTS):
                    gu_chain(way, 0, part).wait_send()
                gu_leaf(way, 0, part).wait_send()
        else:
            for way, part in both:
                gu_chain(way, step, part).wait_send()
                gu_leaf(way, step, part).wait_send()
    for step in range(hops):
        for way, part in both:
            hid_copy(way, step, part, 1, 1).wait_recv()
    for way, part in both:
        if hid_far(way, hops - 1, part):
            hid_copy(way, hops - 1, part, 2, 2).wait_recv()

    made = jnp.concatenate(
        [dot(hidden_ref[pl.ds(e * in_all, in_all), :], down_ref[e]) for e in range(experts)], axis=0
    ).astype(BF16)
    made_ref[...] = dot(by_device_ref[...], made).astype(BF16)

    def home_copy(r):
        peer = lax.rem(me + r, n_ctx)
        return pltpu.make_async_remote_copy(
            src_ref=made_ref.at[pl.ds(pl.multiple_of(peer * each, each), each)],
            dst_ref=back_ref.at[pl.ds(pl.multiple_of(me * each, each), each)],
            send_sem=home_send.at[r],
            recv_sem=home_recv.at[r],
            device_id=(peer, z),
            device_id_type=pl.DeviceIdType.MESH,
        )

    def start_home(r, carry):
        home_copy(r).start()
        return carry

    def wait_home(r, carry):
        home_copy(r).wait_recv()
        return carry

    lax.fori_loop(1, n_ctx, start_home, 0)
    back_ref[own, :] = made_ref[own, :]

    def sent_ctx(r, carry):
        there_copy(r).wait_send()
        return carry

    def sent_home(r, carry):
        home_copy(r).wait_send()
        return carry

    def sent_exp(r, carry):
        sq_copy(r).wait_send()
        return carry

    for way in range(2):
        for part in range(CHUNKS):
            if far(way, part, CHUNKS):
                proj_far(way, part).wait_send()
            proj_near(way, part).wait_send()
    for step in range(hops):
        for way, part in both:
            if hid_far(way, step, part):
                hid_copy(way, step, part, 2).wait_send()
            hid_copy(way, step, part, 1).wait_send()
    lax.fori_loop(1, n_exp, sent_exp, 0)
    lax.fori_loop(1, n_ctx, sent_ctx, 0)
    square = (tokens, tokens)
    at_row = lax.broadcasted_iota(jnp.int32, square, 0)
    at_lane = lax.broadcasted_iota(jnp.int32, square, 1)
    score = jnp.sum(jnp.where(at_row == at_lane, score_ref[...], 0.0), axis=1, keepdims=True)
    lax.fori_loop(1, n_ctx, wait_home, 0)
    out_ref[...] = (dot(spread_ref[...], back_ref[...]) * score).astype(BF16)
    lax.fori_loop(1, n_ctx, sent_home, 0)


def layer(n_ctx, n_exp, query, route, score, gain, keys, values, weight, gate, up, down):
    tokens, local = query.shape
    experts, _, units = gate.shape
    most = 2 * tokens // (experts * n_ctx)
    lots = n_ctx * experts * most
    share = lots // n_exp
    half = n_exp // 2
    heads = local // HD
    dma = pltpu.SemaphoreType.DMA
    vmem = pl.BlockSpec(memory_space=pltpu.VMEM)
    anywhere = pl.BlockSpec(memory_space=pl.ANY)
    return pl.pallas_call(
        functools.partial(layer_kernel, n_ctx, n_exp),
        out_shape=jax.ShapeDtypeStruct((tokens, local), BF16),
        in_specs=[vmem] * 4 + [anywhere] * 6,
        out_specs=vmem,
        scratch_shapes=[
            pltpu.VMEM((n_ctx, 2, tokens, HD), BF16),
            pltpu.VMEM((n_ctx, *weight.shape), BF16),
            pltpu.VMEM((tokens, HD), BF16),
            pltpu.VMEM((heads, HD, tokens), BF16),
            pltpu.VMEM((heads, 1, tokens), F32),
            pltpu.VMEM((heads, HD + ONES, tokens), F32),
            pltpu.VMEM((tokens, local), BF16),
            pltpu.VMEM((experts, local, 2 * units), BF16),
            pltpu.VMEM((experts, units, local), BF16),
            pltpu.VMEM((2, half, tokens, local), BF16),
            pltpu.VMEM((2, half, tokens, local), BF16),
            pltpu.VMEM((tokens, local), BF16),
            pltpu.VMEM((n_exp, tokens, local), BF16),
            pltpu.VMEM((lots, tokens), BF16),
            pltpu.VMEM((tokens, lots), BF16),
            pltpu.VMEM((lots, lots), BF16),
            pltpu.VMEM((lots, lots), BF16),
            pltpu.VMEM((lots, local), BF16),
            pltpu.VMEM((lots, local), BF16),
            pltpu.VMEM((lots, local), BF16),
            pltpu.VMEM((lots, 2 * units), BF16),
            pltpu.VMEM((2, half, share, 2 * units), BF16),
            pltpu.VMEM((2, half, share, 2 * units), BF16),
            pltpu.VMEM((n_exp, 1, HD), F32),
            pltpu.VMEM((n_exp, 1, HD), F32),
            pltpu.VMEM((lots, units), BF16),
            pltpu.VMEM((lots, local), BF16),
            pltpu.VMEM((lots, local), BF16),
            dma((6,)),
            dma((2, MESSAGES)),
            dma((2, MESSAGES)),
            dma((2, half, CHUNKS)),
            dma((2, half, CHUNKS)),
            dma((n_ctx,)),
            dma((n_ctx,)),
            dma((2, half, PARTS)),
            dma((2, half, PARTS)),
            dma((n_exp,)),
            dma((n_exp,)),
            dma((2, half, PARTS)),
            dma((2, half, PARTS)),
            dma((n_ctx,)),
            dma((n_ctx,)),
        ],
        compiler_params=pltpu.CompilerParams(
            collective_id=0, has_side_effects=True, vmem_limit_bytes=VMEM_LIMIT
        ),
        name="layer",
    )(query, route, score, gain, keys, values, weight, gate, up, down)


def body(
    queries,
    keys,
    values,
    routes,
    route_score,
    output_weight,
    norm_gain,
    gate_weight,
    up_weight,
    down_weight,
):
    tokens, local = queries.shape[1:]
    return layer(
        lax.axis_size("ctx"),
        lax.axis_size("exp"),
        queries[0],
        routes[0].reshape(1, tokens),
        route_score,
        norm_gain.reshape(1, local),
        keys[0],
        values[0],
        output_weight,
        gate_weight,
        up_weight,
        down_weight,
    )[None]


def solution(mesh):
    placed = (
        P(None, "ctx", "exp"),
        P(None, "ctx", None),
        P(None, "ctx", None),
        P(None, "ctx", None),
        P(None, "ctx"),
        P("exp", "ctx"),
        P("exp"),
        P("ctx", "exp", None),
        P("ctx", "exp", None),
        P("ctx", None, "exp"),
    )
    return jax.shard_map(
        body, mesh=mesh, in_specs=placed, out_specs=P(None, "ctx", "exp"), check_vma=False
    )
```

```python
import functools
import math

import jax
import jax.numpy as jnp
from jax import lax
from jax.experimental import pallas as pl
from jax.experimental.pallas import tpu as pltpu
from jax.sharding import PartitionSpec as P

HD = 128
EPS = 1e-05
FAR_BELOW = -1e30
F32 = jnp.float32
BF16 = jnp.bfloat16
VMEM_LIMIT = 56 * 1024 * 1024


def dot(a, b):
    return jnp.dot(a, b, preferred_element_type=F32)


NX = 4
NY = 4
STEPS_OFF = (0, 1, -1, 2)
MESSAGES = 36
CHUNKS = 4
PARTS = 2


def layer_kernel(
    n_ctx,
    n_exp,
    query_ref,
    route_ref,
    score_ref,
    gain_ref,
    keys_hbm,
    values_hbm,
    weight_hbm,
    gate_hbm,
    up_hbm,
    down_hbm,
    out_ref,
    kv_ref,
    weight_ref,
    high_ref,
    total_ref,
    attn_ref,
    gu_ref,
    down_ref,
    proj_out,
    proj_in,
    proj_ref,
    term_ref,
    pick_ref,
    spread_ref,
    by_expert_ref,
    by_device_ref,
    packed_ref,
    arrived_ref,
    squared_ref,
    part_ref,
    gu_out,
    gu_in,
    squares_out,
    squares_in,
    hidden_ref,
    made_ref,
    back_ref,
    load_sem,
    flow_send,
    flow_recv,
    proj_send,
    proj_recv,
    there_send,
    there_recv,
    gu_send,
    gu_recv,
    sq_send,
    sq_recv,
    hid_send,
    hid_recv,
    home_send,
    home_recv,
):
    me = lax.axis_index("ctx")
    z = lax.axis_index("exp")
    half = n_exp // 2
    tokens, local = query_ref.shape
    experts, _, twice = gu_ref.shape
    units = twice // 2
    lots = packed_ref.shape[0]
    each = lots // n_ctx
    most = each // experts

    barrier = pltpu.get_barrier_semaphore()

    def greet_ctx(r, carry):
        pl.semaphore_signal(
            barrier, inc=1, device_id=(lax.rem(me + r, n_ctx), z), device_id_type=pl.DeviceIdType.MESH
        )
        return carry

    def greet_exp(r, carry):
        pl.semaphore_signal(
            barrier, inc=1, device_id=(me, lax.rem(z + r, n_exp)), device_id_type=pl.DeviceIdType.MESH
        )
        return carry

    lax.fori_loop(1, n_ctx, greet_ctx, 0)
    lax.fori_loop(1, n_exp, greet_exp, 0)
    kv_heads = keys_hbm.shape[1] // HD
    columns = pl.ds(pl.multiple_of(z * kv_heads // n_exp * HD, HD), HD)
    own_loads = [
        pltpu.make_async_copy(keys_hbm.at[:, columns], kv_ref.at[me, 0], load_sem.at[3]),
        pltpu.make_async_copy(values_hbm.at[:, columns], kv_ref.at[me, 1], load_sem.at[4]),
        pltpu.make_async_copy(weight_hbm, weight_ref.at[me], load_sem.at[5]),
    ]
    for load in own_loads:
        load.start()
    loads = [
        pltpu.make_async_copy(gate_hbm, gu_ref.at[:, :, pl.ds(0, units)], load_sem.at[0]),
        pltpu.make_async_copy(up_hbm, gu_ref.at[:, :, pl.ds(units, units)], load_sem.at[1]),
        pltpu.make_async_copy(down_hbm, down_ref, load_sem.at[2]),
    ]
    for load in loads:
        load.start()

    pl.semaphore_wait(barrier, n_ctx - 1 + n_exp - 1)

    lane = me % 2
    chip = me // 2
    at_x, at_y = chip // NY, chip % NY

    def chip_at(dx, dy):
        return lax.rem(at_x + dx + NX, NX) * NY + lax.rem(at_y + dy + NY, NY)

    class Stream:
        def __init__(self, number, ref, size):
            self.number, self.ref, self.size = number, ref, size

        def chip(self, da, db):
            return chip_at(lane * da + (1 - lane) * db, lane * db + (1 - lane) * da)

        def copy(self, message, da, db, part, to, twin=False):
            block = self.chip(da, db) * 2 + (1 - lane if twin else lane)
            half_size = self.size // 2
            here = self.ref.at[block]
            if part is not None:
                here = self.ref.at[block, pl.ds(part * half_size, half_size)]
            target = chip * 2 + 1 - lane if to is None else self.chip(*to) * 2 + lane
            return pltpu.make_async_remote_copy(
                src_ref=here,
                dst_ref=here,
                send_sem=flow_send.at[self.number, message],
                recv_sem=flow_recv.at[self.number, message],
                device_id=(target, z),
                device_id_type=pl.DeviceIdType.MESH,
            )

        def first(self, side):
            return self.copy(side, 0, 0, None, ((1, 0), (-1, 0))[side])

        def first_in(self, side):
            return self.copy(side, (-1, 1)[side], 0, None, (1, 0))

        def relay(self, side):
            return self.copy(2 + side, (-1, 1)[side], 0, side, ((1, 0), (-1, 0))[side])

        def relay_in(self, side):
            return self.copy(2 + side, 2, 0, side, (1, 0))

        def second(self, i, side):
            return self.copy(4 + 2 * i + side, STEPS_OFF[i], 0, None, ((0, 1), (0, -1))[side])

        def second_in(self, i, side):
            return self.copy(4 + 2 * i + side, STEPS_OFF[i], (-1, 1)[side], None, (0, 1))

        def pass_on(self, i, side):
            return self.copy(
                12 + 2 * i + side, STEPS_OFF[i], (-1, 1)[side], side, ((0, 1), (0, -1))[side]
            )

        def pass_on_in(self, i, side):
            return self.copy(12 + 2 * i + side, STEPS_OFF[i], 2, side, (0, 1))

        def twin(self, i, j):
            return self.copy(20 + 4 * i + j, STEPS_OFF[i], STEPS_OFF[j], None, None)

        def twin_in(self, i, j):
            return self.copy(20 + 4 * j + i, STEPS_OFF[i], STEPS_OFF[j], None, None, True)

        def stage(self, number):
            if number == 0:
                for side in range(2):
                    self.first(side).start()
                self.twin(0, 0).start()
                for side in range(2):
                    self.second(0, side).start()
            if number == 1:
                for side in range(2):
                    self.first_in(side).wait_recv()
                    self.relay(side).start()
                    self.twin(2 - side, 0).start()
                for side in range(2):
                    self.second_in(0, side).wait_recv()
                    self.pass_on(0, side).start()
                    self.twin(0, 2 - side).start()
                for i in (2, 1):
                    for side in range(2):
                        self.second(i, side).start()
            if number == 2:
                for side in range(2):
                    self.relay_in(side).wait_recv()
                for side in range(2):
                    self.second(3, side).start()
                self.twin(3, 0).start()
                for side in range(2):
                    self.pass_on_in(0, side).wait_recv()
                self.twin(0, 3).start()
            if number == 3:
                for i in (1, 2):
                    for side in range(2):
                        self.second_in(i, side).wait_recv()
                        self.pass_on(i, side).start()
                        self.twin(i, 2 - side).start()
            if number == 4:
                for side in range(2):
                    self.second_in(3, side).wait_recv()
                    self.pass_on(3, side).start()
                    self.twin(3, 2 - side).start()
                for i in (1, 2):
                    for side in range(2):
                        self.pass_on_in(i, side).wait_recv()
                    self.twin(i, 3).start()
            if number == 5:
                for side in range(2):
                    self.pass_on_in(3, side).wait_recv()
                self.twin(3, 3).start()

        def sent(self):
            for side in range(2):
                self.first(side).wait_send()
                self.relay(side).wait_send()
                for i in range(4):
                    self.second(i, side).wait_send()
                    self.pass_on(i, side).wait_send()
            for i in range(4):
                for j in range(4):
                    self.twin(i, j).wait_send()

    kv_stream = Stream(0, kv_ref, 2)
    weight_stream = Stream(1, weight_ref, weight_hbm.shape[0])

    def stage(number):
        kv_stream.stage(number)
        weight_stream.stage(number)

    heads = local // HD
    block = 2 * tokens
    factor = math.log2(math.e) / math.sqrt(HD)

    def update(sources, own):
        width = block * len(sources)

        def gathered(which):
            blocks = [kv_ref[pl.ds(source * 2, 2), which].reshape(block, HD) for source in sources]
            return jnp.concatenate(blocks, axis=0) if len(blocks) > 1 else blocks[0]

        keys = gathered(0)
        values = jnp.concatenate([gathered(1), jnp.ones((width, HD), BF16)], axis=1)
        for head in range(heads):
            query = query_ref[:, head * HD : (head + 1) * HD]
            scores = lax.dot_general(
                query, keys, (((1,), (1,)), ((), ())), preferred_element_type=F32
            )
            if own:
                shape = (tokens, width)
                spot = lane * tokens + lax.broadcasted_iota(jnp.int32, shape, 0)
                visible = lax.broadcasted_iota(jnp.int32, shape, 1) <= spot
                scores = jnp.where(visible, scores, FAR_BELOW)
            highest = jnp.max(scores, axis=1, keepdims=True)
            if not own:
                before = high_ref[head]
                highest = jnp.maximum(highest, before)
            weights = jnp.exp2((scores - highest) * factor).astype(BF16)
            summed = dot(weights, values)
            if not own:
                summed = summed + total_ref[head] * jnp.exp2((before - highest) * factor)
            total_ref[head] = summed
            high_ref[head] = highest

    def source_of(i, j):
        kv_stream.twin_in(i, j).wait_recv()
        return kv_stream.chip(STEPS_OFF[i], STEPS_OFF[j])

    def attend(*places):
        sources = [source_of(i, j) for i, j in places]
        if len(sources) == 1:
            pl.when(sources[0] < chip)(lambda: update(sources, False))
            return
        low, high = jnp.minimum(*sources), jnp.maximum(*sources)
        pl.when(high < chip)(lambda: update(sources, False))
        pl.when(jnp.logical_and(low < chip, high >= chip))(lambda: update([low], False))

    in_all = lots // experts

    def make_tables():
        chosen_row = route_ref[...]
        square = (tokens, tokens)
        down_axis = lax.broadcasted_iota(jnp.int32, square, 0)
        over_axis = lax.broadcasted_iota(jnp.int32, square, 1)
        chosen_col = jnp.sum(
            jnp.where(down_axis == over_axis, chosen_row.astype(F32), 0.0), axis=1, keepdims=True
        ).astype(jnp.int32)
        same = chosen_col == chosen_row
        rank_col = jnp.sum(
            jnp.where(same & (over_axis < down_axis), 1.0, 0.0), axis=1, keepdims=True
        ).astype(jnp.int32)
        rank_row = jnp.sum(
            jnp.where(same & (down_axis < over_axis), 1.0, 0.0), axis=0, keepdims=True
        ).astype(jnp.int32)
        slot_col = chosen_col * most + rank_col
        slot_row = chosen_row * most + rank_row
        pick_ref[...] = jnp.where(
            lax.broadcasted_iota(jnp.int32, (lots, tokens), 0) == slot_row, 1.0, 0.0
        ).astype(BF16)
        spread_ref[...] = jnp.where(
            lax.broadcasted_iota(jnp.int32, (tokens, lots), 1) == slot_col, 1.0, 0.0
        ).astype(BF16)
        lot = lax.broadcasted_iota(jnp.int32, (1, lots), 1)
        to_row = lax.broadcasted_iota(jnp.int32, (lots, lots), 0)
        place = (lot % each) // most * in_all + lot // each * most + lot % most
        by_expert_ref[...] = jnp.where(to_row == place, 1.0, 0.0).astype(BF16)
        place = (lot % in_all) // most * each + lot // in_all * most + lot % most
        by_device_ref[...] = jnp.where(to_row == place, 1.0, 0.0).astype(BF16)

    for load in own_loads:
        load.wait()
    stage(0)
    make_tables()
    update([source_of(0, 0)], True)
    stage(1)
    stage(2)
    attend((1, 0), (2, 0))
    attend((0, 1), (0, 2))
    stage(3)
    attend((3, 0), (0, 3))
    attend((1, 1), (1, 2))
    stage(4)
    attend((2, 1), (2, 2))
    attend((3, 1), (3, 2))
    stage(5)
    attend((1, 3), (2, 3))
    attend((3, 3))
    for head in range(heads):
        summed = total_ref[head]
        attn_ref[:, head * HD : (head + 1) * HD] = (summed[:, :HD] / summed[:, HD:]).astype(BF16)
    for i in range(4):
        for j in range(4):
            weight_stream.twin_in(i, j).wait_recv()

    rows = tokens // CHUNKS
    pairs = n_ctx // n_exp

    def place_at(way, offset):
        return lax.rem(z + (offset if way == 0 else n_exp - offset), n_exp)

    def move(source, target, send_sem, recv_sem, way, distance):
        return pltpu.make_async_remote_copy(
            src_ref=source,
            dst_ref=target,
            send_sem=send_sem,
            recv_sem=recv_sem,
            device_id=(me, place_at(way, distance)),
            device_id_type=pl.DeviceIdType.MESH,
        )

    def proj_far(way, part):
        spot = pl.ds(part * rows, rows)
        return move(
            term_ref.at[place_at(way, half), spot],
            proj_in.at[way, 0, spot],
            proj_send.at[way, 0, part],
            proj_recv.at[way, 0, part],
            way,
            2,
        )

    def proj_near(way, part):
        spot = pl.ds(part * rows, rows)
        return move(
            term_ref.at[place_at(way, half - 1), spot],
            proj_in.at[way, half - 1, spot],
            proj_send.at[way, half - 1, part],
            proj_recv.at[way, half - 1, part],
            way,
            1,
        )

    def proj_copy(way, step, part):
        spot = pl.ds(part * rows, rows)
        return move(
            proj_out.at[way, step, spot],
            proj_in.at[way, step, spot],
            proj_send.at[way, step, part],
            proj_recv.at[way, step, part],
            way,
            1,
        )

    def make_term(target):
        columns = jnp.concatenate(
            [weight_ref[target * pairs + i] for i in range(pairs)], axis=1
        )
        term_ref[target] = dot(attn_ref[...], columns).astype(BF16)

    def proj_term(target, part):
        return term_ref[target, pl.ds(part * rows, rows)].astype(F32)

    def far(way, part, parts):
        return (part < parts // 2) == (way == 0)

    def proj_step(step, first):
        for part in range(CHUNKS):
            for way in range(2):
                spot = pl.ds(part * rows, rows)
                term = proj_term(place_at(way, half - 1 - step), part)
                if first:
                    proj_near(way, part).wait_recv()
                    term = term + proj_in[way, half - 1, spot].astype(F32)
                    if far(way, part, CHUNKS):
                        proj_far(way, part).wait_recv()
                        term = term + proj_in[way, 0, spot].astype(F32)
                else:
                    proj_copy(way, step - 1, part).wait_recv()
                    term = term + proj_in[way, step - 1, spot].astype(F32)
                proj_out[way, step, spot] = term.astype(BF16)
                proj_copy(way, step, part).start()

    make_term(place_at(0, half))
    for part in range(CHUNKS):
        for way in range(2):
            if far(way, part, CHUNKS):
                proj_far(way, part).start()
    for way in range(2):
        make_term(place_at(way, half - 1))
        for part in range(CHUNKS):
            proj_near(way, part).start()
    for way in range(2):
        make_term(place_at(way, half - 2))
    proj_step(1, True)

    def proj_loop(step, carry):
        for way in range(2):
            make_term(place_at(way, half - 1 - step))
        proj_step(step, False)
        for i, stream in enumerate((kv_stream, weight_stream)):
            pl.when(step == 2 + i)(stream.sent)
        return carry

    lax.fori_loop(2, half - 1, proj_loop, 0)
    make_term(z)
    for part in range(CHUNKS):
        spot = pl.ds(part * rows, rows)
        term = proj_term(z, part)
        for way in range(2):
            proj_copy(way, half - 2, part).wait_recv()
            term = term + proj_in[way, half - 2, spot].astype(F32)
        proj_ref[spot, :] = term.astype(BF16)

    packed_ref[...] = dot(pick_ref[...], proj_ref[...]).astype(BF16)

    def far_first(r):
        return 1 + lax.rem(r + n_ctx // 3, n_ctx - 1)

    def there_copy(r):
        peer = lax.rem(me + r, n_ctx)
        return pltpu.make_async_remote_copy(
            src_ref=packed_ref.at[pl.ds(pl.multiple_of(peer * each, each), each)],
            dst_ref=arrived_ref.at[pl.ds(pl.multiple_of(me * each, each), each)],
            send_sem=there_send.at[r],
            recv_sem=there_recv.at[r],
            device_id=(peer, z),
            device_id_type=pl.DeviceIdType.MESH,
        )

    def start_there(r, carry):
        there_copy(far_first(r)).start()
        return carry

    def wait_there(r, carry):
        there_copy(r).wait_recv()
        return carry

    lax.fori_loop(1, n_ctx, start_there, 0)
    own = pl.ds(pl.multiple_of(me * each, each), each)
    arrived_ref[own, :] = packed_ref[own, :]
    for load in loads:
        load.wait()
    lax.fori_loop(1, n_ctx, wait_there, 0)

    share = lots // n_exp
    first_expert = lax.rem(z + half, n_exp) * share // in_all

    def make_part(i):
        e = lax.rem(first_expert + i, experts)
        spot = pl.ds(pl.multiple_of(e * in_all, in_all), in_all)
        tokens_in = dot(by_expert_ref[spot, :], arrived_ref[...])
        scaled = (tokens_in * gain_ref[...]).astype(BF16)
        part_ref[spot, :] = dot(scaled, gu_ref[e]).astype(BF16)
        squared_ref[spot, :] = (tokens_in * tokens_in).astype(BF16)

    piece = share // PARTS

    hops = half // 2

    def part_rows(target, part):
        return pl.ds(pl.multiple_of(target * share + part * piece, piece), piece)

    def gu_chain(way, step, part):
        spot = pl.ds(part * piece, piece)
        if step == 0:
            source = part_ref.at[part_rows(place_at(way, half), part)]
        else:
            source = gu_out.at[way, step, spot]
        return move(
            source,
            gu_in.at[way, step, spot],
            gu_send.at[way, step, part],
            gu_recv.at[way, step, part],
            way,
            2,
        )

    def gu_leaf(way, step, part):
        spot = pl.ds(part * piece, piece)
        return move(
            part_ref.at[part_rows(place_at(way, half - 1 - 2 * step), part)],
            gu_in.at[way, hops + step, spot],
            gu_send.at[way, hops + step, part],
            gu_recv.at[way, hops + step, part],
            way,
            1,
        )

    def gu_term(target, part):
        return part_ref[part_rows(target, part), :].astype(F32)

    def gu_arrived(term, way, step, part):
        spot = pl.ds(part * piece, piece)
        gu_leaf(way, step, part).wait_recv()
        term = term + gu_in[way, hops + step, spot].astype(F32)
        if step > 0 or far(way, part, PARTS):
            gu_chain(way, step, part).wait_recv()
            term = term + gu_in[way, step, spot].astype(F32)
        return term

    both = [(way, part) for part in range(PARTS) for way in range(2)]

    def gu_leaves(step):
        for way, part in both:
            gu_leaf(way, step, part).start()

    def gu_step(step):
        gu_leaves(step)
        for way, part in both:
            term = gu_arrived(gu_term(place_at(way, half - 2 * step), part), way, step - 1, part)
            gu_out[way, step, pl.ds(part * piece, piece)] = term.astype(BF16)
            gu_chain(way, step, part).start()

    make_part(0)
    for way, part in both:
        if far(way, part, PARTS):
            gu_chain(way, 0, part).start()
    for i in range(1, experts):
        make_part(i)
    gu_leaves(0)

    squares = lax.dot_general(
        jnp.ones((8, local), BF16),
        squared_ref[...],
        (((1,), (1,)), ((), ())),
        preferred_element_type=F32,
    )
    for to in range(n_exp):
        squares_out[to, :, pl.ds(0, share)] = squares[0:1, to * share : (to + 1) * share]

    def sq_copy(r):
        peer = lax.rem(z + r, n_exp)
        return pltpu.make_async_remote_copy(
            src_ref=squares_out.at[peer],
            dst_ref=squares_in.at[r],
            send_sem=sq_send.at[r],
            recv_sem=sq_recv.at[r],
            device_id=(me, peer),
            device_id_type=pl.DeviceIdType.MESH,
        )

    def start_sq(r, carry):
        sq_copy(r).start()
        return carry

    lax.fori_loop(1, n_exp, start_sq, 0)

    def sent_proj(step, carry):
        for way in range(2):
            for part in range(CHUNKS):
                proj_copy(way, step, part).wait_send()
        return carry

    for step in range(1, hops):
        gu_step(step)
        if step == 1:
            lax.fori_loop(1, half // 2, sent_proj, 0)
        if step == 2:
            lax.fori_loop(half // 2, half - 1, sent_proj, 0)

    def wait_sq(r, carry):
        sq_copy(r).wait_recv()
        return carry

    lax.fori_loop(1, n_exp, wait_sq, 0)
    squares_in[0] = squares_out[z]
    row = jnp.sum(squares_in[...], axis=0)
    at_lane = lax.broadcasted_iota(jnp.int32, (share, HD), 1)
    at_row = lax.broadcasted_iota(jnp.int32, (share, HD), 0)
    column = jnp.sum(jnp.where(at_lane == at_row, row, 0.0), axis=1, keepdims=True)
    scale = lax.rsqrt(column / (local * n_exp) + EPS)

    def hid_copy(way, step, part, distance, ahead=0):
        block = place_at(1 - way, 2 * step + ahead)
        spot = hidden_ref.at[part_rows(block, part)]
        lane_of = (2 - distance) * hops + step
        return move(
            spot, spot, hid_send.at[way, lane_of, part], hid_recv.at[way, lane_of, part], way, distance
        )

    def hid_far(way, step, part):
        return step < hops - 1 or far(way, part, PARTS)

    for part in range(PARTS):
        term = gu_term(z, part)
        for way in range(2):
            term = gu_arrived(term, way, hops - 1, part)
        term = term * scale[part * piece : (part + 1) * piece]
        gate, upper = term[:, :units], term[:, units:]
        hidden = gate / (1.0 + jnp.exp(-gate)) * upper
        hidden_ref[part_rows(z, part), :] = hidden.astype(BF16)
        for way in range(2):
            hid_copy(way, 0, part, 2).start()
            hid_copy(way, 0, part, 1).start()

    for step in range(hops):
        for way, part in both:
            if step > 0:
                hid_copy(way, step - 1, part, 2, 2).wait_recv()
                if hid_far(way, step, part):
                    hid_copy(way, step, part, 2).start()
                hid_copy(way, step, part, 1).start()
        if step == 0:
            for way, part in both:
                if far(way, part, PARTS):
                    gu_chain(way, 0, part).wait_send()
                gu_leaf(way, 0, part).wait_send()
        else:
            for way, part in both:
                gu_chain(way, step, part).wait_send()
                gu_leaf(way, step, part).wait_send()
    for step in range(hops):
        for way, part in both:
            hid_copy(way, step, part, 1, 1).wait_recv()
    for way, part in both:
        if hid_far(way, hops - 1, part):
            hid_copy(way, hops - 1, part, 2, 2).wait_recv()

    made = jnp.concatenate(
        [dot(hidden_ref[pl.ds(e * in_all, in_all), :], down_ref[e]) for e in range(experts)], axis=0
    ).astype(BF16)
    made_ref[...] = dot(by_device_ref[...], made).astype(BF16)

    def home_copy(r):
        peer = lax.rem(me + r, n_ctx)
        return pltpu.make_async_remote_copy(
            src_ref=made_ref.at[pl.ds(pl.multiple_of(peer * each, each), each)],
            dst_ref=back_ref.at[pl.ds(pl.multiple_of(me * each, each), each)],
            send_sem=home_send.at[r],
            recv_sem=home_recv.at[r],
            device_id=(peer, z),
            device_id_type=pl.DeviceIdType.MESH,
        )

    def start_home(r, carry):
        home_copy(far_first(r)).start()
        return carry

    def wait_home(r, carry):
        home_copy(r).wait_recv()
        return carry

    lax.fori_loop(1, n_ctx, start_home, 0)
    back_ref[own, :] = made_ref[own, :]

    def sent_ctx(r, carry):
        there_copy(r).wait_send()
        return carry

    def sent_home(r, carry):
        home_copy(r).wait_send()
        return carry

    def sent_exp(r, carry):
        sq_copy(r).wait_send()
        return carry

    for way in range(2):
        for part in range(CHUNKS):
            if far(way, part, CHUNKS):
                proj_far(way, part).wait_send()
            proj_near(way, part).wait_send()
    for step in range(hops):
        for way, part in both:
            if hid_far(way, step, part):
                hid_copy(way, step, part, 2).wait_send()
            hid_copy(way, step, part, 1).wait_send()
    lax.fori_loop(1, n_exp, sent_exp, 0)
    lax.fori_loop(1, n_ctx, sent_ctx, 0)
    square = (tokens, tokens)
    at_row = lax.broadcasted_iota(jnp.int32, square, 0)
    at_lane = lax.broadcasted_iota(jnp.int32, square, 1)
    score = jnp.sum(jnp.where(at_row == at_lane, score_ref[...], 0.0), axis=1, keepdims=True)
    lax.fori_loop(1, n_ctx, wait_home, 0)
    out_ref[...] = (dot(spread_ref[...], back_ref[...]) * score).astype(BF16)
    lax.fori_loop(1, n_ctx, sent_home, 0)


def layer(n_ctx, n_exp, query, route, score, gain, keys, values, weight, gate, up, down):
    tokens, local = query.shape
    experts, _, units = gate.shape
    most = 2 * tokens // (experts * n_ctx)
    lots = n_ctx * experts * most
    share = lots // n_exp
    half = n_exp // 2
    heads = local // HD
    dma = pltpu.SemaphoreType.DMA
    vmem = pl.BlockSpec(memory_space=pltpu.VMEM)
    anywhere = pl.BlockSpec(memory_space=pl.ANY)
    return pl.pallas_call(
        functools.partial(layer_kernel, n_ctx, n_exp),
        out_shape=jax.ShapeDtypeStruct((tokens, local), BF16),
        in_specs=[vmem] * 4 + [anywhere] * 6,
        out_specs=vmem,
        scratch_shapes=[
            pltpu.VMEM((n_ctx, 2, tokens, HD), BF16),
            pltpu.VMEM((n_ctx, *weight.shape), BF16),
            pltpu.VMEM((heads, tokens, 1), F32),
            pltpu.VMEM((heads, tokens, 2 * HD), F32),
            pltpu.VMEM((tokens, local), BF16),
            pltpu.VMEM((experts, local, 2 * units), BF16),
            pltpu.VMEM((experts, units, local), BF16),
            pltpu.VMEM((2, half, tokens, local), BF16),
            pltpu.VMEM((2, half, tokens, local), BF16),
            pltpu.VMEM((tokens, local), BF16),
            pltpu.VMEM((n_exp, tokens, local), BF16),
            pltpu.VMEM((lots, tokens), BF16),
            pltpu.VMEM((tokens, lots), BF16),
            pltpu.VMEM((lots, lots), BF16),
            pltpu.VMEM((lots, lots), BF16),
            pltpu.VMEM((lots, local), BF16),
            pltpu.VMEM((lots, local), BF16),
            pltpu.VMEM((lots, local), BF16),
            pltpu.VMEM((lots, 2 * units), BF16),
            pltpu.VMEM((2, half, share, 2 * units), BF16),
            pltpu.VMEM((2, half, share, 2 * units), BF16),
            pltpu.VMEM((n_exp, 1, HD), F32),
            pltpu.VMEM((n_exp, 1, HD), F32),
            pltpu.VMEM((lots, units), BF16),
            pltpu.VMEM((lots, local), BF16),
            pltpu.VMEM((lots, local), BF16),
            dma((6,)),
            dma((2, MESSAGES)),
            dma((2, MESSAGES)),
            dma((2, half, CHUNKS)),
            dma((2, half, CHUNKS)),
            dma((n_ctx,)),
            dma((n_ctx,)),
            dma((2, half, PARTS)),
            dma((2, half, PARTS)),
            dma((n_exp,)),
            dma((n_exp,)),
            dma((2, half, PARTS)),
            dma((2, half, PARTS)),
            dma((n_ctx,)),
            dma((n_ctx,)),
        ],
        compiler_params=pltpu.CompilerParams(
            collective_id=0, has_side_effects=True, vmem_limit_bytes=VMEM_LIMIT
        ),
        name="layer",
    )(query, route, score, gain, keys, values, weight, gate, up, down)


def body(
    queries,
    keys,
    values,
    routes,
    route_score,
    output_weight,
    norm_gain,
    gate_weight,
    up_weight,
    down_weight,
):
    tokens, local = queries.shape[1:]
    return layer(
        lax.axis_size("ctx"),
        lax.axis_size("exp"),
        queries[0],
        routes[0].reshape(1, tokens),
        route_score,
        norm_gain.reshape(1, local),
        keys[0],
        values[0],
        output_weight,
        gate_weight,
        up_weight,
        down_weight,
    )[None]


def solution(mesh):
    placed = (
        P(None, "ctx", "exp"),
        P(None, "ctx", None),
        P(None, "ctx", None),
        P(None, "ctx", None),
        P(None, "ctx"),
        P("exp", "ctx"),
        P("exp"),
        P("ctx", "exp", None),
        P("ctx", "exp", None),
        P("ctx", None, "exp"),
    )
    return jax.shard_map(
        body, mesh=mesh, in_specs=placed, out_specs=P(None, "ctx", "exp"), check_vma=False
    )
```
